256 devices in a mesh: pop: 16 (over z_hi, x, core), dp: 16 (over z_lo, y).
Axes of the slice: x: 4, y: 4, z: 8 (z_hi: 2, z_lo: 4; z = z_hi * 4 + z_lo), core: 2. Of those that a mesh axis runs over, the one named last changes fastest.
Arguments:
- state_pool: bfloat16 [16384, 2048], P('dp'), may hold values from -6 to 6
- probe_row: int32 [16384], P('dp'), may hold values from 0 to 1023
- action: int32 [16384], P('dp'), may hold values from 0 to 17
- w_hidden: bfloat16 [16, 2048, 1024], P('pop'), may hold values from -0.125 to 0.125
- w_head: bfloat16 [16, 18, 1024], P('pop'), may hold values from -0.1875 to 0.1875
- targets: float32 [16, 16384], P('pop', 'dp'), may hold values from -6 to 6
Outputs:
- grad_hidden: float32 [16, 2048, 1024], P('pop', 'dp')
- grad_head: float32 [16, 18, 1024], P('pop', None, 'dp')
The draws below stay inside these ranges and needn't reach their ends.
All inputs are finite; a program needn't handle non-finite values.
Results may differ from the reference program's by a relative error of at most 0.013.
Values sent between devices are 32-bit elements; how exact they have to be, the bound alone decides.
No kernel may reach another device: no remote copies, remote signals or barrier semaphores. Data moves between devices by JAX's collectives and lax.ppermute only.
A program may use at most 128 MiB of HBM per device.

```python
import math
import jax
import jax.numpy as jnp
from jax import lax

FEAT = 2048
HID = 1024
ACTIONS = 18
PROBE_DEV = 1024
PROBES = 16384
POOL_ROWS = 16384
AGENTS = 16


def with_ends(entries, stream_key, least, high):
    longest = entries.shape.index(max(entries.shape))
    spots = []
    for shift in (0, 1):
        where = [jax.random.randint(jax.random.fold_in(stream_key, axis), (), 0, length) for axis, length in enumerate(entries.shape)]
        where[longest] = (where[longest] + shift) % entries.shape[longest]
        spots.append(tuple(where))
    return entries.at[spots[0]].set(least).at[spots[1]].set(high)


def steps_of(own_key, extent, cuts, low, largest):
    def one(axis_at, parts):
        heights = jax.random.uniform(jax.random.fold_in(jax.random.fold_in(own_key, 6), axis_at), (parts,), jnp.float32, low / len(cuts), largest / len(cuts))
        return jnp.repeat(jnp.exp(heights), extent[axis_at] // parts).reshape((-1,) + (1,) * (len(extent) - axis_at - 1))

    level = one(*cuts[0])
    for cut in cuts[1:]:
        level = level * one(*cut)
    return level


def normal_values(own_key, dims, width, bound, shards=(), held_as=jnp.bfloat16):
    array = jax.random.normal(own_key, dims, jnp.float32) * width
    if len(shards) > 0:
        array = steps_of(own_key, dims, shards, -0.22, 0.18) * array
    return jnp.clip(array, min=-bound, max=bound).astype(held_as)


def setup_inputs(seed: int = 0) -> dict:
    keys = jax.random.split(jax.random.key(seed), 7)
    state_pool = normal_values(keys[0], (POOL_ROWS, FEAT), 1.0, 6.0, ((0, 16),))
    probe_row = with_ends(jax.random.randint(keys[1], (PROBES,), 0, PROBE_DEV), jax.random.fold_in(keys[1], 1), 0, PROBE_DEV - 1).astype(jnp.int32)
    action = with_ends(jax.random.randint(keys[2], (PROBES,), 0, ACTIONS), jax.random.fold_in(keys[2], 1), 0, ACTIONS - 1).astype(jnp.int32)
    w_hidden = normal_values(keys[3], (AGENTS, FEAT, HID), FEAT ** -0.5, 0.125, ((0, 16),))
    w_head = normal_values(keys[4], (AGENTS, ACTIONS, HID), HID ** -0.5, 0.1875, ((0, 16),))
    targets = normal_values(keys[5], (AGENTS, PROBES), 1.0, 6.0, ((0, 16), (1, 16)), jnp.float32)
    return dict(state_pool=state_pool, probe_row=probe_row, action=action, w_hidden=w_hidden, w_head=w_head, targets=targets)


def reference(state_pool, probe_row, action, w_hidden, w_head, targets):
    offsets = jnp.arange(PROBES, dtype=jnp.int32) // PROBE_DEV * PROBE_DEV
    features = jnp.take(state_pool, (offsets + probe_row).astype(jnp.int32), axis=0)
    scaling = math.sqrt(HID / PROBES)
    onehot = (action[:, None] == jnp.arange(ACTIONS, dtype=jnp.int32)[None, :]).astype(jnp.float32)

    def forward_parts(w_one, w_two):
        preact = jnp.dot(features.astype(jnp.float32), w_one.astype(jnp.float32), preferred_element_type=jnp.float32)
        hidden = jax.nn.silu(preact).astype(jnp.bfloat16)
        wide = w_two.astype(jnp.float32)
        centered = wide - lax.optimization_barrier(jnp.mean(wide, axis=0, keepdims=True))
        values = jnp.take(centered, action, axis=0)
        return (preact, hidden, values)

    def forward(weights):
        preact, hidden, values = forward_parts(weights[0], weights[1])
        return lax.optimization_barrier(jnp.sum(hidden.astype(jnp.float32) * values, axis=1))
    embedding = lax.map(forward, (w_hidden, w_head))
    distances = lax.map(lambda row: lax.optimization_barrier(jnp.sum((row[None, :] - embedding) ** 2, axis=1)), embedding)
    kernel = jnp.exp(-distances / PROBES)
    factor = jnp.linalg.cholesky(kernel)
    inverse = jax.scipy.linalg.cho_solve((factor, True), jnp.eye(AGENTS, dtype=jnp.float32))
    mixing = inverse * kernel
    pulled = jnp.dot(mixing, embedding, precision=lax.Precision.HIGHEST)
    diverse = 2.0 * (lax.optimization_barrier(jnp.sum(mixing, axis=1))[:, None] * embedding - pulled)
    task = scaling * (embedding - targets)
    spread = scaling * diverse

    def backward(items):
        w_one, w_two, task_row, spread_row = items
        preact, hidden, values = forward_parts(w_one, w_two)
        sig = jax.nn.sigmoid(preact)
        slope = sig * (1.0 + preact * (1.0 - sig))
        dz_task = (task_row[:, None] * values * slope).astype(jnp.bfloat16)
        dz_div = (spread_row[:, None] * values * slope).astype(jnp.bfloat16)
        grad_one = jnp.dot(features.T.astype(jnp.float32), dz_task.astype(jnp.float32), preferred_element_type=jnp.float32) + jnp.dot(features.T.astype(jnp.float32), dz_div.astype(jnp.float32), preferred_element_type=jnp.float32)
        weighted = (task_row + spread_row)[:, None] * hidden.astype(jnp.float32)
        grad_two = jnp.dot(onehot.T, weighted, precision=lax.Precision.HIGHEST) - lax.optimization_barrier(jnp.sum(weighted, axis=0))[None, :] / ACTIONS
        return (grad_one, grad_two)
    grad_hidden, grad_head = lax.map(backward, (w_hidden, w_head, task, spread))
    return (grad_hidden, grad_head)
```

```python
import functools
import math

import jax
import jax.numpy as jnp
from jax import lax
from jax.experimental import pallas as pl
from jax.experimental.pallas import tpu as pltpu
from jax.sharding import PartitionSpec as P

HID = 1024
ACTIONS = 18
PAD = 32
CHUNKS = (64, 32, 32)
F32 = jnp.float32
BF16 = jnp.bfloat16
NT = (((1,), (1,)), ((), ()))
TN = (((0,), (0,)), ((), ()))
VMEM_SPEC = pl.BlockSpec(memory_space=pltpu.VMEM)
ANY_SPEC = pl.BlockSpec(memory_space=pl.ANY)


def params(mib=48):
    return pltpu.CompilerParams(vmem_limit_bytes=mib * 1024 * 1024)


def split3(v):
    hi = v.astype(BF16)
    rest = v - hi.astype(F32)
    mid = rest.astype(BF16)
    low = (rest - mid.astype(F32)).astype(BF16)
    return jnp.concatenate([hi, mid, low], axis=0)


def join3(v):
    return v[:PAD] + v[PAD : 2 * PAD] + v[2 * PAD :]


def row_onehot(start, size, row):
    ids = lax.broadcasted_iota(jnp.int32, (size, row.shape[1]), 0) + start
    return jnp.where(ids == row, 1.0, 0.0).astype(BF16)


def forward_kernel(pool_ref, w_ref, head_ref, row_ref, act_ref, hid_ref, slope_ref, emb_ref, acc_ref):
    step = pl.program_id(0)
    rows = pool_ref.shape[0]
    tile = 256

    @pl.when(step == 0)
    def _():
        acc_ref[...] = jnp.zeros_like(acc_ref)

    for i in range(rows // tile):
        here = pl.ds(i * tile, tile)
        v = jnp.dot(pool_ref[here, :], w_ref[...], preferred_element_type=F32)
        sig = 0.5 * jnp.tanh(0.5 * v) + 0.5
        hid = (v * sig).astype(BF16)
        hid_ref[here, :] = hid
        slope_ref[here, :] = sig * (1.0 + v * (1.0 - sig))
        acc_ref[:, here] += lax.dot_general(head_ref[...], hid, NT, preferred_element_type=F32)

    @pl.when(step == pl.num_programs(0) - 1)
    def _():
        logits = acc_ref[...]
        parts = split3(logits - jnp.sum(logits, axis=0, keepdims=True) / ACTIONS)
        picked = jnp.zeros((3 * PAD, row_ref.shape[1]), F32)
        for i in range(rows // tile):
            picked += jnp.dot(
                parts[:, i * tile : (i + 1) * tile],
                row_onehot(i * tile, tile, row_ref[...]),
                preferred_element_type=F32,
            )
        chosen = lax.broadcasted_iota(jnp.int32, (PAD, row_ref.shape[1]), 0) == act_ref[...]
        emb_ref[...] = jnp.sum(jnp.where(chosen, join3(picked), 0.0), axis=0, keepdims=True)


def forward(pool, w, head, row, act):
    rows, feat = pool.shape
    hid = w.shape[1]
    tile = 256
    probes = row.shape[1]
    return pl.pallas_call(
        forward_kernel,
        grid=(hid // tile,),
        in_specs=[
            pl.BlockSpec((rows, feat), lambda j: (0, 0)),
            pl.BlockSpec((feat, tile), lambda j: (0, j)),
            pl.BlockSpec((PAD, tile), lambda j: (0, j)),
            pl.BlockSpec((1, probes), lambda j: (0, 0)),
            pl.BlockSpec((1, probes), lambda j: (0, 0)),
        ],
        out_specs=[
            pl.BlockSpec((rows, tile), lambda j: (0, j)),
            pl.BlockSpec((rows, tile), lambda j: (0, j)),
            pl.BlockSpec((1, probes), lambda j: (0, 0)),
        ],
        out_shape=[
            jax.ShapeDtypeStruct((rows, hid), BF16),
            jax.ShapeDtypeStruct((rows, hid), F32),
            jax.ShapeDtypeStruct((1, probes), F32),
        ],
        scratch_shapes=[pltpu.VMEM((PAD, rows), F32)],
        compiler_params=params(),
        name="forward",
    )(pool, w, head, row, act)


def distance_kernel(near_ref, far_ref, out_ref):
    pop = jnp.concatenate([near_ref[...], far_ref[...]], axis=0)
    agents = pop.shape[0]
    lanes = lax.broadcasted_iota(jnp.int32, (agents, 128), 1)
    total = jnp.zeros((agents, 128), F32)
    for i in range(agents):
        gap = pop - pop[i : i + 1, :]
        total = jnp.where(lanes == i, jnp.sum(gap * gap, axis=1, keepdims=True), total)
    out_ref[...] = total


def distance_parts(near, far):
    return pl.pallas_call(
        distance_kernel,
        in_specs=[VMEM_SPEC] * 2,
        out_specs=VMEM_SPEC,
        out_shape=jax.ShapeDtypeStruct((2 * near.shape[0], 128), F32),
        compiler_params=params(),
        name="distances",
    )(near, far)


def coeff_kernel(
    total_probes, scaling, d0, d1, d2, d3, near_ref, far_ref, target_ref, row_ref, act_ref, head_ref, hid_hbm, slope_hbm,
    dz_ref, ghead_ref, hid_ref, slope_ref, sems,
):
    slope_copy = pltpu.make_async_copy(slope_hbm, slope_ref, sems.at[0])
    hid_copy = pltpu.make_async_copy(hid_hbm, hid_ref, sems.at[1])
    slope_copy.start()
    hid_copy.start()
    pop = jnp.concatenate([near_ref[...], far_ref[...]], axis=0)
    agents = pop.shape[0]
    lanes = lax.broadcasted_iota(jnp.int32, (agents, 128), 1)
    subs = lax.broadcasted_iota(jnp.int32, (agents, 128), 0)
    kern = jnp.exp(-((d0[...] + d1[...]) + (d2[...] + d3[...])) / total_probes)
    system = jnp.where(lanes < agents, kern, jnp.where((lanes == agents) & (subs == 0), 1.0, 0.0))
    for k in range(agents):
        pivot_row = system[k : k + 1, :] / system[k : k + 1, k : k + 1]
        system = jnp.where(subs == k, pivot_row, system - system[:, k : k + 1] * pivot_row)
    mix = system[:, agents : agents + 1] * kern[:, 0:1]
    emb = pop[0:1, :]
    pulled = jnp.sum(mix * pop, axis=0, keepdims=True)
    diverse = 2.0 * (jnp.sum(mix, axis=0, keepdims=True) * emb - pulled)
    coeff = scaling * (emb - target_ref[...]) + scaling * diverse

    probes = row_ref.shape[1]
    rows = slope_ref.shape[0]
    tile = 256
    chosen = lax.broadcasted_iota(jnp.int32, (PAD, probes), 0) == act_ref[...]
    marked = split3(jnp.where(chosen, coeff, 0.0))
    head = head_ref[...].astype(F32)
    centered = head - jnp.sum(head, axis=0, keepdims=True) / ACTIONS
    cent_hi = centered.astype(BF16)
    cent_lo = (centered - cent_hi.astype(F32)).astype(BF16)
    cents = jnp.concatenate([cent_hi, cent_lo, cent_hi], axis=0)
    sums = []
    for i in range(rows // tile):
        sums.append(
            join3(lax.dot_general(marked, row_onehot(i * tile, tile, row_ref[...]), NT, preferred_element_type=F32))
        )
    slope_copy.wait()
    for i in range(rows // tile):
        here = pl.ds(i * tile, tile)
        part_hi = sums[i].astype(BF16)
        part_lo = (sums[i] - part_hi.astype(F32)).astype(BF16)
        stacked = jnp.concatenate([part_hi, part_hi, part_lo], axis=0)
        pulls = lax.dot_general(stacked, cents, TN, preferred_element_type=F32)
        dz_ref[here, :] = (pulls * slope_ref[here, :]).astype(BF16)
    hid_copy.wait()
    total = jnp.zeros((3 * PAD, hid_ref.shape[1]), F32)
    for i in range(rows // tile):
        even = split3(sums[i] - jnp.sum(sums[i], axis=0, keepdims=True) / ACTIONS)
        total += jnp.dot(even, hid_ref[pl.ds(i * tile, tile), :], preferred_element_type=F32)
    ghead_ref[...] = join3(total)


def coefficients(total_probes, dists, near, far, target, row, act, head, hid, slope):
    rows, width = hid.shape
    scaling = math.sqrt(HID / total_probes)
    return pl.pallas_call(
        functools.partial(coeff_kernel, total_probes, scaling),
        in_specs=[VMEM_SPEC] * 10 + [ANY_SPEC] * 2,
        out_specs=[VMEM_SPEC] * 2,
        out_shape=[
            jax.ShapeDtypeStruct((rows, width), BF16),
            jax.ShapeDtypeStruct((PAD, width), F32),
        ],
        scratch_shapes=[
            pltpu.VMEM((rows, width), BF16),
            pltpu.VMEM((rows, width), F32),
            pltpu.SemaphoreType.DMA((2,)),
        ],
        compiler_params=params(),
        name="coefficients",
    )(*dists, near, far, target, row, act, head, hid, slope)


def turn_kernel(order_ref, pool_ref, out_ref):
    out_ref[0] = pool_ref[...].T


def turned_pool(order, pool):
    rows, feat = pool.shape
    blocks = order.shape[0]
    width = feat // blocks
    return pl.pallas_call(
        turn_kernel,
        grid_spec=pltpu.PrefetchScalarGridSpec(
            num_scalar_prefetch=1,
            grid=(blocks,),
            in_specs=[pl.BlockSpec((rows, width), lambda i, order: (0, order[i]))],
            out_specs=pl.BlockSpec((1, width, rows), lambda i, order: (i, 0, 0)),
        ),
        out_shape=jax.ShapeDtypeStruct((blocks, width, rows), BF16),
        compiler_params=params(),
        name="turned_pool",
    )(order, pool)


def grad_kernel(pool_ref, dz_ref, *out_refs):
    blocks, rows, depth = pool_ref.shape
    per = blocks // len(out_refs)
    for g, out_ref in enumerate(out_refs):
        left = pool_ref[g * per : (g + 1) * per].reshape(per * rows, depth)
        out_ref[...] = jnp.dot(left, dz_ref[...], preferred_element_type=F32)


def grad_chunk(turned, dz, start, size):
    blocks, _, depth = turned.shape
    width = dz.shape[1]
    pieces = 8
    return pl.pallas_call(
        grad_kernel,
        grid=(1,),
        in_specs=[
            pl.BlockSpec((blocks, size, depth), lambda i: (0, start // size, 0)),
            pl.BlockSpec(dz.shape, lambda i: (0, 0)),
        ],
        out_specs=[pl.BlockSpec((blocks // pieces * size, width), lambda i: (0, 0))] * pieces,
        out_shape=[jax.ShapeDtypeStruct((blocks // pieces * size, width), F32)] * pieces,
        compiler_params=params(),
        name="gradient",
    )(turned, dz)


def shift_y(v, s):
    return lax.ppermute(v, "dp", [(z * 4 + y, z * 4 + (y + s) % 4) for z in range(4) for y in range(4)])


def shift_z(v, s):
    return lax.ppermute(v, "dp", [(z * 4 + y, (z + s) % 4 * 4 + y) for z in range(4) for y in range(4)])


def swap(v, axis, mask):
    return lax.ppermute(v, axis, [(i, i ^ mask) for i in range(16)])


def body(state_pool, probe_row, action, w_hidden, w_head, targets):
    probes = probe_row.shape[0]
    total_probes = probes * lax.axis_size("dp")
    place = lax.axis_index("dp")
    z, y = place // 4, place % 4
    row = probe_row.reshape(1, probes)
    act = action.reshape(1, probes)
    head = jnp.pad(w_head[0], ((0, PAD - ACTIONS), (0, 0)))

    hid, slope, emb = forward(state_pool, w_hidden[0], head, row, act)

    steps_y = jnp.array([2, 2, 2, 2, 1, 1, 1, 1, 3, 3, 3, 3, 0, 0, 0, 0], jnp.int32)
    steps_z = jnp.array([0, 1, 2, 3] * 4, jnp.int32)
    order = (z + steps_z) % 4 * 4 + (y + steps_y) % 4
    turned = turned_pool(order.astype(jnp.int32), state_pool)

    pair = jnp.concatenate([emb, swap(emb, "pop", 1)], axis=0)
    near = jnp.concatenate([pair] + [swap(pair, "pop", m) for m in (2, 4, 6)], axis=0)
    far = swap(near, "pop", 8)
    part = distance_parts(near, far)
    part = part + swap(part, "dp", 1) + swap(part, "dp", 2) + swap(part, "dp", 3)
    dists = [part] + [swap(part, "dp", m) for m in (4, 8, 12)]
    dz, ghead = coefficients(total_probes, dists, near, far, targets, row, act, head, hid, slope)

    outs = []
    start = 0
    for size in CHUNKS:
        a2, b2, a1, b1, a3, b3, a0, b0 = grad_chunk(turned, dz, start, size)
        from_a, from_b = shift_y(a2, 1), shift_y(b2, -1)
        got_b1, got_a3 = shift_y(b1, 1), shift_y(a3, -1)
        got_a1, got_b3 = shift_y(a1 + from_a, 1), shift_y(b3 + from_b, -1)
        a0 = a0 + got_a1 + got_a3
        b0 = b0 + got_b1 + got_b3
        own = a0[:size]
        for s, block in ((1, a0[size:]), (2, b0[:size]), (3, b0[size:])):
            own = own + shift_z(block, s)
        outs.append(own)
        start += size

    cols = ghead.shape[1] // 16
    heads = ghead[:ACTIONS].reshape(ACTIONS, 4, 4, cols).transpose(2, 1, 0, 3)
    pick = lambda v, i: lax.dynamic_index_in_dim(v, i % 4, 0, keepdims=False)
    heads_y = pick(heads, y)
    for s in (1, 2, 3):
        heads_y = heads_y + shift_y(pick(heads, y + s), s)
    grad_two = pick(heads_y, z)
    for s in (1, 2, 3):
        grad_two = grad_two + shift_z(pick(heads_y, z + s), s)
    return (jnp.concatenate(outs, axis=0)[None], grad_two[None])


def solution(mesh):
    placed = (
        P("dp", None),
        P("dp"),
        P("dp"),
        P("pop", None, None),
        P("pop", None, None),
        P("pop", "dp"),
    )
    return jax.shard_map(
        body,
        mesh=mesh,
        in_specs=placed,
        out_specs=(P("pop", "dp", None), P("pop", None, "dp")),
        check_vma=False,
    )
```

```python
import functools
import math

import jax
import jax.numpy as jnp
from jax import lax
from jax.experimental import pallas as pl
from jax.experimental.pallas import tpu as pltpu
from jax.sharding import PartitionSpec as P

HID = 1024
ACTIONS = 18
PAD = 32
CHUNKS = (64, 64)
SHARES = (0, 2, 4, 6, 1, 3, 5, 7)
HALF, BASES = 16, 17
F32 = jnp.float32
BF16 = jnp.bfloat16
NT = (((1,), (1,)), ((), ()))
TN = (((0,), (0,)), ((), ()))
VMEM_SPEC = pl.BlockSpec(memory_space=pltpu.VMEM)
SMEM_SPEC = pl.BlockSpec(memory_space=pltpu.SMEM)
ANY_SPEC = pl.BlockSpec(memory_space=pl.ANY)


def params(mib):
    return pltpu.CompilerParams(vmem_limit_bytes=mib * 1024 * 1024)


def cost(us):
    return pl.CostEstimate(flops=int(us * 1.1e9), bytes_accessed=0, transcendentals=0)


def split3(v):
    hi = v.astype(BF16)
    rest = v - hi.astype(F32)
    mid = rest.astype(BF16)
    low = (rest - mid.astype(F32)).astype(BF16)
    return jnp.concatenate([hi, mid, low], axis=0)


def join3(v):
    return v[:PAD] + v[PAD : 2 * PAD] + v[2 * PAD :]


def row_onehot(start, size, row):
    ids = lax.broadcasted_iota(jnp.int32, (size, row.shape[1]), 0) + start
    return jnp.where(ids == row, 1.0, 0.0).astype(BF16)


def sigmoid(v):
    return 0.5 * jnp.tanh(0.5 * v) + 0.5


def forward_kernel(pool_ref, w_ref, head_ref, row_ref, act_ref, hid_ref, slope_ref, emb_ref, acc_ref):
    step = pl.program_id(0)
    rows = pool_ref.shape[0]
    tile = 512

    @pl.when(step == 0)
    def _():
        acc_ref[...] = jnp.zeros_like(acc_ref)

    for i in range(rows // tile):
        here = pl.ds(i * tile, tile)
        v = jnp.dot(pool_ref[here, :], w_ref[...], preferred_element_type=F32)
        sig = sigmoid(v)
        hid = (v * sig).astype(BF16)
        hid_ref[here, :] = hid
        slope_ref[here, :] = sig * (1.0 + v * (1.0 - sig))
        acc_ref[:, here] += lax.dot_general(head_ref[...], hid, NT, preferred_element_type=F32)

    @pl.when(step == pl.num_programs(0) - 1)
    def _():
        logits = acc_ref[...]
        parts = split3(logits - jnp.sum(logits, axis=0, keepdims=True) / ACTIONS)
        picked = jnp.zeros((3 * PAD, row_ref.shape[1]), F32)
        for i in range(0, rows, 256):
            picked += jnp.dot(parts[:, i : i + 256], row_onehot(i, 256, row_ref[...]), preferred_element_type=F32)
        chosen = lax.broadcasted_iota(jnp.int32, (PAD, row_ref.shape[1]), 0) == act_ref[...]
        emb_ref[...] = jnp.sum(jnp.where(chosen, join3(picked), 0.0), axis=0, keepdims=True)


def forward(pool, w, head, row, act):
    rows, feat = pool.shape
    hid = w.shape[1]
    tile = 512
    probes = row.shape[1]
    return pl.pallas_call(
        forward_kernel,
        grid=(hid // tile,),
        in_specs=[
            pl.BlockSpec((rows, feat), lambda j: (0, 0)),
            pl.BlockSpec((feat, tile), lambda j: (0, j)),
            pl.BlockSpec((PAD, tile), lambda j: (0, j)),
            pl.BlockSpec((1, probes), lambda j: (0, 0)),
            pl.BlockSpec((1, probes), lambda j: (0, 0)),
        ],
        out_specs=[
            pl.BlockSpec((rows, tile), lambda j: (0, j)),
            pl.BlockSpec((rows, tile), lambda j: (0, j)),
            pl.BlockSpec((1, probes), lambda j: (0, 0)),
        ],
        out_shape=[
            jax.ShapeDtypeStruct((rows, hid), BF16),
            jax.ShapeDtypeStruct((rows, hid), F32),
            jax.ShapeDtypeStruct((1, probes), F32),
        ],
        scratch_shapes=[pltpu.VMEM((PAD, rows), F32)],
        compiler_params=params(32),
        cost_estimate=cost(11),
        name="forward",
    )(pool, w, head, row, act)


def distance_kernel(near_ref, far_ref, out_ref):
    pop = jnp.concatenate([near_ref[...], far_ref[...]], axis=0)
    agents = pop.shape[0]
    lanes = lax.broadcasted_iota(jnp.int32, (agents, 128), 1)
    total = jnp.zeros((agents, 128), F32)
    for i in range(agents):
        gap = pop - pop[i : i + 1, :]
        total = jnp.where(lanes == i, jnp.sum(gap * gap, axis=1, keepdims=True), total)
    out_ref[...] = total


def distance_parts(near, far):
    return pl.pallas_call(
        distance_kernel,
        in_specs=[VMEM_SPEC] * 2,
        out_specs=VMEM_SPEC,
        out_shape=jax.ShapeDtypeStruct((2 * near.shape[0], 128), F32),
        compiler_params=params(16),
        name="distances",
    )(near, far)


def partner_kernel(plan_ref, a_ref, b_ref, c_ref, d_ref, w_ref, slope_ref, turned_ref, rows_ref):
    share = a_ref.shape[0]
    for j, ref in enumerate((a_ref, b_ref, c_ref, d_ref)):
        rows_ref[pl.ds(j * share, share), :] = ref[...].astype(BF16)
    v = jnp.dot(rows_ref[...], w_ref[...], preferred_element_type=F32)
    sig = sigmoid(v)
    slope_ref[...] = sig * (1.0 + v * (1.0 - sig))
    width = turned_ref.shape[1]
    for i in range(turned_ref.shape[0]):
        turned_ref[i] = rows_ref[:, pl.ds(pl.multiple_of(plan_ref[i] * width, width), width)].T


def partner_part(plan, shares, w, blocks=16):
    share, feat = shares[0].shape
    half = w.shape[1] // 2
    return pl.pallas_call(
        partner_kernel,
        grid_spec=pltpu.PrefetchScalarGridSpec(
            num_scalar_prefetch=1,
            grid=(1,),
            in_specs=[pl.BlockSpec((share, feat), lambda i, plan: (0, 0))] * 4
            + [pl.BlockSpec((feat, half), lambda i, plan: (0, plan[HALF]))],
            out_specs=[
                pl.BlockSpec((4 * share, half), lambda i, plan: (0, 0)),
                pl.BlockSpec((blocks, feat // blocks, 4 * share), lambda i, plan: (0, 0, 0)),
            ],
            scratch_shapes=[pltpu.VMEM((4 * share, feat), BF16)],
        ),
        out_shape=[
            jax.ShapeDtypeStruct((4 * share, half), F32),
            jax.ShapeDtypeStruct((blocks, feat // blocks, 4 * share), BF16),
        ],
        compiler_params=params(32),
        cost_estimate=cost(7),
        name="partner",
    )(plan, *shares, w)


def coeff_kernel(
    total_probes, scaling, plan_ref, d0, d1, d2, d3, near_ref, far_ref, near2_ref, far2_ref, target_ref, target2_ref,
    row_ref, act_ref, row2_ref, head_ref, slope_a_ref, slope_b_ref, slope_hbm, turned_hbm,
    dz_ref, sums_ref, slope_ref, sem,
):
    del turned_hbm
    width = slope_ref.shape[1]
    columns = pl.ds(pl.multiple_of(plan_ref[HALF] * width, width), width)
    slope_copy = pltpu.make_async_copy(slope_hbm.at[:, columns], slope_ref, sem)
    slope_copy.start()
    pop = jnp.concatenate([near_ref[...], far_ref[...]], axis=0)
    pop2 = jnp.concatenate([near2_ref[...], far2_ref[...]], axis=0)
    agents = pop.shape[0]
    lanes = lax.broadcasted_iota(jnp.int32, (agents, 128), 1)
    subs = lax.broadcasted_iota(jnp.int32, (agents, 128), 0)
    kern = jnp.exp(-((d0[...] + d1[...]) + (d2[...] + d3[...])) / total_probes)
    system = jnp.where(lanes < agents, kern, jnp.where((lanes == agents) & (subs == 0), 1.0, 0.0))
    for k in range(agents):
        pivot_row = system[k : k + 1, :] / system[k : k + 1, k : k + 1]
        system = jnp.where(subs == k, pivot_row, system - system[:, k : k + 1] * pivot_row)
    mix = system[:, agents : agents + 1] * kern[:, 0:1]

    def marked(people, target, act):
        emb = people[0:1, :]
        pulled = jnp.sum(mix * people, axis=0, keepdims=True)
        diverse = 2.0 * (jnp.sum(mix, axis=0, keepdims=True) * emb - pulled)
        coeff = scaling * (emb - target) + scaling * diverse
        chosen = lax.broadcasted_iota(jnp.int32, (PAD, act.shape[1]), 0) == act
        return split3(jnp.where(chosen, coeff, 0.0))

    head = head_ref[:, columns].astype(F32)
    centered = head - jnp.sum(head, axis=0, keepdims=True) / ACTIONS
    cent_hi = centered.astype(BF16)
    cent_lo = (centered - cent_hi.astype(F32)).astype(BF16)
    cents = jnp.concatenate([cent_hi, cent_lo, cent_hi], axis=0)

    def scaled(sums, slope):
        part_hi = sums.astype(BF16)
        part_lo = (sums - part_hi.astype(F32)).astype(BF16)
        stacked = jnp.concatenate([part_hi, part_hi, part_lo], axis=0)
        pulls = lax.dot_general(stacked, cents, TN, preferred_element_type=F32)
        return (pulls * slope).astype(BF16)

    rows = slope_ref.shape[0]
    tile = 256
    mine = marked(pop, target_ref[...], act_ref[0:1, :])
    theirs = marked(pop2, target2_ref[...], row2_ref[1:2, :])
    for i in range(rows // tile):
        here = pl.ds(i * tile, tile)
        hot = row_onehot(i * tile, tile, row_ref[...])
        sums_ref[:, here] = join3(lax.dot_general(mine, hot, NT, preferred_element_type=F32))
    share = rows // len(SHARES)
    per = slope_a_ref.shape[0] // tile
    for i in range(rows // tile):
        hot = jnp.concatenate(
            [
                row_onehot(plan_ref[BASES + j] * share, share, row2_ref[0:1, :])
                for j in range(i * tile // share, (i + 1) * tile // share)
            ],
            axis=0,
        )
        sums = join3(lax.dot_general(theirs, hot, NT, preferred_element_type=F32))
        slope2_ref = slope_a_ref if i < per else slope_b_ref
        dz_ref[pl.ds(rows + i * tile, tile), :] = scaled(sums, slope2_ref[pl.ds(i % per * tile, tile), :])
    slope_copy.wait()
    for i in range(rows // tile):
        here = pl.ds(i * tile, tile)
        dz_ref[here, :] = scaled(sums_ref[:, here], slope_ref[here, :])


def coefficients(total_probes, plan, dists, people, targets, row, act, row2, head, slopes, slope, turned):
    rows, width = slope.shape
    scaling = math.sqrt(HID / total_probes)
    return pl.pallas_call(
        functools.partial(coeff_kernel, total_probes, scaling),
        in_specs=[SMEM_SPEC] + [VMEM_SPEC] * 16 + [ANY_SPEC] * 2,
        out_specs=[VMEM_SPEC] * 2,
        out_shape=[
            jax.ShapeDtypeStruct((2 * rows, width // 2), BF16),
            jax.ShapeDtypeStruct((PAD, rows), F32),
        ],
        scratch_shapes=[
            pltpu.VMEM((rows, width // 2), F32),
            pltpu.SemaphoreType.DMA(()),
        ],
        compiler_params=params(24),
        cost_estimate=cost(4),
        name="coefficients",
    )(plan, *dists, *people, *targets, row, act, row2, head, *slopes, slope, turned)


def head_kernel(sums_ref, hid_ref, after_hbm, out_ref):
    del after_hbm
    sums = sums_ref[...]
    even = split3(sums - jnp.sum(sums, axis=0, keepdims=True) / ACTIONS)
    out_ref[...] = join3(jnp.dot(even, hid_ref[...], preferred_element_type=F32))


def head_gradient(sums, hid, after):
    return pl.pallas_call(
        head_kernel,
        in_specs=[VMEM_SPEC] * 2 + [ANY_SPEC],
        out_specs=VMEM_SPEC,
        out_shape=jax.ShapeDtypeStruct((PAD, hid.shape[1]), F32),
        compiler_params=params(16),
        cost_estimate=cost(2),
        name="head_gradient",
    )(sums, hid, after)


def turn_kernel(plan_ref, pool_ref, after_hbm, out_ref):
    del plan_ref, after_hbm
    out_ref[0] = pool_ref[...].T


def turned_pool(plan, pool, after, blocks=16):
    rows, feat = pool.shape
    width = feat // blocks
    return pl.pallas_call(
        turn_kernel,
        grid_spec=pltpu.PrefetchScalarGridSpec(
            num_scalar_prefetch=1,
            grid=(blocks,),
            in_specs=[pl.BlockSpec((rows, width), lambda i, plan: (0, plan[i])), ANY_SPEC],
            out_specs=pl.BlockSpec((1, width, rows), lambda i, plan: (i, 0, 0)),
        ),
        out_shape=jax.ShapeDtypeStruct((blocks, width, rows), BF16),
        compiler_params=params(16),
        cost_estimate=cost(8),
        name="turned_pool",
    )(plan, pool, after)


def grad_kernel(first, chunks, own_ref, a_ref, b_ref, dz_ref, *out_refs):
    mine, part = own_ref.shape[2], a_ref.shape[2]
    per = 2
    groups = len(out_refs) // len(chunks)
    for g in range(groups):
        here = slice(first + g * per, first + (g + 1) * per)
        total = jnp.zeros((per * own_ref.shape[1], dz_ref.shape[1]), F32)
        for ref, start, depth in ((own_ref, 0, mine), (a_ref, mine, part), (b_ref, mine + part, part)):
            left = ref[here].reshape(per * ref.shape[1], depth)
            total += jnp.dot(left, dz_ref[start : start + depth, :], preferred_element_type=F32)
        total = total.reshape(per, own_ref.shape[1], dz_ref.shape[1])
        at = 0
        for c, size in enumerate(chunks):
            out_refs[g * len(chunks) + c][...] = total[:, at : at + size].reshape(per * size, dz_ref.shape[1])
            at += size


def gradient(own, a, b, dz, first, groups):
    width = dz.shape[1]
    shapes = [jax.ShapeDtypeStruct((2 * size, width), F32) for _ in range(groups) for size in CHUNKS]
    outs = pl.pallas_call(
        functools.partial(grad_kernel, 2 * first, CHUNKS),
        in_specs=[VMEM_SPEC] * 4,
        out_specs=[VMEM_SPEC] * len(shapes),
        out_shape=shapes,
        compiler_params=params(24),
        cost_estimate=cost(groups),
        name="gradient",
    )(own, a, b, dz)
    return [outs[i : i + len(CHUNKS)] for i in range(0, len(outs), len(CHUNKS))]


def shift_y(v, s):
    return lax.ppermute(v, "dp", [(z * 4 + y, z * 4 + (y + s) % 4) for z in range(4) for y in range(4)])


def shift_z(v, s):
    return lax.ppermute(v, "dp", [(z * 4 + y, (z + s) % 4 * 4 + y) for z in range(4) for y in range(4)])


def swap(v, axis, mask):
    return lax.ppermute(v, axis, [(i, i ^ mask) for i in range(16)])


def to_partner_rows(v):
    return lax.ppermute(
        v,
        ("pop", "dp"),
        [(p * 16 + d, (p ^ (8 if d // 4 in (0, 3) else 0)) * 16 + (d ^ 12)) for p in range(16) for d in range(16)],
    )


def body(state_pool, probe_row, action, w_hidden, w_head, targets):
    probes = probe_row.shape[0]
    total_probes = probes * lax.axis_size("dp")
    place, agent = lax.axis_index("dp"), lax.axis_index("pop")
    z, y = place // 4, place % 4
    rows = state_pool.shape[0]
    share = rows // len(SHARES)
    w = w_hidden[0]

    where = agent % len(SHARES)
    cut = lambda i: lax.dynamic_slice_in_dim(state_pool, i * share, share, 0).astype(F32)
    share0 = to_partner_rows(cut(where))
    share4 = to_partner_rows(cut(where ^ 4))
    row = probe_row.reshape(1, probes)
    act = action.reshape(1, probes)
    row_act2 = swap(jnp.concatenate([row, act], axis=0), "dp", 12)
    targets2 = swap(targets, "dp", 12)
    head = jnp.pad(w_head[0], ((0, PAD - ACTIONS), (0, 0)))

    steps_y = jnp.array([2] * 4 + [1] * 4 + [3] * 4 + [0] * 4, jnp.int32)
    steps_z = jnp.array([0, 3, 1, 2] * 4, jnp.int32)
    order = (z ^ steps_z) * 4 + (y + steps_y) % 4
    bases = where ^ jnp.array(SHARES, jnp.int32)
    plan = jnp.concatenate([order, (z // 2)[None], bases]).astype(jnp.int32)

    hid, slope, emb = forward(state_pool, w, head, row, act)
    turned = turned_pool(plan, state_pool, emb)

    pair = jnp.concatenate([emb, swap(emb, "pop", 1)], axis=0)
    near = jnp.concatenate([pair] + [swap(pair, "pop", m) for m in (2, 4, 6)], axis=0)
    share2, share6 = swap(share0, "pop", 2), swap(share0, "pop", 6)
    far = swap(near, "pop", 8)
    near2, far2 = swap(near, "dp", 12), swap(far, "dp", 12)
    part = distance_parts(near, far)
    part = part + swap(part, "dp", 1) + swap(part, "dp", 2) + swap(part, "dp", 3)
    dists = [part] + [swap(part, "dp", m) for m in (4, 8, 12)]

    shares = [share0, share2, share4, share6]
    slope_a, turned_a = partner_part(plan, shares, w)
    slope_b, turned_b = partner_part(plan, [swap(v, "pop", 1) for v in shares], w)
    dz, sums = coefficients(
        total_probes, plan, dists, [near, far, near2, far2], [targets, targets2], row, act, row_act2, head,
        [slope_a, slope_b], slope, turned,
    )

    a2s, b2s = gradient(turned, turned_a, turned_b, dz, 0, 2)
    from_a = [shift_y(v, 1) for v in a2s]
    from_b = [shift_y(v, -1) for v in b2s]
    a1s, b1s, a3s, b3s, a0s, b0s = gradient(turned, turned_a, turned_b, dz, 2, 6)
    outs = []
    for i, size in enumerate(CHUNKS):
        got_1 = shift_y(jnp.concatenate([a1s[i] + from_a[i], b1s[i]], axis=0), 1)
        got_3 = shift_y(jnp.concatenate([a3s[i], b3s[i] + from_b[i]], axis=0), -1)
        got_z = swap(b0s[i] + got_1[2 * size :] + got_3[2 * size :], "dp", 4)
        kept = a0s[i] + got_1[: 2 * size] + got_3[: 2 * size] + got_z
        other = swap(kept[size:], "dp", 12)
        low = z < 2
        outs.append(jnp.concatenate([jnp.where(low, kept[:size], other), jnp.where(low, other, kept[:size])], axis=1))

    ghead = head_gradient(sums, hid, from_b[-1])
    cols = ghead.shape[1] // 16
    heads = ghead[:ACTIONS].reshape(ACTIONS, 4, 4, cols).transpose(2, 1, 0, 3)
    pick = lambda v, i: lax.dynamic_index_in_dim(v, i % 4, 0, keepdims=False)
    heads_y = pick(heads, y)
    for s in (1, 2, 3):
        heads_y = heads_y + shift_y(pick(heads, y + s), s)
    grad_two = pick(heads_y, z)
    for s in (1, 2, 3):
        grad_two = grad_two + shift_z(pick(heads_y, z + s), s)
    return (jnp.concatenate(outs, axis=0)[None], grad_two[None])


def solution(mesh):
    placed = (
        P("dp", None),
        P("dp"),
        P("dp"),
        P("pop", None, None),
        P("pop", None, None),
        P("pop", "dp"),
    )
    return jax.shard_map(
        body,
        mesh=mesh,
        in_specs=placed,
        out_specs=(P("pop", "dp", None), P("pop", None, "dp")),
        check_vma=False,
    )
```

```python
import functools
import math

import jax
import jax.numpy as jnp
from jax import lax
from jax.experimental import pallas as pl
from jax.experimental.pallas import tpu as pltpu
from jax.sharding import PartitionSpec as P

HID = 1024
ACTIONS = 18
PAD = 32
CHUNKS = (80, 48)
EXTRA = 8
SHARES = (0, 2, 4, 6, 1, 3, 5, 7)
STEPS = [(y, z) for y in (2, 1, 3, 0) for z in (0, 3, 1, 2)]
F32 = jnp.float32
BF16 = jnp.bfloat16
NT = (((1,), (1,)), ((), ()))
TN = (((0,), (0,)), ((), ()))
VMEM_SPEC = pl.BlockSpec(memory_space=pltpu.VMEM)
HBM_SPEC = pl.BlockSpec(memory_space=pltpu.HBM)


def params(mib):
    return pltpu.CompilerParams(vmem_limit_bytes=mib * 1024 * 1024)


def cost(us):
    return pl.CostEstimate(flops=int(us * 1.1e9), bytes_accessed=0, transcendentals=0)


def after(value, *first):
    return lax.optimization_barrier((value, first))[0]


def spot():
    place = lax.axis_index("dp")
    return place // 4, place % 4, lax.axis_index("pop") % len(SHARES)


def block_of(z, y, i):
    step_y, step_z = STEPS[i]
    return (z ^ step_z) * 4 + (y + step_y) % 4


def turn(rows_ref, turned_ref, z, y, blocks):
    width = turned_ref.shape[1]
    for i in blocks:
        start = pl.multiple_of(block_of(z, y, i) * width, width)
        turned_ref[i] = rows_ref[:, pl.ds(start, width)].T


def padded(head_ref, wide_ref):
    wide_ref[...] = jnp.zeros_like(wide_ref)
    wide_ref[0:ACTIONS, :] = head_ref[0].astype(F32)


def split3(v):
    hi = v.astype(BF16)
    rest = v - hi.astype(F32)
    mid = rest.astype(BF16)
    low = (rest - mid.astype(F32)).astype(BF16)
    return jnp.concatenate([hi, mid, low], axis=0)


def join3(v):
    return v[:PAD] + v[PAD : 2 * PAD] + v[2 * PAD :]


def row_onehot(start, size, row):
    ids = lax.broadcasted_iota(jnp.int32, (size, row.shape[1]), 0) + start
    return jnp.where(ids == row, 1.0, 0.0).astype(BF16)


def sigmoid(v):
    return 0.5 * jnp.tanh(0.5 * v) + 0.5


def forward_kernel(
    pool_hbm, w_hbm, head_ref, row_ref, act_ref, target_ref, hid_ref, slope_ref, turned_ref, emb_ref, facts_ref,
    acc_ref, pool_ref, w_ref, wide_ref, sems,
):
    z, y, _ = spot()
    rows, hidden = hid_ref.shape
    tile, width = rows // 2, hidden // 2
    row_of = lambda i: pl.ds(i * tile, tile)
    pools = [pltpu.make_async_copy(pool_hbm.at[row_of(i), :], pool_ref.at[row_of(i), :], sems.at[i]) for i in range(2)]
    halves = [
        pltpu.make_async_copy(w_hbm.at[0, :, pl.ds(j * width, width)], w_ref.at[j], sems.at[2 + j]) for j in range(2)
    ]
    for copy in (pools[0], halves[0], halves[1], pools[1]):
        copy.start()
    padded(head_ref, wide_ref)
    facts_ref[0:1, :] = target_ref[...]
    facts_ref[1:2, :] = row_ref[...].astype(F32)
    facts_ref[2:3, :] = act_ref[...].astype(F32)
    facts_ref[3:, :] = jnp.zeros((facts_ref.shape[0] - 3, facts_ref.shape[1]), F32)
    pools[0].wait()
    for i in range(2):
        if i == 1:
            pools[1].wait()
        for j in range(2):
            if i == 0:
                halves[j].wait()
            columns = slice(j * width, (j + 1) * width)
            v = jnp.dot(pool_ref[row_of(i), :], w_ref[j], preferred_element_type=F32)
            sig = sigmoid(v)
            hid = (v * sig).astype(BF16)
            hid_ref[row_of(i), columns] = hid

            @pl.when(z // 2 == j)
            def _():
                slope_ref[row_of(i), :] = sig * (1.0 + v * (1.0 - sig))

            logits = lax.dot_general(wide_ref[:, columns].astype(BF16), hid, NT, preferred_element_type=F32)
            if j == 0:
                acc_ref[:, row_of(i)] = logits
            else:
                acc_ref[:, row_of(i)] += logits
                if i == 1:
                    turn(pool_ref, turned_ref, z, y, range(turned_ref.shape[0]))
    logits = acc_ref[...]
    parts = split3(logits - jnp.sum(logits, axis=0, keepdims=True) / ACTIONS)
    picked = jnp.zeros((3 * PAD, row_ref.shape[1]), F32)
    for i in range(0, rows, 256):
        picked += jnp.dot(parts[:, i : i + 256], row_onehot(i, 256, row_ref[...]), preferred_element_type=F32)
    chosen = lax.broadcasted_iota(jnp.int32, (PAD, row_ref.shape[1]), 0) == act_ref[...]
    emb_ref[...] = jnp.sum(jnp.where(chosen, join3(picked), 0.0), axis=0, keepdims=True)


def forward(pool, w, head, row, act, target):
    rows, feat = pool.shape
    hid = w.shape[2]
    probes = row.shape[1]
    blocks = len(STEPS)
    return pl.pallas_call(
        forward_kernel,
        in_specs=[HBM_SPEC] * 2 + [VMEM_SPEC] * 4,
        out_specs=[VMEM_SPEC] * 5,
        out_shape=[
            jax.ShapeDtypeStruct((rows, hid), BF16),
            jax.ShapeDtypeStruct((rows, hid // 2), F32),
            jax.ShapeDtypeStruct((blocks, feat // blocks, rows), BF16),
            jax.ShapeDtypeStruct((1, probes), F32),
            jax.ShapeDtypeStruct((8, probes), F32),
        ],
        scratch_shapes=[
            pltpu.VMEM((PAD, rows), F32),
            pltpu.VMEM((rows, feat), BF16),
            pltpu.VMEM((2, feat, hid // 2), BF16),
            pltpu.VMEM((PAD, hid), F32),
            pltpu.SemaphoreType.DMA((4,)),
        ],
        compiler_params=params(24),
        cost_estimate=cost(0.3),
        name="forward",
    )(pool, w, head, row, act, target)


def distance_kernel(near_ref, far_ref, facts_ref, out_ref, pack_ref):
    pop = jnp.concatenate([near_ref[...], far_ref[...]], axis=0)
    agents = pop.shape[0]
    lanes = lax.broadcasted_iota(jnp.int32, (agents, 128), 1)
    total = jnp.zeros((agents, 128), F32)
    for i in range(agents):
        gap = pop - pop[i : i + 1, :]
        total = jnp.where(lanes == i, jnp.sum(gap * gap, axis=1, keepdims=True), total)
    out_ref[...] = total
    pack_ref[0:agents, :] = pop
    pack_ref[agents:, :] = facts_ref[...]


def distance_parts(near, far, facts):
    agents, probes = 2 * near.shape[0], near.shape[1]
    return pl.pallas_call(
        distance_kernel,
        in_specs=[VMEM_SPEC] * 3,
        out_specs=[VMEM_SPEC] * 2,
        out_shape=[
            jax.ShapeDtypeStruct((agents, 128), F32),
            jax.ShapeDtypeStruct((agents + facts.shape[0], probes), F32),
        ],
        compiler_params=params(16),
        cost_estimate=cost(0.2),
        name="distances",
    )(near, far, facts)


def partner_kernel(a_ref, b_ref, c_ref, d_ref, w_hbm, slope_ref, turned_ref, rows_ref, w_ref, sem):
    z, y, _ = spot()
    share, width = a_ref.shape[0], w_ref.shape[1]
    columns = pl.ds(pl.multiple_of(z // 2 * width, width), width)
    copy = pltpu.make_async_copy(w_hbm.at[0, :, columns], w_ref, sem)
    copy.start()
    for j, ref in enumerate((a_ref, b_ref, c_ref, d_ref)):
        rows_ref[pl.ds(j * share, share), :] = ref[...].astype(BF16)
    copy.wait()
    v = jnp.dot(rows_ref[...], w_ref[...], preferred_element_type=F32)
    sig = sigmoid(v)
    slope_ref[...] = sig * (1.0 + v * (1.0 - sig))
    turn(rows_ref, turned_ref, z, y, range(turned_ref.shape[0]))


def partner_part(shares, w):
    share, feat = shares[0].shape
    half = w.shape[2] // 2
    blocks = len(STEPS)
    return pl.pallas_call(
        partner_kernel,
        in_specs=[VMEM_SPEC] * 4 + [HBM_SPEC],
        out_specs=[VMEM_SPEC] * 2,
        out_shape=[
            jax.ShapeDtypeStruct((4 * share, half), F32),
            jax.ShapeDtypeStruct((blocks, feat // blocks, 4 * share), BF16),
        ],
        scratch_shapes=[
            pltpu.VMEM((4 * share, feat), BF16),
            pltpu.VMEM((feat, half), BF16),
            pltpu.SemaphoreType.DMA(()),
        ],
        compiler_params=params(16),
        cost_estimate=cost(0.3),
        name="partner",
    )(*shares, w)


def coeff_kernel(
    total_probes, scaling, d0, d1, near_ref, far_ref, facts_ref, pack_ref, head_ref,
    slope_a_ref, slope_b_ref, slope_ref, hid_ref, dz_ref, heads_ref, sums_ref, wide_ref, ghead_ref,
):
    z, y, share_place = spot()
    width = slope_ref.shape[1]
    columns = pl.ds(pl.multiple_of(z // 2 * width, width), width)
    padded(head_ref, wide_ref)
    pop = jnp.concatenate([near_ref[...], far_ref[...]], axis=0)
    agents = pop.shape[0]
    pop2 = pack_ref[0:agents, :]
    row, act = facts_ref[1:2, :].astype(jnp.int32), facts_ref[2:3, :].astype(jnp.int32)
    row2 = pack_ref[agents + 1 : agents + 2, :].astype(jnp.int32)
    act2 = pack_ref[agents + 2 : agents + 3, :].astype(jnp.int32)
    lanes = lax.broadcasted_iota(jnp.int32, (agents, 128), 1)
    subs = lax.broadcasted_iota(jnp.int32, (agents, 128), 0)
    kern = jnp.exp(-(d0[...] + d1[...]) / total_probes)
    system = jnp.where(lanes < agents, kern, jnp.where((lanes == agents) & (subs == 0), 1.0, 0.0))
    for k in range(agents):
        pivot_row = system[k : k + 1, :] / system[k : k + 1, k : k + 1]
        system = jnp.where(subs == k, pivot_row, system - system[:, k : k + 1] * pivot_row)
    mix = system[:, agents : agents + 1] * kern[:, 0:1]

    def marked(people, target, act):
        emb = people[0:1, :]
        pulled = jnp.sum(mix * people, axis=0, keepdims=True)
        diverse = 2.0 * (jnp.sum(mix, axis=0, keepdims=True) * emb - pulled)
        coeff = scaling * (emb - target) + scaling * diverse
        chosen = lax.broadcasted_iota(jnp.int32, (PAD, act.shape[1]), 0) == act
        return split3(jnp.where(chosen, coeff, 0.0))

    head = wide_ref[:, columns]
    centered = head - jnp.sum(head, axis=0, keepdims=True) / ACTIONS
    cent_hi = centered.astype(BF16)
    cent_lo = (centered - cent_hi.astype(F32)).astype(BF16)
    cents = jnp.concatenate([cent_hi, cent_lo, cent_hi], axis=0)

    def scaled(sums, slope):
        part_hi = sums.astype(BF16)
        part_lo = (sums - part_hi.astype(F32)).astype(BF16)
        stacked = jnp.concatenate([part_hi, part_hi, part_lo], axis=0)
        pulls = lax.dot_general(stacked, cents, TN, preferred_element_type=F32)
        return (pulls * slope).astype(BF16)

    rows = slope_ref.shape[0]
    tile = 256
    mine = marked(pop, facts_ref[0:1, :], act)
    theirs = marked(pop2, pack_ref[agents : agents + 1, :], act2)
    for i in range(rows // tile):
        here = pl.ds(i * tile, tile)
        hot = row_onehot(i * tile, tile, row)
        sums_ref[:, here] = join3(lax.dot_general(mine, hot, NT, preferred_element_type=F32))
    share = rows // len(SHARES)
    per = slope_a_ref.shape[0] // tile
    for i in range(rows // tile):
        hot = jnp.concatenate(
            [
                row_onehot((share_place ^ SHARES[j]) * share, share, row2)
                for j in range(i * tile // share, (i + 1) * tile // share)
            ],
            axis=0,
        )
        sums = join3(lax.dot_general(theirs, hot, NT, preferred_element_type=F32))
        slope2_ref = slope_a_ref if i < per else slope_b_ref
        dz_ref[pl.ds(rows + i * tile, tile), :] = scaled(sums, slope2_ref[pl.ds(i % per * tile, tile), :])
    for i in range(rows // tile):
        here = pl.ds(i * tile, tile)
        dz_ref[here, :] = scaled(sums_ref[:, here], slope_ref[here, :])


    sums = sums_ref[...]
    even = split3(sums - jnp.sum(sums, axis=0, keepdims=True) / ACTIONS)
    ghead_ref[...] = join3(jnp.dot(even, hid_ref[...], preferred_element_type=F32))
    blocks = heads_ref.shape[0]
    cols = ghead_ref.shape[1] // blocks
    for i in range(blocks):
        place = block_of(z, y, i)
        pair = ghead_ref[:, pl.ds(pl.multiple_of(place // 2 * 2 * cols, 2 * cols), 2 * cols)]
        mine = jnp.where(place % 2 == 0, pair[:, :cols], pair[:, cols:])
        laid = [mine[g * EXTRA : (g + 1) * EXTRA] for g in range(3)]
        rest = jnp.zeros((EXTRA, heads_ref.shape[2] - 3 * cols), F32)
        heads_ref[i] = jnp.concatenate(laid + [rest], axis=1)


def coefficients(total_probes, dists, near, far, facts, pack, head, slopes, slope, hid):
    rows, width = hid.shape
    scaling = math.sqrt(HID / total_probes)
    return pl.pallas_call(
        functools.partial(coeff_kernel, total_probes, scaling),
        in_specs=[VMEM_SPEC] * 11,
        out_specs=[VMEM_SPEC] * 2,
        out_shape=[
            jax.ShapeDtypeStruct((2 * rows, width // 2), BF16),
            jax.ShapeDtypeStruct((len(STEPS), EXTRA, width // 2), F32),
        ],
        scratch_shapes=[
            pltpu.VMEM((PAD, rows), F32),
            pltpu.VMEM((PAD, width), F32),
            pltpu.VMEM((PAD, width), F32),
        ],
        compiler_params=params(16),
        cost_estimate=cost(0.3),
        name="coefficients",
    )(*dists, near, far, facts, pack, head, *slopes, slope, hid)


def grad_kernel(first, per, chunks, own_ref, a_ref, b_ref, dz_ref, heads_ref, *out_refs):
    mine, part = own_ref.shape[2], a_ref.shape[2]
    begin, end = chunks[0][0], chunks[-1][0] + chunks[-1][1]
    rows, width = end - begin, dz_ref.shape[1]
    for g in range(len(out_refs) // len(chunks)):
        for p in range(0, per, 2):
            block = first + g * per + p
            total = jnp.zeros((2 * rows, width), F32)
            for ref, start, depth in ((own_ref, 0, mine), (a_ref, mine, part), (b_ref, mine + part, part)):
                left = ref[block : block + 2, begin:end, :].reshape(2 * rows, depth)
                total += jnp.dot(left, dz_ref[start : start + depth, :], preferred_element_type=F32)
            for q in range(2):
                for c, (at, size, extra) in enumerate(chunks):
                    out_ref = out_refs[g * len(chunks) + c]
                    from_row = q * rows + at - begin
                    out_ref[p + q, 0:size, :] = total[from_row : from_row + size]
                    if extra:
                        out_ref[p + q, size:, :] = heads_ref[block + q]


def gradient(own, a, b, dz, heads, first, per, groups, which):
    width = dz.shape[1]
    chunks = [(sum(CHUNKS[:c]), CHUNKS[c], c == len(CHUNKS) - 1) for c in which]
    shapes = [
        jax.ShapeDtypeStruct((per, size + (EXTRA if extra else 0), width), F32)
        for _ in range(groups)
        for _, size, extra in chunks
    ]
    outs = pl.pallas_call(
        functools.partial(grad_kernel, first, per, chunks),
        in_specs=[VMEM_SPEC] * 5,
        out_specs=[VMEM_SPEC] * len(shapes),
        out_shape=shapes,
        compiler_params=params(16),
        cost_estimate=cost(0.3),
        name="gradient",
    )(own, a, b, dz, heads)
    return [outs[i : i + len(chunks)] for i in range(0, len(outs), len(chunks))]


def add_kernel(at, into_ref, more_ref, out_ref):
    here = slice(at, at + more_ref.shape[0])
    out_ref[here] = into_ref[here] + more_ref[...]


def add_into(into, more, at):
    return pl.pallas_call(
        functools.partial(add_kernel, at),
        in_specs=[VMEM_SPEC] * 2,
        out_specs=VMEM_SPEC,
        out_shape=jax.ShapeDtypeStruct(into.shape, F32),
        input_output_aliases={0: 0},
        compiler_params=params(16),
        cost_estimate=cost(0.1),
        name="add_into",
    )(into, more)


def fold_kernel(a_ref, b_ref, c_ref, *out_refs):
    for i, out_ref in enumerate(out_refs):
        out_ref[...] = a_ref[i] + (b_ref[i] + c_ref[i])


def fold(a, b, c):
    blocks = a.shape[0]
    return pl.pallas_call(
        fold_kernel,
        in_specs=[VMEM_SPEC] * 3,
        out_specs=[VMEM_SPEC] * blocks,
        out_shape=[jax.ShapeDtypeStruct(a.shape[1:], F32)] * blocks,
        compiler_params=params(16),
        cost_estimate=cost(0.1),
        name="fold",
    )(a, b, c)


def finish_kernel(*refs):
    out_ref, two_ref = refs[-2:]
    z, _, _ = spot()
    width = refs[0].shape[1]
    left = pl.ds(pl.multiple_of(z // 2 * width, width), width)
    right = pl.ds(pl.multiple_of((1 - z // 2) * width, width), width)
    at = 0
    for c, size in enumerate(CHUNKS):
        own, one, two, three = refs[4 * c : 4 * c + 4]
        out_ref[0, at : at + size, left] = own[0:size, :] + one[0:size, :]
        out_ref[0, at : at + size, right] = two[0:size, :] + three[0:size, :]
        at += size
    heads = sum(ref[CHUNKS[-1] :, :] for ref in refs[-6:-2])
    cols = two_ref.shape[2]
    for g in range(3):
        count = min(EXTRA, ACTIONS - g * EXTRA)
        two_ref[0, g * EXTRA : g * EXTRA + count, :] = heads[0:count, g * cols : (g + 1) * cols]


def finish(pieces, cols):
    rows, width = sum(CHUNKS), pieces[0].shape[1]
    return pl.pallas_call(
        finish_kernel,
        grid=(1,),
        in_specs=[VMEM_SPEC] * len(pieces),
        out_specs=[
            pl.BlockSpec((1, rows, 2 * width), lambda i: (0, 0, 0)),
            pl.BlockSpec((1, ACTIONS, cols), lambda i: (0, 0, 0)),
        ],
        out_shape=[
            jax.ShapeDtypeStruct((1, rows, 2 * width), F32),
            jax.ShapeDtypeStruct((1, ACTIONS, cols), F32),
        ],
        compiler_params=params(16),
        cost_estimate=cost(0.1),
        name="finish",
    )(*pieces)


def shift_y(v, s):
    return lax.ppermute(v, "dp", [(z * 4 + y, z * 4 + (y + s) % 4) for z in range(4) for y in range(4)])


def swap(v, axis, mask):
    return lax.ppermute(v, axis, [(i, i ^ mask) for i in range(16)])


def to_partner_rows(v):
    return lax.ppermute(
        v,
        ("pop", "dp"),
        [(p * 16 + d, (p ^ (8 if d // 4 in (0, 3) else 0)) * 16 + (d ^ 12)) for p in range(16) for d in range(16)],
    )


def body(state_pool, probe_row, action, w_hidden, w_head, targets):
    probes = probe_row.shape[0]
    total_probes = probes * lax.axis_size("dp")
    share = state_pool.shape[0] // len(SHARES)
    row = probe_row.reshape(1, probes)
    act = action.reshape(1, probes)

    _, _, where = spot()
    cut = lambda i: lax.dynamic_slice_in_dim(state_pool, i * share, share, 0).astype(F32)
    share0 = to_partner_rows(cut(where))
    share4 = to_partner_rows(cut(where ^ 4))

    hid, slope, turned, near, facts = forward(state_pool, w_hidden, w_head, row, act, targets)
    for mask in (1, 2):
        near = jnp.concatenate([near, swap(near, "pop", mask)], axis=0)
    share0 = after(share0, near)
    near = jnp.concatenate([near, swap(near, "pop", 4)], axis=0)
    share2, share6 = swap(share0, "pop", 2), swap(share0, "pop", 6)
    far = swap(near, "pop", 8)
    part, pack = distance_parts(near, far, facts)
    part = part + swap(part, "dp", 1)
    pack = after(pack, part)
    part = part + swap(part, "dp", 2)
    pack = swap(pack, "dp", 12)
    part = part + swap(part, "dp", 4)
    dists = [part, swap(part, "dp", 8)]

    shares = after([share0, share2, share4, share6], part)
    slopes_a, turned_a = partner_part(shares, w_hidden)
    slopes_b, turned_b = partner_part([swap(v, "pop", 1) for v in shares], w_hidden)
    dz, heads = coefficients(
        total_probes, dists, near, far, facts, pack, w_head, [slopes_a, slopes_b], slope, hid
    )

    count = len(CHUNKS)
    a2s, b2s = gradient(turned, turned_a, turned_b, dz, heads, 0, 2, 2, range(count))
    from_a, from_b = [], []
    for i in range(count):
        from_a.append(shift_y(a2s[i], 1))
        from_b.append(shift_y(b2s[i], -1))
    pieces = []
    for i in range(count):
        (ones,), (threes,), (zeros,) = gradient(turned, turned_a, turned_b, dz, heads, 4, 4, 3, [i])
        ones, threes = add_into(ones, from_a[i], 0), add_into(threes, from_b[i], 2)
        dz = after(dz, ones, threes)
        own, to_3, to_1, to_2 = fold(zeros, shift_y(ones, 1), shift_y(threes, -1))
        three, two, one = swap(to_3, "dp", 12), swap(to_2, "dp", 8), swap(to_1, "dp", 4)
        pieces += [own, one, two, three]
    return tuple(finish(pieces, w_head.shape[2] // 16))


def solution(mesh):
    placed = (
        P("dp", None),
        P("dp"),
        P("dp"),
        P("pop", None, None),
        P("pop", None, None),
        P("pop", "dp"),
    )
    return jax.shard_map(
        body,
        mesh=mesh,
        in_specs=placed,
        out_specs=(P("pop", "dp", None), P("pop", None, "dp")),
        check_vma=False,
    )
```

```python
import functools
import math

import jax
import jax.numpy as jnp
from jax import lax
from jax.experimental import pallas as pl
from jax.experimental.pallas import tpu as pltpu
from jax.sharding import PartitionSpec as P

HID = 1024
ACTIONS = 18
PAD = 32
CHUNKS = (64, 64)
EXTRA = 8
SHARES = (0, 2, 4, 6, 1, 3, 5, 7)
STEPS = [(y, z) for y in (2, 1, 3, 0) for z in (0, 3, 1, 2)]
F32 = jnp.float32
BF16 = jnp.bfloat16
NT = (((1,), (1,)), ((), ()))
TN = (((0,), (0,)), ((), ()))
VMEM_SPEC = pl.BlockSpec(memory_space=pltpu.VMEM)
HBM_SPEC = pl.BlockSpec(memory_space=pltpu.HBM)


def params(mib):
    return pltpu.CompilerParams(vmem_limit_bytes=mib * 1024 * 1024)


def cost(us):
    return pl.CostEstimate(flops=int(us * 1.1e9), bytes_accessed=0, transcendentals=0)


def after(value, *first):
    return lax.optimization_barrier((value, first))[0]


def spot():
    place = lax.axis_index("dp")
    return place // 4, place % 4, lax.axis_index("pop") % len(SHARES)


def block_of(z, y, i):
    step_y, step_z = STEPS[i]
    return (z ^ step_z) * 4 + (y + step_y) % 4


def turn(rows_ref, turned_ref, z, y, blocks):
    width = turned_ref.shape[1]
    for i in blocks:
        start = pl.multiple_of(block_of(z, y, i) * width, width)
        turned_ref[i] = rows_ref[:, pl.ds(start, width)].T


def padded(head_ref, wide_ref):
    wide_ref[...] = jnp.zeros_like(wide_ref)
    wide_ref[0:ACTIONS, :] = head_ref[0].astype(F32)


def split3(v):
    hi = v.astype(BF16)
    rest = v - hi.astype(F32)
    mid = rest.astype(BF16)
    low = (rest - mid.astype(F32)).astype(BF16)
    return jnp.concatenate([hi, mid, low], axis=0)


def join3(v):
    return v[:PAD] + v[PAD : 2 * PAD] + v[2 * PAD :]


def row_onehot(start, size, row):
    ids = lax.broadcasted_iota(jnp.int32, (size, row.shape[1]), 0) + start
    return jnp.where(ids == row, 1.0, 0.0).astype(BF16)


def sigmoid(v):
    return 0.5 * jnp.tanh(0.5 * v) + 0.5


def forward_kernel(
    pool_hbm, w_hbm, head_ref, row_ref, act_ref, target_ref, hid_ref, slope_ref, turned_ref, emb_ref, facts_ref,
    acc_ref, pool_ref, w_ref, wide_ref, sems,
):
    z, y, _ = spot()
    rows, hidden = hid_ref.shape
    tile, width = rows // 2, hidden // 2
    row_of = lambda i: pl.ds(i * tile, tile)
    pools = [pltpu.make_async_copy(pool_hbm.at[row_of(i), :], pool_ref.at[row_of(i), :], sems.at[i]) for i in range(2)]
    halves = [
        pltpu.make_async_copy(w_hbm.at[0, :, pl.ds(j * width, width)], w_ref.at[j], sems.at[2 + j]) for j in range(2)
    ]
    for copy in (pools[0], halves[0], halves[1], pools[1]):
        copy.start()
    padded(head_ref, wide_ref)
    facts_ref[0:1, :] = target_ref[...]
    facts_ref[1:2, :] = row_ref[...].astype(F32)
    facts_ref[2:3, :] = act_ref[...].astype(F32)
    facts_ref[3:, :] = jnp.zeros((facts_ref.shape[0] - 3, facts_ref.shape[1]), F32)
    pools[0].wait()
    for i in range(2):
        if i == 1:
            pools[1].wait()
        for j in range(2):
            if i == 0:
                halves[j].wait()
            columns = slice(j * width, (j + 1) * width)
            v = jnp.dot(pool_ref[row_of(i), :], w_ref[j], preferred_element_type=F32)
            sig = sigmoid(v)
            hid = (v * sig).astype(BF16)
            hid_ref[row_of(i), columns] = hid

            @pl.when(z // 2 == j)
            def _():
                slope_ref[row_of(i), :] = sig * (1.0 + v * (1.0 - sig))

            logits = lax.dot_general(wide_ref[:, columns].astype(BF16), hid, NT, preferred_element_type=F32)
            if j == 0:
                acc_ref[:, row_of(i)] = logits
            else:
                acc_ref[:, row_of(i)] += logits
                if i == 1:
                    turn(pool_ref, turned_ref, z, y, range(turned_ref.shape[0]))
    logits = acc_ref[...]
    parts = split3(logits - jnp.sum(logits, axis=0, keepdims=True) / ACTIONS)
    picked = jnp.zeros((3 * PAD, row_ref.shape[1]), F32)
    for i in range(0, rows, 256):
        picked += jnp.dot(parts[:, i : i + 256], row_onehot(i, 256, row_ref[...]), preferred_element_type=F32)
    chosen = lax.broadcasted_iota(jnp.int32, (PAD, row_ref.shape[1]), 0) == act_ref[...]
    emb_ref[...] = jnp.sum(jnp.where(chosen, join3(picked), 0.0), axis=0, keepdims=True)


def forward(pool, w, head, row, act, target):
    rows, feat = pool.shape
    hid = w.shape[2]
    probes = row.shape[1]
    blocks = len(STEPS)
    return pl.pallas_call(
        forward_kernel,
        in_specs=[HBM_SPEC] * 2 + [VMEM_SPEC] * 4,
        out_specs=[VMEM_SPEC] * 5,
        out_shape=[
            jax.ShapeDtypeStruct((rows, hid), BF16),
            jax.ShapeDtypeStruct((rows, hid // 2), F32),
            jax.ShapeDtypeStruct((blocks, feat // blocks, rows), BF16),
            jax.ShapeDtypeStruct((1, probes), F32),
            jax.ShapeDtypeStruct((8, probes), F32),
        ],
        scratch_shapes=[
            pltpu.VMEM((PAD, rows), F32),
            pltpu.VMEM((rows, feat), BF16),
            pltpu.VMEM((2, feat, hid // 2), BF16),
            pltpu.VMEM((PAD, hid), F32),
            pltpu.SemaphoreType.DMA((4,)),
        ],
        compiler_params=params(42),
        cost_estimate=cost(0.3),
        name="forward",
    )(pool, w, head, row, act, target)


def distance_kernel(near_ref, far_ref, facts_ref, out_ref, pack_ref):
    pop = jnp.concatenate([near_ref[...], far_ref[...]], axis=0)
    agents = pop.shape[0]
    lanes = lax.broadcasted_iota(jnp.int32, (agents, 128), 1)
    total = jnp.zeros((agents, 128), F32)
    for i in range(agents):
        gap = pop - pop[i : i + 1, :]
        total = jnp.where(lanes == i, jnp.sum(gap * gap, axis=1, keepdims=True), total)
    out_ref[...] = total
    pack_ref[0:agents, :] = pop
    pack_ref[agents:, :] = facts_ref[...]


def distance_parts(near, far, facts):
    agents, probes = 2 * near.shape[0], near.shape[1]
    return pl.pallas_call(
        distance_kernel,
        in_specs=[VMEM_SPEC] * 3,
        out_specs=[VMEM_SPEC] * 2,
        out_shape=[
            jax.ShapeDtypeStruct((agents, 128), F32),
            jax.ShapeDtypeStruct((agents + facts.shape[0], probes), F32),
        ],
        compiler_params=params(16),
        cost_estimate=cost(0.2),
        name="distances",
    )(near, far, facts)


def partner_kernel(a_ref, b_ref, c_ref, d_ref, w_hbm, slope_ref, turned_ref, rows_ref, w_ref, sem):
    z, y, _ = spot()
    share, width = a_ref.shape[0], w_ref.shape[1]
    columns = pl.ds(pl.multiple_of(z // 2 * width, width), width)
    copy = pltpu.make_async_copy(w_hbm.at[0, :, columns], w_ref, sem)
    copy.start()
    for j, ref in enumerate((a_ref, b_ref, c_ref, d_ref)):
        rows_ref[pl.ds(j * share, share), :] = ref[...].astype(BF16)
    copy.wait()
    v = jnp.dot(rows_ref[...], w_ref[...], preferred_element_type=F32)
    sig = sigmoid(v)
    slope_ref[...] = sig * (1.0 + v * (1.0 - sig))
    turn(rows_ref, turned_ref, z, y, range(turned_ref.shape[0]))


def partner_part(shares, w):
    share, feat = shares[0].shape
    half = w.shape[2] // 2
    blocks = len(STEPS)
    return pl.pallas_call(
        partner_kernel,
        in_specs=[VMEM_SPEC] * 4 + [HBM_SPEC],
        out_specs=[VMEM_SPEC] * 2,
        out_shape=[
            jax.ShapeDtypeStruct((4 * share, half), F32),
            jax.ShapeDtypeStruct((blocks, feat // blocks, 4 * share), BF16),
        ],
        scratch_shapes=[
            pltpu.VMEM((4 * share, feat), BF16),
            pltpu.VMEM((feat, half), BF16),
            pltpu.SemaphoreType.DMA(()),
        ],
        compiler_params=params(16),
        cost_estimate=cost(0.3),
        name="partner",
    )(*shares, w)


def coeff_kernel(
    total_probes, scaling, d0, d1, near_ref, far_ref, facts_ref, pack_ref, head_ref,
    slope_a_ref, slope_b_ref, slope_ref, hid_ref, dz_ref, heads_ref, sums_ref, wide_ref, ghead_ref,
):
    z, y, share_place = spot()
    width = slope_ref.shape[1]
    columns = pl.ds(pl.multiple_of(z // 2 * width, width), width)
    padded(head_ref, wide_ref)
    pop = jnp.concatenate([near_ref[...], far_ref[...]], axis=0)
    agents = pop.shape[0]
    pop2 = pack_ref[0:agents, :]
    row, act = facts_ref[1:2, :].astype(jnp.int32), facts_ref[2:3, :].astype(jnp.int32)
    row2 = pack_ref[agents + 1 : agents + 2, :].astype(jnp.int32)
    act2 = pack_ref[agents + 2 : agents + 3, :].astype(jnp.int32)
    lanes = lax.broadcasted_iota(jnp.int32, (agents, 128), 1)
    subs = lax.broadcasted_iota(jnp.int32, (agents, 128), 0)
    kern = jnp.exp(-(d0[...] + d1[...]) / total_probes)
    system = jnp.where(lanes < agents, kern, jnp.where((lanes == agents) & (subs == 0), 1.0, 0.0))
    for k in range(agents):
        pivot_row = system[k : k + 1, :] / system[k : k + 1, k : k + 1]
        system = jnp.where(subs == k, pivot_row, system - system[:, k : k + 1] * pivot_row)
    mix = system[:, agents : agents + 1] * kern[:, 0:1]

    def marked(people, target, act):
        emb = people[0:1, :]
        pulled = jnp.sum(mix * people, axis=0, keepdims=True)
        diverse = 2.0 * (jnp.sum(mix, axis=0, keepdims=True) * emb - pulled)
        coeff = scaling * (emb - target) + scaling * diverse
        chosen = lax.broadcasted_iota(jnp.int32, (PAD, act.shape[1]), 0) == act
        return split3(jnp.where(chosen, coeff, 0.0))

    head = wide_ref[:, columns]
    centered = head - jnp.sum(head, axis=0, keepdims=True) / ACTIONS
    cent_hi = centered.astype(BF16)
    cent_lo = (centered - cent_hi.astype(F32)).astype(BF16)
    cents = jnp.concatenate([cent_hi, cent_lo, cent_hi], axis=0)

    def scaled(sums, slope):
        part_hi = sums.astype(BF16)
        part_lo = (sums - part_hi.astype(F32)).astype(BF16)
        stacked = jnp.concatenate([part_hi, part_hi, part_lo], axis=0)
        pulls = lax.dot_general(stacked, cents, TN, preferred_element_type=F32)
        return (pulls * slope).astype(BF16)

    rows = slope_ref.shape[0]
    tile = 256
    mine = marked(pop, facts_ref[0:1, :], act)
    theirs = marked(pop2, pack_ref[agents : agents + 1, :], act2)
    for i in range(rows // tile):
        here = pl.ds(i * tile, tile)
        hot = row_onehot(i * tile, tile, row)
        sums_ref[:, here] = join3(lax.dot_general(mine, hot, NT, preferred_element_type=F32))
    share = rows // len(SHARES)
    per = slope_a_ref.shape[0] // tile
    for i in range(rows // tile):
        hot = jnp.concatenate(
            [
                row_onehot((share_place ^ SHARES[j]) * share, share, row2)
                for j in range(i * tile // share, (i + 1) * tile // share)
            ],
            axis=0,
        )
        sums = join3(lax.dot_general(theirs, hot, NT, preferred_element_type=F32))
        slope2_ref = slope_a_ref if i < per else slope_b_ref
        dz_ref[pl.ds(rows + i * tile, tile), :] = scaled(sums, slope2_ref[pl.ds(i % per * tile, tile), :])
    for i in range(rows // tile):
        here = pl.ds(i * tile, tile)
        dz_ref[here, :] = scaled(sums_ref[:, here], slope_ref[here, :])


    sums = sums_ref[...]
    even = split3(sums - jnp.sum(sums, axis=0, keepdims=True) / ACTIONS)
    ghead_ref[...] = join3(jnp.dot(even, hid_ref[...], preferred_element_type=F32))
    blocks = heads_ref.shape[0]
    cols = ghead_ref.shape[1] // blocks
    for i in range(blocks):
        place = block_of(z, y, i)
        pair = ghead_ref[:, pl.ds(pl.multiple_of(place // 2 * 2 * cols, 2 * cols), 2 * cols)]
        mine = jnp.where(place % 2 == 0, pair[:, :cols], pair[:, cols:])
        laid = [mine[g * EXTRA : (g + 1) * EXTRA] for g in range(3)]
        rest = jnp.zeros((EXTRA, heads_ref.shape[2] - 3 * cols), F32)
        heads_ref[i] = jnp.concatenate(laid + [rest], axis=1)


def coefficients(total_probes, dists, near, far, facts, pack, head, slopes, slope, hid):
    rows, width = hid.shape
    scaling = math.sqrt(HID / total_probes)
    return pl.pallas_call(
        functools.partial(coeff_kernel, total_probes, scaling),
        in_specs=[VMEM_SPEC] * 11,
        out_specs=[VMEM_SPEC] * 2,
        out_shape=[
            jax.ShapeDtypeStruct((2 * rows, width // 2), BF16),
            jax.ShapeDtypeStruct((len(STEPS), EXTRA, width // 2), F32),
        ],
        scratch_shapes=[
            pltpu.VMEM((PAD, rows), F32),
            pltpu.VMEM((PAD, width), F32),
            pltpu.VMEM((PAD, width), F32),
        ],
        compiler_params=params(16),
        cost_estimate=cost(0.3),
        name="coefficients",
    )(*dists, near, far, facts, pack, head, *slopes, slope, hid)


def grad_kernel(first, per, chunks, own_ref, a_ref, b_ref, dz_ref, heads_ref, *out_refs):
    mine, part = own_ref.shape[2], a_ref.shape[2]
    begin, end = chunks[0][0], chunks[-1][0] + chunks[-1][1]
    rows, width = end - begin, dz_ref.shape[1]
    for g in range(len(out_refs) // len(chunks)):
        for p in range(0, per, 2):
            block = first + g * per + p
            total = jnp.zeros((2 * rows, width), F32)
            for ref, start, depth in ((own_ref, 0, mine), (a_ref, mine, part), (b_ref, mine + part, part)):
                left = ref[block : block + 2, begin:end, :].reshape(2 * rows, depth)
                total += jnp.dot(left, dz_ref[start : start + depth, :], preferred_element_type=F32)
            for q in range(2):
                for c, (at, size, extra) in enumerate(chunks):
                    out_ref = out_refs[g * len(chunks) + c]
                    from_row = q * rows + at - begin
                    out_ref[p + q, 0:size, :] = total[from_row : from_row + size]
                    if extra:
                        out_ref[p + q, size:, :] = heads_ref[block + q]


def gradient(own, a, b, dz, heads, first, per, groups, which):
    width = dz.shape[1]
    chunks = [(sum(CHUNKS[:c]), CHUNKS[c], c == len(CHUNKS) - 1) for c in which]
    shapes = [
        jax.ShapeDtypeStruct((per, size + (EXTRA if extra else 0), width), F32)
        for _ in range(groups)
        for _, size, extra in chunks
    ]
    outs = pl.pallas_call(
        functools.partial(grad_kernel, first, per, chunks),
        in_specs=[VMEM_SPEC] * 5,
        out_specs=[VMEM_SPEC] * len(shapes),
        out_shape=shapes,
        compiler_params=params(16),
        cost_estimate=cost(0.3),
        name="gradient",
    )(own, a, b, dz, heads)
    return [outs[i : i + len(chunks)] for i in range(0, len(outs), len(chunks))]


def add_kernel(at, into_ref, more_ref, out_ref):
    here = slice(at, at + more_ref.shape[0])
    out_ref[here] = into_ref[here] + more_ref[...]


def add_into(into, more, at):
    return pl.pallas_call(
        functools.partial(add_kernel, at),
        in_specs=[VMEM_SPEC] * 2,
        out_specs=VMEM_SPEC,
        out_shape=jax.ShapeDtypeStruct(into.shape, F32),
        input_output_aliases={0: 0},
        compiler_params=params(16),
        cost_estimate=cost(0.1),
        name="add_into",
    )(into, more)


def fold_kernel(a_ref, b_ref, c_ref, *out_refs):
    for i, out_ref in enumerate(out_refs):
        out_ref[...] = a_ref[i] + (b_ref[i] + c_ref[i])


def fold(a, b, c):
    blocks = a.shape[0]
    return pl.pallas_call(
        fold_kernel,
        in_specs=[VMEM_SPEC] * 3,
        out_specs=[VMEM_SPEC] * blocks,
        out_shape=[jax.ShapeDtypeStruct(a.shape[1:], F32)] * blocks,
        compiler_params=params(16),
        cost_estimate=cost(0.1),
        name="fold",
    )(a, b, c)


def finish_kernel(*refs):
    out_ref, two_ref = refs[-2:]
    z, _, _ = spot()
    width = refs[0].shape[1]
    left = pl.ds(pl.multiple_of(z // 2 * width, width), width)
    right = pl.ds(pl.multiple_of((1 - z // 2) * width, width), width)
    at = 0
    for c, size in enumerate(CHUNKS):
        own, one, two, three = refs[4 * c : 4 * c + 4]
        out_ref[0, at : at + size, left] = own[0:size, :] + one[0:size, :]
        out_ref[0, at : at + size, right] = two[0:size, :] + three[0:size, :]
        at += size
    heads = sum(ref[CHUNKS[-1] :, :] for ref in refs[-6:-2])
    cols = two_ref.shape[2]
    for g in range(3):
        count = min(EXTRA, ACTIONS - g * EXTRA)
        two_ref[g * EXTRA : g * EXTRA + count] = heads[0:count, g * cols : (g + 1) * cols].reshape(count, 1, cols)


def finish(pieces, cols):
    rows, width = sum(CHUNKS), pieces[0].shape[1]
    return pl.pallas_call(
        finish_kernel,
        grid=(1,),
        in_specs=[VMEM_SPEC] * len(pieces),
        out_specs=[
            pl.BlockSpec((1, rows, 2 * width), lambda i: (0, 0, 0)),
            pl.BlockSpec((ACTIONS, 1, cols), lambda i: (0, 0, 0)),
        ],
        out_shape=[
            jax.ShapeDtypeStruct((1, rows, 2 * width), F32),
            jax.ShapeDtypeStruct((ACTIONS, 1, cols), F32),
        ],
        compiler_params=params(16),
        cost_estimate=cost(0.1),
        name="finish",
    )(*pieces)


def shift_y(v, s):
    return lax.ppermute(v, "dp", [(z * 4 + y, z * 4 + (y + s) % 4) for z in range(4) for y in range(4)])


def swap(v, axis, mask):
    return lax.ppermute(v, axis, [(i, i ^ mask) for i in range(16)])


def to_partner_rows(v):
    return lax.ppermute(
        v,
        ("pop", "dp"),
        [(p * 16 + d, (p ^ (8 if d // 4 in (0, 3) else 0)) * 16 + (d ^ 12)) for p in range(16) for d in range(16)],
    )


def body(state_pool, probe_row, action, w_hidden, w_head, targets):
    probes = probe_row.shape[0]
    total_probes = probes * lax.axis_size("dp")
    share = state_pool.shape[0] // len(SHARES)
    row = probe_row.reshape(1, probes)
    act = action.reshape(1, probes)

    _, _, where = spot()
    cut = lambda i: lax.dynamic_slice_in_dim(state_pool, i * share, share, 0).astype(F32)
    share0 = to_partner_rows(cut(where))
    next_share = cut(where ^ 4)

    hid, slope, turned, near, facts = forward(state_pool, w_hidden, w_head, row, act, targets)
    for mask in (1, 2, 4):
        near = jnp.concatenate([near, swap(near, "pop", mask)], axis=0)
    far = swap(near, "pop", 8)
    share4 = to_partner_rows(after(next_share, far))
    share0 = after(share0, far)
    share2, share6 = swap(share0, "pop", 2), swap(share0, "pop", 6)
    part, pack = distance_parts(near, far, facts)
    part = part + swap(part, "dp", 1)
    pack = after(pack, part)
    part = part + swap(part, "dp", 2)
    pack = swap(pack, "dp", 12)
    part = part + swap(part, "dp", 4)
    dists = [part, swap(part, "dp", 8)]

    shares = after([share0, share2, share4, share6], part)
    slopes_a, turned_a = partner_part(shares, w_hidden)
    slopes_b, turned_b = partner_part([swap(v, "pop", 1) for v in shares], w_hidden)
    dz, heads = coefficients(
        total_probes, dists, near, far, facts, pack, w_head, [slopes_a, slopes_b], slope, hid
    )

    count = len(CHUNKS)
    a2s, b2s = gradient(turned, turned_a, turned_b, dz, heads, 0, 2, 2, range(count))
    from_a, from_b = [], []
    for i in range(count):
        from_a.append(shift_y(a2s[i], 1))
        from_b.append(shift_y(b2s[i], -1))
    pieces = []
    for i in range(count):
        (ones,), (threes,), (zeros,) = gradient(turned, turned_a, turned_b, dz, heads, 4, 4, 3, [i])
        ones, threes = add_into(ones, from_a[i], 0), add_into(threes, from_b[i], 2)
        dz = after(dz, ones, threes)
        got = after((shift_y(ones, 1), shift_y(threes, -1)), *pieces)
        own, to_3, to_1, to_2 = fold(zeros, *got)
        three, two, one = swap(to_3, "dp", 12), swap(to_2, "dp", 8), swap(to_1, "dp", 4)
        pieces += [own, one, two, three]
    grad_one, grad_two = finish(pieces, w_head.shape[2] // 16)
    return grad_one, grad_two.transpose(1, 0, 2)


def solution(mesh):
    placed = (
        P("dp", None),
        P("dp"),
        P("dp"),
        P("pop", None, None),
        P("pop", None, None),
        P("pop", "dp"),
    )
    return jax.shard_map(
        body,
        mesh=mesh,
        in_specs=placed,
        out_specs=(P("pop", "dp", None), P("pop", None, "dp")),
        check_vma=False,
    )
```

```python
import functools
import math

import jax
import jax.numpy as jnp
from jax import lax
from jax.experimental import pallas as pl
from jax.experimental.pallas import tpu as pltpu
from jax.sharding import PartitionSpec as P

HID = 1024
ACTIONS = 18
PAD = 32
CHUNKS = (80, 48)
EXTRA = 8
SHARES = (0, 2, 4, 6, 1, 3, 5, 7)
STEPS = [(y, z) for y in (2, 1, 3, 0) for z in (0, 3, 1, 2)]
F32 = jnp.float32
BF16 = jnp.bfloat16
NT = (((1,), (1,)), ((), ()))
TN = (((0,), (0,)), ((), ()))
VMEM_SPEC = pl.BlockSpec(memory_space=pltpu.VMEM)
HBM_SPEC = pl.BlockSpec(memory_space=pltpu.HBM)


def params(mib):
    return pltpu.CompilerParams(vmem_limit_bytes=mib * 1024 * 1024)


def cost(us):
    return pl.CostEstimate(flops=int(us * 1.1e9), bytes_accessed=0, transcendentals=0)


def after(value, *first):
    return lax.optimization_barrier((value, first))[0]


def spot():
    place = lax.axis_index("dp")
    return place // 4, place % 4, lax.axis_index("pop") % len(SHARES)


def block_of(z, y, i):
    step_y, step_z = STEPS[i]
    return (z ^ step_z) * 4 + (y + step_y) % 4


def turn(rows_ref, turned_ref, z, y, blocks):
    width = turned_ref.shape[1]
    for i in blocks:
        start = pl.multiple_of(block_of(z, y, i) * width, width)
        turned_ref[i] = rows_ref[:, pl.ds(start, width)].T


def padded(head_ref, wide_ref):
    wide_ref[...] = jnp.zeros_like(wide_ref)
    wide_ref[0:ACTIONS, :] = head_ref[0].astype(F32)


def split3(v):
    hi = v.astype(BF16)
    rest = v - hi.astype(F32)
    mid = rest.astype(BF16)
    low = (rest - mid.astype(F32)).astype(BF16)
    return jnp.concatenate([hi, mid, low], axis=0)


def join3(v):
    return v[:PAD] + v[PAD : 2 * PAD] + v[2 * PAD :]


def row_onehot(start, size, row):
    ids = lax.broadcasted_iota(jnp.int32, (size, row.shape[1]), 0) + start
    return jnp.where(ids == row, 1.0, 0.0).astype(BF16)


def sigmoid(v):
    return 0.5 * jnp.tanh(0.5 * v) + 0.5


def forward_kernel(
    pool_hbm, w_hbm, head_ref, row_ref, act_ref, target_ref, hid_ref, slope_ref, turned_ref, emb_ref, facts_ref,
    acc_ref, pool_ref, w_ref, wide_ref, sems,
):
    z, y, _ = spot()
    rows, hidden = hid_ref.shape
    tile, width = rows // 2, hidden // 2
    row_of = lambda i: pl.ds(i * tile, tile)
    pools = [pltpu.make_async_copy(pool_hbm.at[row_of(i), :], pool_ref.at[row_of(i), :], sems.at[i]) for i in range(2)]
    halves = [
        pltpu.make_async_copy(w_hbm.at[0, :, pl.ds(j * width, width)], w_ref.at[j], sems.at[2 + j]) for j in range(2)
    ]
    for copy in (pools[0], halves[0], halves[1], pools[1]):
        copy.start()
    padded(head_ref, wide_ref)
    facts_ref[0:1, :] = target_ref[...]
    facts_ref[1:2, :] = row_ref[...].astype(F32)
    facts_ref[2:3, :] = act_ref[...].astype(F32)
    facts_ref[3:, :] = jnp.zeros((facts_ref.shape[0] - 3, facts_ref.shape[1]), F32)
    pools[0].wait()
    for i in range(2):
        if i == 1:
            pools[1].wait()
        for j in range(2):
            if i == 0:
                halves[j].wait()
            columns = slice(j * width, (j + 1) * width)
            v = jnp.dot(pool_ref[row_of(i), :], w_ref[j], preferred_element_type=F32)
            sig = sigmoid(v)
            hid = (v * sig).astype(BF16)
            hid_ref[row_of(i), columns] = hid

            @pl.when(z // 2 == j)
            def _():
                slope_ref[row_of(i), :] = sig * (1.0 + v * (1.0 - sig))

            logits = lax.dot_general(wide_ref[:, columns].astype(BF16), hid, NT, preferred_element_type=F32)
            if j == 0:
                acc_ref[:, row_of(i)] = logits
            else:
                acc_ref[:, row_of(i)] += logits
                if i == 1:
                    turn(pool_ref, turned_ref, z, y, range(turned_ref.shape[0]))
    logits = acc_ref[...]
    parts = split3(logits - jnp.sum(logits, axis=0, keepdims=True) / ACTIONS)
    picked = jnp.zeros((3 * PAD, row_ref.shape[1]), F32)
    for i in range(0, rows, 256):
        picked += jnp.dot(parts[:, i : i + 256], row_onehot(i, 256, row_ref[...]), preferred_element_type=F32)
    chosen = lax.broadcasted_iota(jnp.int32, (PAD, row_ref.shape[1]), 0) == act_ref[...]
    emb_ref[...] = jnp.sum(jnp.where(chosen, join3(picked), 0.0), axis=0, keepdims=True)


def forward(pool, w, head, row, act, target):
    rows, feat = pool.shape
    hid = w.shape[2]
    probes = row.shape[1]
    blocks = len(STEPS)
    return pl.pallas_call(
        forward_kernel,
        in_specs=[HBM_SPEC] * 2 + [VMEM_SPEC] * 4,
        out_specs=[VMEM_SPEC] * 5,
        out_shape=[
            jax.ShapeDtypeStruct((rows, hid), BF16),
            jax.ShapeDtypeStruct((rows, hid // 2), F32),
            jax.ShapeDtypeStruct((blocks, feat // blocks, rows), BF16),
            jax.ShapeDtypeStruct((1, probes), F32),
            jax.ShapeDtypeStruct((8, probes), F32),
        ],
        scratch_shapes=[
            pltpu.VMEM((PAD, rows), F32),
            pltpu.VMEM((rows, feat), BF16),
            pltpu.VMEM((2, feat, hid // 2), BF16),
            pltpu.VMEM((PAD, hid), F32),
            pltpu.SemaphoreType.DMA((4,)),
        ],
        compiler_params=params(42),
        cost_estimate=cost(0.3),
        name="forward",
    )(pool, w, head, row, act, target)


def distance_kernel(near_ref, far_ref, facts_ref, out_ref, pack_ref):
    pop = jnp.concatenate([near_ref[...], far_ref[...]], axis=0)
    agents = pop.shape[0]
    lanes = lax.broadcasted_iota(jnp.int32, (agents, 128), 1)
    total = jnp.zeros((agents, 128), F32)
    for i in range(agents):
        gap = pop - pop[i : i + 1, :]
        total = jnp.where(lanes == i, jnp.sum(gap * gap, axis=1, keepdims=True), total)
    out_ref[...] = total
    pack_ref[0:agents, :] = pop
    pack_ref[agents:, :] = facts_ref[...]


def distance_parts(near, far, facts):
    agents, probes = 2 * near.shape[0], near.shape[1]
    return pl.pallas_call(
        distance_kernel,
        in_specs=[VMEM_SPEC] * 3,
        out_specs=[VMEM_SPEC] * 2,
        out_shape=[
            jax.ShapeDtypeStruct((agents, 128), F32),
            jax.ShapeDtypeStruct((agents + facts.shape[0], probes), F32),
        ],
        compiler_params=params(16),
        cost_estimate=cost(0.2),
        name="distances",
    )(near, far, facts)


def partner_kernel(a_ref, b_ref, c_ref, d_ref, w_hbm, slope_ref, turned_ref, rows_ref, w_ref, sem):
    z, y, _ = spot()
    share, width = a_ref.shape[0], w_ref.shape[1]
    columns = pl.ds(pl.multiple_of(z // 2 * width, width), width)
    copy = pltpu.make_async_copy(w_hbm.at[0, :, columns], w_ref, sem)
    copy.start()
    for j, ref in enumerate((a_ref, b_ref, c_ref, d_ref)):
        rows_ref[pl.ds(j * share, share), :] = ref[...].astype(BF16)
    copy.wait()
    v = jnp.dot(rows_ref[...], w_ref[...], preferred_element_type=F32)
    sig = sigmoid(v)
    slope_ref[...] = sig * (1.0 + v * (1.0 - sig))
    turn(rows_ref, turned_ref, z, y, range(turned_ref.shape[0]))


def partner_part(shares, w):
    share, feat = shares[0].shape
    half = w.shape[2] // 2
    blocks = len(STEPS)
    return pl.pallas_call(
        partner_kernel,
        in_specs=[VMEM_SPEC] * 4 + [HBM_SPEC],
        out_specs=[VMEM_SPEC] * 2,
        out_shape=[
            jax.ShapeDtypeStruct((4 * share, half), F32),
            jax.ShapeDtypeStruct((blocks, feat // blocks, 4 * share), BF16),
        ],
        scratch_shapes=[
            pltpu.VMEM((4 * share, feat), BF16),
            pltpu.VMEM((feat, half), BF16),
            pltpu.SemaphoreType.DMA(()),
        ],
        compiler_params=params(16),
        cost_estimate=cost(0.3),
        name="partner",
    )(*shares, w)


def coeff_kernel(
    total_probes, scaling, d0, d1, near_ref, far_ref, facts_ref, pack_ref, head_ref,
    slope_a_ref, slope_b_ref, slope_ref, hid_ref, dz_ref, heads_ref, sums_ref, wide_ref, ghead_ref,
):
    z, y, share_place = spot()
    width = slope_ref.shape[1]
    columns = pl.ds(pl.multiple_of(z // 2 * width, width), width)
    padded(head_ref, wide_ref)
    pop = jnp.concatenate([near_ref[...], far_ref[...]], axis=0)
    agents = pop.shape[0]
    pop2 = pack_ref[0:agents, :]
    row, act = facts_ref[1:2, :].astype(jnp.int32), facts_ref[2:3, :].astype(jnp.int32)
    row2 = pack_ref[agents + 1 : agents + 2, :].astype(jnp.int32)
    act2 = pack_ref[agents + 2 : agents + 3, :].astype(jnp.int32)
    lanes = lax.broadcasted_iota(jnp.int32, (agents, 128), 1)
    subs = lax.broadcasted_iota(jnp.int32, (agents, 128), 0)
    kern = jnp.exp(-(d0[...] + d1[...]) / total_probes)
    system = jnp.where(lanes < agents, kern, jnp.where((lanes == agents) & (subs == 0), 1.0, 0.0))
    for k in range(agents):
        pivot_row = system[k : k + 1, :] / system[k : k + 1, k : k + 1]
        system = jnp.where(subs == k, pivot_row, system - system[:, k : k + 1] * pivot_row)
    mix = system[:, agents : agents + 1] * kern[:, 0:1]

    def marked(people, target, act):
        emb = people[0:1, :]
        pulled = jnp.sum(mix * people, axis=0, keepdims=True)
        diverse = 2.0 * (jnp.sum(mix, axis=0, keepdims=True) * emb - pulled)
        coeff = scaling * (emb - target) + scaling * diverse
        chosen = lax.broadcasted_iota(jnp.int32, (PAD, act.shape[1]), 0) == act
        return split3(jnp.where(chosen, coeff, 0.0))

    head = wide_ref[:, columns]
    centered = head - jnp.sum(head, axis=0, keepdims=True) / ACTIONS
    cent_hi = centered.astype(BF16)
    cent_lo = (centered - cent_hi.astype(F32)).astype(BF16)
    cents = jnp.concatenate([cent_hi, cent_lo, cent_hi], axis=0)

    def scaled(sums, slope):
        part_hi = sums.astype(BF16)
        part_lo = (sums - part_hi.astype(F32)).astype(BF16)
        stacked = jnp.concatenate([part_hi, part_hi, part_lo], axis=0)
        pulls = lax.dot_general(stacked, cents, TN, preferred_element_type=F32)
        return (pulls * slope).astype(BF16)

    rows = slope_ref.shape[0]
    tile = 256
    mine = marked(pop, facts_ref[0:1, :], act)
    theirs = marked(pop2, pack_ref[agents : agents + 1, :], act2)
    for i in range(rows // tile):
        here = pl.ds(i * tile, tile)
        hot = row_onehot(i * tile, tile, row)
        sums_ref[:, here] = join3(lax.dot_general(mine, hot, NT, preferred_element_type=F32))
    share = rows // len(SHARES)
    per = slope_a_ref.shape[0] // tile
    for i in range(rows // tile):
        hot = jnp.concatenate(
            [
                row_onehot((share_place ^ SHARES[j]) * share, share, row2)
                for j in range(i * tile // share, (i + 1) * tile // share)
            ],
            axis=0,
        )
        sums = join3(lax.dot_general(theirs, hot, NT, preferred_element_type=F32))
        slope2_ref = slope_a_ref if i < per else slope_b_ref
        dz_ref[pl.ds(rows + i * tile, tile), :] = scaled(sums, slope2_ref[pl.ds(i % per * tile, tile), :])
    for i in range(rows // tile):
        here = pl.ds(i * tile, tile)
        dz_ref[here, :] = scaled(sums_ref[:, here], slope_ref[here, :])


    sums = sums_ref[...]
    even = split3(sums - jnp.sum(sums, axis=0, keepdims=True) / ACTIONS)
    ghead_ref[...] = join3(jnp.dot(even, hid_ref[...], preferred_element_type=F32))
    blocks = heads_ref.shape[0]
    cols = ghead_ref.shape[1] // blocks
    for i in range(blocks):
        place = block_of(z, y, i)
        pair = ghead_ref[:, pl.ds(pl.multiple_of(place // 2 * 2 * cols, 2 * cols), 2 * cols)]
        mine = jnp.where(place % 2 == 0, pair[:, :cols], pair[:, cols:])
        laid = [mine[g * EXTRA : (g + 1) * EXTRA] for g in range(3)]
        rest = jnp.zeros((EXTRA, heads_ref.shape[2] - 3 * cols), F32)
        heads_ref[i] = jnp.concatenate(laid + [rest], axis=1)


def coefficients(total_probes, dists, near, far, facts, pack, head, slopes, slope, hid):
    rows, width = hid.shape
    scaling = math.sqrt(HID / total_probes)
    return pl.pallas_call(
        functools.partial(coeff_kernel, total_probes, scaling),
        in_specs=[VMEM_SPEC] * 11,
        out_specs=[VMEM_SPEC] * 2,
        out_shape=[
            jax.ShapeDtypeStruct((2 * rows, width // 2), BF16),
            jax.ShapeDtypeStruct((len(STEPS), EXTRA, width // 2), F32),
        ],
        scratch_shapes=[
            pltpu.VMEM((PAD, rows), F32),
            pltpu.VMEM((PAD, width), F32),
            pltpu.VMEM((PAD, width), F32),
        ],
        compiler_params=params(16),
        cost_estimate=cost(0.3),
        name="coefficients",
    )(*dists, near, far, facts, pack, head, *slopes, slope, hid)


def grad_kernel(plan, *refs):
    own_ref, a_ref, b_ref, dz_ref, heads_ref = refs[:5]
    mine, part = own_ref.shape[2], a_ref.shape[2]
    width = dz_ref.shape[1]
    for blocks, begin, end, outs, more in plan:
        rows = end - begin
        total = jnp.zeros((2 * rows, width), F32)
        for ref, start, depth in ((own_ref, 0, mine), (a_ref, mine, part), (b_ref, mine + part, part)):
            left = jnp.concatenate([ref[i, begin:end, :] for i in blocks], axis=0)
            total += jnp.dot(left, dz_ref[start : start + depth, :], preferred_element_type=F32)
        for q, block in enumerate(blocks):
            for out, at, size, extra in outs:
                out_ref, slot = refs[out[q][0]], out[q][1]
                value = total[q * rows + at : q * rows + at + size]
                heads = heads_ref[block] if extra else None
                if more is not None:
                    add_ref, add_slot = refs[more[q][0]], more[q][1]
                    value = value + add_ref[add_slot, 0:size, :]
                    heads = heads + add_ref[add_slot, size:, :] if extra else None
                out_ref[slot, 0:size, :] = value
                if extra:
                    out_ref[slot, size:, :] = heads


def gradient(parts, groups, which, more=None):
    dz = parts[3]
    width = dz.shape[1]
    chunks = [(sum(CHUNKS[:c]), CHUNKS[c], c == len(CHUNKS) - 1) for c in which]
    begin, end = chunks[0][0], chunks[-1][0] + chunks[-1][1]
    shapes = [
        jax.ShapeDtypeStruct((len(group), size + (EXTRA if extra else 0), width), F32)
        for group in groups
        for _, size, extra in chunks
    ]
    extras = [] if more is None else [more]
    first = len(parts) + len(extras)
    places = [(block, g, slot) for g, group in enumerate(groups) for slot, block in enumerate(group)]
    plan = []
    for k in range(0, len(places), 2):
        pair = places[k : k + 2]
        outs = [
            ([(first + g * len(chunks) + c, slot) for _, g, slot in pair], at - begin, size, extra)
            for c, (at, size, extra) in enumerate(chunks)
        ]
        added = None if more is None else [(len(parts), k), (len(parts), k + 1)]
        plan.append(([block for block, _, _ in pair], begin, end, outs, added))
    outs = pl.pallas_call(
        functools.partial(grad_kernel, plan),
        in_specs=[VMEM_SPEC] * first,
        out_specs=[VMEM_SPEC] * len(shapes),
        out_shape=shapes,
        compiler_params=params(16),
        cost_estimate=cost(0.3),
        name="gradient",
    )(*parts, *extras)
    return [outs[i : i + len(chunks)] for i in range(0, len(outs), len(chunks))]


def add_kernel(at, into_ref, more_ref, out_ref):
    here = slice(at, at + more_ref.shape[0])
    out_ref[here] = into_ref[here] + more_ref[...]


def add_into(into, more, at):
    return pl.pallas_call(
        functools.partial(add_kernel, at),
        in_specs=[VMEM_SPEC] * 2,
        out_specs=VMEM_SPEC,
        out_shape=jax.ShapeDtypeStruct(into.shape, F32),
        input_output_aliases={0: 0},
        compiler_params=params(16),
        cost_estimate=cost(0.1),
        name="add_into",
    )(into, more)


def fold_kernel(a_ref, b_ref, c_ref, *out_refs):
    for i, out_ref in enumerate(out_refs):
        out_ref[...] = a_ref[i] + (b_ref[i] + c_ref[i])


def fold(a, b, c):
    blocks = a.shape[0]
    return pl.pallas_call(
        fold_kernel,
        in_specs=[VMEM_SPEC] * 3,
        out_specs=[VMEM_SPEC] * blocks,
        out_shape=[jax.ShapeDtypeStruct(a.shape[1:], F32)] * blocks,
        compiler_params=params(16),
        cost_estimate=cost(0.1),
        name="fold",
    )(a, b, c)


def finish_kernel(*refs):
    out_ref, two_ref = refs[-2:]
    z, _, _ = spot()
    width = refs[0].shape[1]
    left = pl.ds(pl.multiple_of(z // 2 * width, width), width)
    right = pl.ds(pl.multiple_of((1 - z // 2) * width, width), width)
    at = 0
    for c, size in enumerate(CHUNKS[:-1]):
        own, one, two, three = refs[4 * c : 4 * c + 4]
        out_ref[0, at : at + size, left] = own[...] + one[...]
        out_ref[0, at : at + size, right] = two[...] + three[...]
        at += size
    own, other = refs[-4:-2]
    out_ref[0, at:, left] = own[0 : CHUNKS[-1], :]
    out_ref[0, at:, right] = other[0 : CHUNKS[-1], :]
    heads = own[CHUNKS[-1] :, :] + other[CHUNKS[-1] :, :]
    cols = two_ref.shape[2]
    for g in range(3):
        count = min(EXTRA, ACTIONS - g * EXTRA)
        two_ref[g * EXTRA : g * EXTRA + count] = heads[0:count, g * cols : (g + 1) * cols].reshape(count, 1, cols)


def finish(pieces, cols):
    rows, width = sum(CHUNKS), pieces[0].shape[1]
    return pl.pallas_call(
        finish_kernel,
        grid=(1,),
        in_specs=[VMEM_SPEC] * len(pieces),
        out_specs=[
            pl.BlockSpec((1, rows, 2 * width), lambda i: (0, 0, 0)),
            pl.BlockSpec((ACTIONS, 1, cols), lambda i: (0, 0, 0)),
        ],
        out_shape=[
            jax.ShapeDtypeStruct((1, rows, 2 * width), F32),
            jax.ShapeDtypeStruct((ACTIONS, 1, cols), F32),
        ],
        compiler_params=params(16),
        cost_estimate=cost(0.1),
        name="finish",
    )(*pieces)


def shift_y(v, s):
    return lax.ppermute(v, "dp", [(z * 4 + y, z * 4 + (y + s) % 4) for z in range(4) for y in range(4)])


def swap(v, axis, mask):
    return lax.ppermute(v, axis, [(i, i ^ mask) for i in range(16)])


def to_partner_rows(v):
    return lax.ppermute(
        v,
        ("pop", "dp"),
        [(p * 16 + d, (p ^ (8 if d // 4 in (0, 3) else 0)) * 16 + (d ^ 12)) for p in range(16) for d in range(16)],
    )


def body(state_pool, probe_row, action, w_hidden, w_head, targets):
    probes = probe_row.shape[0]
    total_probes = probes * lax.axis_size("dp")
    share = state_pool.shape[0] // len(SHARES)
    row = probe_row.reshape(1, probes)
    act = action.reshape(1, probes)

    _, _, where = spot()
    cut = lambda i: lax.dynamic_slice_in_dim(state_pool, i * share, share, 0).astype(F32)
    share0 = to_partner_rows(cut(where))
    next_share = cut(where ^ 4)

    hid, slope, turned, near, facts = forward(state_pool, w_hidden, w_head, row, act, targets)
    for mask in (1, 2, 4):
        near = jnp.concatenate([near, swap(near, "pop", mask)], axis=0)
    far = swap(near, "pop", 8)
    share4 = to_partner_rows(after(next_share, far))
    share0 = after(share0, far)
    share2, share6 = swap(share0, "pop", 2), swap(share0, "pop", 6)
    part, pack = distance_parts(near, far, facts)
    part = part + swap(part, "dp", 1)
    pack = after(pack, part)
    part = part + swap(part, "dp", 2)
    pack = swap(pack, "dp", 12)
    part = part + swap(part, "dp", 4)
    dists = [part, swap(part, "dp", 8)]

    shares = after([share0, share2, share4, share6], pack, *dists)
    slopes_a, turned_a = partner_part(shares, w_hidden)
    slopes_b, turned_b = partner_part([swap(v, "pop", 1) for v in shares], w_hidden)
    dz, heads = coefficients(
        total_probes, dists, near, far, facts, pack, w_head, [slopes_a, slopes_b], slope, hid
    )

    parts = [turned, turned_a, turned_b, dz, heads]
    early, last = range(len(CHUNKS) - 1), [len(CHUNKS) - 1]
    a2s, b2s = gradient(parts, [[0, 1], [2, 3]], early)
    from_a, from_b = [], []
    for i in early:
        from_a.append(shift_y(a2s[i], 1))
        from_b.append(shift_y(b2s[i], -1))
    parts[3] = after(dz, *a2s)
    away = [4 * g + k for g in range(4) for k in (2, 3)]
    ((sent,),) = gradient(parts, [away], last)
    met = swap(sent, "dp", 4)
    pieces = []
    waiting = []
    for i in early:
        (ones,), (threes,), (zeros,) = gradient(parts, [[4, 5, 6, 7], [8, 9, 10, 11], [12, 13, 14, 15]], [i])
        ones, threes = add_into(ones, from_a[i], 0), add_into(threes, from_b[i], 2)
        parts[3] = after(dz, ones, threes)
        waiting.append((zeros, shift_y(ones, 1), shift_y(threes, -1)))
    kept = [[0], [1], [4, 5], [8, 9], [12, 13]]
    (a2,), (b2,), (ones,), (threes,), (zeros,) = gradient(parts, kept, last, met)
    last_a, last_b = shift_y(a2, 1), shift_y(b2, -1)
    ones, threes = add_into(ones, last_a, 0), add_into(threes, last_b, 1)
    waiting.append((zeros, shift_y(ones, 1), shift_y(threes, -1)))
    for i in early:
        own, to_3, to_1, to_2 = fold(*after(waiting[i], *pieces))
        three, two, one = swap(to_3, "dp", 12), swap(to_2, "dp", 8), swap(to_1, "dp", 4)
        pieces += [own, one, two, three]
    own, to_3 = fold(*after(waiting[-1], *pieces[:-4]))
    pieces += [own, swap(to_3, "dp", 12)]
    grad_one, grad_two = finish(pieces, w_head.shape[2] // 16)
    return grad_one, grad_two.transpose(1, 0, 2)


def solution(mesh):
    placed = (
        P("dp", None),
        P("dp"),
        P("dp"),
        P("pop", None, None),
        P("pop", None, None),
        P("pop", "dp"),
    )
    return jax.shard_map(
        body,
        mesh=mesh,
        in_specs=placed,
        out_specs=(P("pop", "dp", None), P("pop", None, "dp")),
        check_vma=False,
    )
```

```python
import functools
import math

import jax
import jax.numpy as jnp
from jax import lax
from jax.experimental import pallas as pl
from jax.experimental.pallas import tpu as pltpu
from jax.sharding import PartitionSpec as P

HID = 1024
ACTIONS = 18
PAD = 32
CHUNKS = (48, 48, 32)
EXTRA = 8
SHARES = (0, 2, 4, 6, 1, 3, 5, 7)
STEPS = [(y, z) for y in (2, 1, 3, 0) for z in (0, 3, 1, 2)]
F32 = jnp.float32
BF16 = jnp.bfloat16
NT = (((1,), (1,)), ((), ()))
TN = (((0,), (0,)), ((), ()))
VMEM_SPEC = pl.BlockSpec(memory_space=pltpu.VMEM)
HBM_SPEC = pl.BlockSpec(memory_space=pltpu.HBM)


def params(mib):
    return pltpu.CompilerParams(vmem_limit_bytes=mib * 1024 * 1024)


def cost(us):
    return pl.CostEstimate(flops=int(us * 1.1e9), bytes_accessed=0, transcendentals=0)


def after(value, *first):
    return lax.optimization_barrier((value, first))[0]


def spot():
    place = lax.axis_index("dp")
    return place // 4, place % 4, lax.axis_index("pop") % len(SHARES)


def block_of(z, y, i):
    step_y, step_z = STEPS[i]
    return (z ^ step_z) * 4 + (y + step_y) % 4


def turn(rows_ref, turned_ref, z, y, blocks):
    width = turned_ref.shape[1]
    for i in blocks:
        start = pl.multiple_of(block_of(z, y, i) * width, width)
        turned_ref[i] = rows_ref[:, pl.ds(start, width)].T


def padded(head_ref, wide_ref):
    wide_ref[...] = jnp.zeros_like(wide_ref)
    wide_ref[0:ACTIONS, :] = head_ref[0].astype(F32)


def split3(v):
    hi = v.astype(BF16)
    rest = v - hi.astype(F32)
    mid = rest.astype(BF16)
    low = (rest - mid.astype(F32)).astype(BF16)
    return jnp.concatenate([hi, mid, low], axis=0)


def join3(v):
    return v[:PAD] + v[PAD : 2 * PAD] + v[2 * PAD :]


def row_onehot(start, size, row):
    ids = lax.broadcasted_iota(jnp.int32, (size, row.shape[1]), 0) + start
    return jnp.where(ids == row, 1.0, 0.0).astype(BF16)


def sigmoid(v):
    return 0.5 * jnp.tanh(0.5 * v) + 0.5


def forward_kernel(
    pool_hbm, w_hbm, head_ref, row_ref, act_ref, target_ref, hid_ref, slope_ref, turned_ref, emb_ref, facts_ref,
    acc_ref, pool_ref, w_ref, wide_ref, sems,
):
    z, y, _ = spot()
    rows, hidden = hid_ref.shape
    tile, width = rows // 2, hidden // 2
    row_of = lambda i: pl.ds(i * tile, tile)
    pools = [pltpu.make_async_copy(pool_hbm.at[row_of(i), :], pool_ref.at[row_of(i), :], sems.at[i]) for i in range(2)]
    halves = [
        pltpu.make_async_copy(w_hbm.at[0, :, pl.ds(j * width, width)], w_ref.at[j], sems.at[2 + j]) for j in range(2)
    ]
    for copy in (pools[0], halves[0], halves[1], pools[1]):
        copy.start()
    padded(head_ref, wide_ref)
    facts_ref[0:1, :] = target_ref[...]
    facts_ref[1:2, :] = row_ref[...].astype(F32)
    facts_ref[2:3, :] = act_ref[...].astype(F32)
    facts_ref[3:, :] = jnp.zeros((facts_ref.shape[0] - 3, facts_ref.shape[1]), F32)
    pools[0].wait()
    for i in range(2):
        if i == 1:
            pools[1].wait()
        for j in range(2):
            if i == 0:
                halves[j].wait()
            columns = slice(j * width, (j + 1) * width)
            v = jnp.dot(pool_ref[row_of(i), :], w_ref[j], preferred_element_type=F32)
            sig = sigmoid(v)
            hid = (v * sig).astype(BF16)
            hid_ref[row_of(i), columns] = hid

            @pl.when(z // 2 == j)
            def _():
                slope_ref[row_of(i), :] = sig * (1.0 + v * (1.0 - sig))

            logits = lax.dot_general(wide_ref[:, columns].astype(BF16), hid, NT, preferred_element_type=F32)
            if j == 0:
                acc_ref[:, row_of(i)] = logits
            else:
                acc_ref[:, row_of(i)] += logits
                if i == 1:
                    turn(pool_ref, turned_ref, z, y, range(turned_ref.shape[0]))
    logits = acc_ref[...]
    parts = split3(logits - jnp.sum(logits, axis=0, keepdims=True) / ACTIONS)
    picked = jnp.zeros((3 * PAD, row_ref.shape[1]), F32)
    for i in range(0, rows, 256):
        picked += jnp.dot(parts[:, i : i + 256], row_onehot(i, 256, row_ref[...]), preferred_element_type=F32)
    chosen = lax.broadcasted_iota(jnp.int32, (PAD, row_ref.shape[1]), 0) == act_ref[...]
    emb_ref[...] = jnp.sum(jnp.where(chosen, join3(picked), 0.0), axis=0, keepdims=True)


def forward(pool, w, head, row, act, target):
    rows, feat = pool.shape
    hid = w.shape[2]
    probes = row.shape[1]
    blocks = len(STEPS)
    return pl.pallas_call(
        forward_kernel,
        in_specs=[HBM_SPEC] * 2 + [VMEM_SPEC] * 4,
        out_specs=[VMEM_SPEC] * 5,
        out_shape=[
            jax.ShapeDtypeStruct((rows, hid), BF16),
            jax.ShapeDtypeStruct((rows, hid // 2), F32),
            jax.ShapeDtypeStruct((blocks, feat // blocks, rows), BF16),
            jax.ShapeDtypeStruct((1, probes), F32),
            jax.ShapeDtypeStruct((8, probes), F32),
        ],
        scratch_shapes=[
            pltpu.VMEM((PAD, rows), F32),
            pltpu.VMEM((rows, feat), BF16),
            pltpu.VMEM((2, feat, hid // 2), BF16),
            pltpu.VMEM((PAD, hid), F32),
            pltpu.SemaphoreType.DMA((4,)),
        ],
        compiler_params=params(42),
        cost_estimate=cost(0.3),
        name="forward",
    )(pool, w, head, row, act, target)


def distance_kernel(near_ref, far_ref, facts_ref, out_ref, pack_ref):
    pop = jnp.concatenate([near_ref[...], far_ref[...]], axis=0)
    agents = pop.shape[0]
    lanes = lax.broadcasted_iota(jnp.int32, (agents, 128), 1)
    total = jnp.zeros((agents, 128), F32)
    for i in range(agents):
        gap = pop - pop[i : i + 1, :]
        total = jnp.where(lanes == i, jnp.sum(gap * gap, axis=1, keepdims=True), total)
    out_ref[...] = total
    pack_ref[0:agents, :] = pop
    pack_ref[agents:, :] = facts_ref[...]


def distance_parts(near, far, facts):
    agents, probes = 2 * near.shape[0], near.shape[1]
    return pl.pallas_call(
        distance_kernel,
        in_specs=[VMEM_SPEC] * 3,
        out_specs=[VMEM_SPEC] * 2,
        out_shape=[
            jax.ShapeDtypeStruct((agents, 128), F32),
            jax.ShapeDtypeStruct((agents + facts.shape[0], probes), F32),
        ],
        compiler_params=params(16),
        cost_estimate=cost(0.2),
        name="distances",
    )(near, far, facts)


def partner_rows(z, y, share_refs, w_hbm, turned_ref, rows_ref, w_ref, sem):
    share, width = share_refs[0].shape[0], w_ref.shape[1]
    columns = pl.ds(pl.multiple_of(z // 2 * width, width), width)
    copy = pltpu.make_async_copy(w_hbm.at[0, :, columns], w_ref, sem)
    copy.start()
    for j, ref in enumerate(share_refs):
        rows_ref[pl.ds(j * share, share), :] = ref[...].astype(BF16)
    copy.wait()
    v = jnp.dot(rows_ref[...], w_ref[...], preferred_element_type=F32)
    turn(rows_ref, turned_ref, z, y, range(turned_ref.shape[0]))
    sig = sigmoid(v)
    return sig * (1.0 + v * (1.0 - sig))


def marked_sums(marked, hot):
    return join3(lax.dot_general(marked, hot, NT, preferred_element_type=F32))


def scaled(sums, cents, slope):
    part_hi = sums.astype(BF16)
    part_lo = (sums - part_hi.astype(F32)).astype(BF16)
    stacked = jnp.concatenate([part_hi, part_hi, part_lo], axis=0)
    return (lax.dot_general(stacked, cents, TN, preferred_element_type=F32) * slope).astype(BF16)


def partner_hot(where, first, share, row):
    return jnp.concatenate([row_onehot((where ^ SHARES[j]) * share, share, row) for j in (first, first + 1)], axis=0)


def partner_a_kernel(a_ref, b_ref, c_ref, d_ref, w_hbm, slope_ref, turned_ref, rows_ref, w_ref, sem):
    z, y, _ = spot()
    slope_ref[...] = partner_rows(z, y, (a_ref, b_ref, c_ref, d_ref), w_hbm, turned_ref, rows_ref, w_ref, sem)


def partner_b_kernel(
    a_ref, b_ref, c_ref, d_ref, w_hbm, marked_ref, cents_ref, pack_ref, dz_ref, turned_ref, rows_ref, w_ref, sem
):
    z, y, where = spot()
    share = a_ref.shape[0]
    slope = partner_rows(z, y, (a_ref, b_ref, c_ref, d_ref), w_hbm, turned_ref, rows_ref, w_ref, sem)
    row = pack_ref[17:18, :].astype(jnp.int32)
    for i in range(2):
        here = slice(2 * i * share, 2 * (i + 1) * share)
        sums = marked_sums(marked_ref[...], partner_hot(where, 4 + 2 * i, share, row))
        dz_ref[here, :] = scaled(sums, cents_ref[...], slope[here])


def partner_part(shares, w, more=()):
    share, feat = shares[0].shape
    half = w.shape[2] // 2
    blocks = len(STEPS)
    return pl.pallas_call(
        partner_b_kernel if more else partner_a_kernel,
        in_specs=[VMEM_SPEC] * 4 + [HBM_SPEC] + [VMEM_SPEC] * len(more),
        out_specs=[VMEM_SPEC] * 2,
        out_shape=[
            jax.ShapeDtypeStruct((4 * share, half), BF16 if more else F32),
            jax.ShapeDtypeStruct((blocks, feat // blocks, 4 * share), BF16),
        ],
        scratch_shapes=[
            pltpu.VMEM((4 * share, feat), BF16),
            pltpu.VMEM((feat, half), BF16),
            pltpu.SemaphoreType.DMA(()),
        ],
        compiler_params=params(16),
        cost_estimate=cost(0.3),
        name="partner",
    )(*shares, w, *more)


def coeff_kernel(
    total_probes, scaling, d0, d1, near_ref, far_ref, facts_ref, pack_ref, head_ref, slope_a_ref, slope_ref, hid_ref,
    dz_ref, heads_ref, marked_ref, cents_ref, sums_ref, wide_ref, ghead_ref,
):
    z, y, where = spot()
    width = slope_ref.shape[1]
    columns = pl.ds(pl.multiple_of(z // 2 * width, width), width)
    padded(head_ref, wide_ref)
    pop = jnp.concatenate([near_ref[...], far_ref[...]], axis=0)
    agents = pop.shape[0]
    pop2 = pack_ref[0:agents, :]
    row, act = facts_ref[1:2, :].astype(jnp.int32), facts_ref[2:3, :].astype(jnp.int32)
    row2 = pack_ref[agents + 1 : agents + 2, :].astype(jnp.int32)
    act2 = pack_ref[agents + 2 : agents + 3, :].astype(jnp.int32)
    lanes = lax.broadcasted_iota(jnp.int32, (agents, 128), 1)
    subs = lax.broadcasted_iota(jnp.int32, (agents, 128), 0)
    kern = jnp.exp(-(d0[...] + d1[...]) / total_probes)
    system = jnp.where(lanes < agents, kern, jnp.where((lanes == agents) & (subs == 0), 1.0, 0.0))
    for k in range(agents):
        pivot_row = system[k : k + 1, :] / system[k : k + 1, k : k + 1]
        system = jnp.where(subs == k, pivot_row, system - system[:, k : k + 1] * pivot_row)
    mix = system[:, agents : agents + 1] * kern[:, 0:1]

    def marked(people, target, act):
        emb = people[0:1, :]
        pulled = jnp.sum(mix * people, axis=0, keepdims=True)
        diverse = 2.0 * (jnp.sum(mix, axis=0, keepdims=True) * emb - pulled)
        coeff = scaling * (emb - target) + scaling * diverse
        chosen = lax.broadcasted_iota(jnp.int32, (PAD, act.shape[1]), 0) == act
        return split3(jnp.where(chosen, coeff, 0.0))

    head = wide_ref[:, columns]
    centered = head - jnp.sum(head, axis=0, keepdims=True) / ACTIONS
    cent_hi = centered.astype(BF16)
    cent_lo = (centered - cent_hi.astype(F32)).astype(BF16)
    cents = jnp.concatenate([cent_hi, cent_lo, cent_hi], axis=0)

    rows = slope_ref.shape[0]
    tile = 256
    mine = marked(pop, facts_ref[0:1, :], act)
    theirs = marked(pop2, pack_ref[agents : agents + 1, :], act2)
    marked_ref[...] = theirs
    cents_ref[...] = cents
    for i in range(rows // tile):
        here = pl.ds(i * tile, tile)
        sums = marked_sums(mine, row_onehot(i * tile, tile, row))
        sums_ref[:, here] = sums
        dz_ref[here, :] = scaled(sums, cents, slope_ref[here, :])
    share = tile // 2
    for i in range(slope_a_ref.shape[0] // tile):
        sums = marked_sums(theirs, partner_hot(where, 2 * i, share, row2))
        dz_ref[pl.ds(rows + i * tile, tile), :] = scaled(sums, cents, slope_a_ref[pl.ds(i * tile, tile), :])
    sums = sums_ref[...]
    even = split3(sums - jnp.sum(sums, axis=0, keepdims=True) / ACTIONS)
    ghead_ref[...] = join3(jnp.dot(even, hid_ref[...], preferred_element_type=F32))
    blocks = heads_ref.shape[0]
    cols = ghead_ref.shape[1] // blocks
    for i in range(blocks):
        place = block_of(z, y, i)
        pair = ghead_ref[:, pl.ds(pl.multiple_of(place // 2 * 2 * cols, 2 * cols), 2 * cols)]
        mine = jnp.where(place % 2 == 0, pair[:, :cols], pair[:, cols:])
        laid = [mine[g * EXTRA : (g + 1) * EXTRA] for g in range(3)]
        rest = jnp.zeros((EXTRA, heads_ref.shape[2] - 3 * cols), F32)
        heads_ref[i] = jnp.concatenate(laid + [rest], axis=1)


def coefficients(total_probes, dists, near, far, facts, pack, head, slope_a, slope, hid):
    rows, width = hid.shape
    half = width // 2
    scaling = math.sqrt(HID / total_probes)
    return pl.pallas_call(
        functools.partial(coeff_kernel, total_probes, scaling),
        in_specs=[VMEM_SPEC] * 10,
        out_specs=[VMEM_SPEC] * 4,
        out_shape=[
            jax.ShapeDtypeStruct((rows + slope_a.shape[0], half), BF16),
            jax.ShapeDtypeStruct((len(STEPS), EXTRA, half), F32),
            jax.ShapeDtypeStruct((3 * PAD, rows), BF16),
            jax.ShapeDtypeStruct((3 * PAD, half), BF16),
        ],
        scratch_shapes=[
            pltpu.VMEM((PAD, rows), F32),
            pltpu.VMEM((PAD, width), F32),
            pltpu.VMEM((PAD, width), F32),
        ],
        compiler_params=params(16),
        cost_estimate=cost(0.3),
        name="coefficients",
    )(*dists, near, far, facts, pack, head, slope_a, slope, hid)


def grad_kernel(plan, *refs):
    own_ref, a_ref, b_ref, dz_ref, dz_b_ref, heads_ref = refs[:6]
    mine, part = own_ref.shape[2], a_ref.shape[2]
    width = dz_ref.shape[1]
    products = ((own_ref, dz_ref, 0, mine), (a_ref, dz_ref, mine, part), (b_ref, dz_b_ref, 0, part))
    for blocks, begin, end, outs, more in plan:
        rows = end - begin
        total = jnp.zeros((2 * rows, width), F32)
        for ref, right_ref, start, depth in products:
            left = jnp.concatenate([ref[i, begin:end, :] for i in blocks], axis=0)
            total += jnp.dot(left, right_ref[start : start + depth, :], preferred_element_type=F32)
        for q, block in enumerate(blocks):
            for out, at, size, extra in outs:
                out_ref, slot = refs[out[q][0]], out[q][1]
                value = total[q * rows + at : q * rows + at + size]
                heads = heads_ref[block] if extra else None
                if more is not None:
                    add_ref, add_slot = refs[more[q][0]], more[q][1]
                    value = value + add_ref[add_slot, 0:size, :]
                    heads = heads + add_ref[add_slot, size:, :] if extra else None
                out_ref[slot, 0:size, :] = value
                if extra:
                    out_ref[slot, size:, :] = heads


def gradient(parts, groups, which, more=None):
    dz = parts[3]
    width = dz.shape[1]
    chunks = [(sum(CHUNKS[:c]), CHUNKS[c], c == len(CHUNKS) - 1) for c in which]
    begin, end = chunks[0][0], chunks[-1][0] + chunks[-1][1]
    shapes = [
        jax.ShapeDtypeStruct((len(group), size + (EXTRA if extra else 0), width), F32)
        for group in groups
        for _, size, extra in chunks
    ]
    extras = [] if more is None else [more]
    first = len(parts) + len(extras)
    places = [(block, g, slot) for g, group in enumerate(groups) for slot, block in enumerate(group)]
    plan = []
    for k in range(0, len(places), 2):
        pair = places[k : k + 2]
        outs = [
            ([(first + g * len(chunks) + c, slot) for _, g, slot in pair], at - begin, size, extra)
            for c, (at, size, extra) in enumerate(chunks)
        ]
        added = None if more is None else [(len(parts), k), (len(parts), k + 1)]
        plan.append(([block for block, _, _ in pair], begin, end, outs, added))
    outs = pl.pallas_call(
        functools.partial(grad_kernel, plan),
        in_specs=[VMEM_SPEC] * first,
        out_specs=[VMEM_SPEC] * len(shapes),
        out_shape=shapes,
        compiler_params=params(16),
        cost_estimate=cost(0.3),
        name="gradient",
    )(*parts, *extras)
    return [outs[i : i + len(chunks)] for i in range(0, len(outs), len(chunks))]


def add_kernel(at, into_ref, more_ref, out_ref):
    here = slice(at, at + more_ref.shape[0])
    out_ref[here] = into_ref[here] + more_ref[...]


def add_into(into, more, at):
    return pl.pallas_call(
        functools.partial(add_kernel, at),
        in_specs=[VMEM_SPEC] * 2,
        out_specs=VMEM_SPEC,
        out_shape=jax.ShapeDtypeStruct(into.shape, F32),
        input_output_aliases={0: 0},
        compiler_params=params(16),
        cost_estimate=cost(0.1),
        name="add_into",
    )(into, more)


def fold_kernel(count, *refs):
    at = 0
    for out_ref in refs[count:]:
        size = out_ref.shape[0]
        out_ref[...] = sum((ref[at : at + size] for ref in refs[1:count]), refs[0][at : at + size])
        at += size


def fold(terms, per):
    blocks = terms[0].shape[0] // per
    return pl.pallas_call(
        functools.partial(fold_kernel, len(terms)),
        in_specs=[VMEM_SPEC] * len(terms),
        out_specs=[VMEM_SPEC] * blocks,
        out_shape=[jax.ShapeDtypeStruct((per, *terms[0].shape[1:]), F32)] * blocks,
        compiler_params=params(16),
        cost_estimate=cost(0.1),
        name="fold",
    )(*terms)


def finish_kernel(*refs):
    out_ref, two_ref = refs[-2:]
    z, _, _ = spot()
    width = refs[0].shape[2]
    left = pl.ds(pl.multiple_of(z // 2 * width, width), width)
    right = pl.ds(pl.multiple_of((1 - z // 2) * width, width), width)
    at = 0
    for c, size in enumerate(CHUNKS):
        own, other = refs[2 * c : 2 * c + 2]
        out_ref[0, at : at + size, left] = own[0, 0:size, :]
        out_ref[0, at : at + size, right] = other[0, 0:size, :]
        at += size
    heads = own[0, CHUNKS[-1] :, :] + other[0, CHUNKS[-1] :, :]
    cols = two_ref.shape[2]
    for g in range(3):
        count = min(EXTRA, ACTIONS - g * EXTRA)
        two_ref[g * EXTRA : g * EXTRA + count] = heads[0:count, g * cols : (g + 1) * cols].reshape(count, 1, cols)


def finish(pieces, cols):
    rows, width = sum(CHUNKS), pieces[0].shape[2]
    return pl.pallas_call(
        finish_kernel,
        grid=(1,),
        in_specs=[VMEM_SPEC] * len(pieces),
        out_specs=[
            pl.BlockSpec((1, rows, 2 * width), lambda i: (0, 0, 0)),
            pl.BlockSpec((ACTIONS, 1, cols), lambda i: (0, 0, 0)),
        ],
        out_shape=[
            jax.ShapeDtypeStruct((1, rows, 2 * width), F32),
            jax.ShapeDtypeStruct((ACTIONS, 1, cols), F32),
        ],
        compiler_params=params(16),
        cost_estimate=cost(0.1),
        name="finish",
    )(*pieces)


def shift_y(v, s):
    return lax.ppermute(v, "dp", [(z * 4 + y, z * 4 + (y + s) % 4) for z in range(4) for y in range(4)])


def swap(v, axis, mask):
    return lax.ppermute(v, axis, [(i, i ^ mask) for i in range(16)])


def to_partner_rows(v):
    return lax.ppermute(
        v,
        ("pop", "dp"),
        [(p * 16 + d, (p ^ (8 if d // 4 in (0, 3) else 0)) * 16 + (d ^ 12)) for p in range(16) for d in range(16)],
    )


def body(state_pool, probe_row, action, w_hidden, w_head, targets):
    probes = probe_row.shape[0]
    total_probes = probes * lax.axis_size("dp")
    share = state_pool.shape[0] // len(SHARES)
    row = probe_row.reshape(1, probes)
    act = action.reshape(1, probes)

    _, _, where = spot()
    cut = lambda i: lax.dynamic_slice_in_dim(state_pool, i * share, share, 0).astype(F32)
    share0 = to_partner_rows(cut(where))
    next_share = cut(where ^ 4)

    hid, slope, turned, near, facts = forward(state_pool, w_hidden, w_head, row, act, targets)
    for mask in (1, 2, 4):
        near = jnp.concatenate([near, swap(near, "pop", mask)], axis=0)
    far = swap(near, "pop", 8)
    share4 = to_partner_rows(after(next_share, far))
    share0 = after(share0, far)
    share2, share6 = swap(share0, "pop", 2), swap(share0, "pop", 6)
    part, pack = distance_parts(near, far, facts)
    part = part + swap(part, "dp", 1)
    pack = after(pack, part)
    part = part + swap(part, "dp", 2)
    pack = swap(pack, "dp", 12)
    part = part + swap(part, "dp", 4)
    dists = [part, swap(part, "dp", 8)]

    swapped0 = swap(after(share0, pack), "pop", 1)
    share0, share2, share4, share6 = after([share0, share2, share4, share6], pack, *dists)
    swapped = [swapped0] + [swap(v, "pop", 1) for v in (share2, share4, share6)]
    slope_a, turned_a = partner_part([share0, share2, share4, share6], w_hidden)
    dz, heads, marks, cents = coefficients(
        total_probes, dists, near, far, facts, pack, w_head, slope_a, slope, hid
    )
    dz_b, turned_b = partner_part(swapped, w_hidden, (marks, cents, pack))

    parts = [turned, turned_a, turned_b, dz, dz_b, heads]
    tie = lambda *first: parts[:3] + [after(dz, *first)] + parts[4:]
    early, last = range(len(CHUNKS) - 1), [len(CHUNKS) - 1]
    a2s, b2s = gradient(parts, [[0, 1], [2, 3]], early)
    from_a, from_b = [], []
    for i in early:
        from_a.append(shift_y(a2s[i], 1))
        from_b.append(shift_y(b2s[i], -1))
    away = [4 * g + k for g in range(4) for k in (2, 3)]
    waiting = []
    tied = tie(*a2s)
    for i in early:
        (ones,), (threes,), (zeros,) = gradient(tied, [[4, 5, 6, 7], [8, 9, 10, 11], [12, 13, 14, 15]], [i])
        if i == 0:
            ((sent,),) = gradient(tie(*a2s), [away], last)
            met = swap(sent, "dp", 4)
        ones, threes = add_into(ones, from_a[i], 0), add_into(threes, from_b[i], 2)
        waiting.append((zeros, shift_y(ones, 1), shift_y(threes, -1)))
        tied = tie(ones, threes)
    (a2,), (b2,), (ones,), (threes,), (zeros,) = gradient(tied, [[0], [1], [4, 5], [8, 9], [12, 13]], last, met)
    last_a, last_b = shift_y(a2, 1), shift_y(b2, -1)
    near_0, away_0 = fold(waiting[0], 2)
    met_0 = swap(away_0, "dp", 4)
    own_0, to_0 = fold((near_0, met_0), 1)
    other_0 = swap(to_0, "dp", 12)
    near_1, away_1 = fold(waiting[1], 2)
    met_1 = swap(away_1, "dp", 4)
    last_a, last_b = (last_a, last_b)
    ones, threes = add_into(ones, last_a, 0), add_into(threes, last_b, 1)
    own_2, to_2 = fold((zeros, shift_y(ones, 1), shift_y(threes, -1)), 1)
    other_2 = swap(to_2, "dp", 12)
    own_1, to_1 = fold((near_1, after(met_1, to_2)), 1)
    other_1 = swap(to_1, "dp", 12)
    pieces = [own_0, other_0, own_1, other_1, own_2, other_2]
    grad_one, grad_two = finish(pieces, w_head.shape[2] // 16)
    return grad_one, grad_two.transpose(1, 0, 2)


def solution(mesh):
    placed = (
        P("dp", None),
        P("dp"),
        P("dp"),
        P("pop", None, None),
        P("pop", None, None),
        P("pop", "dp"),
    )
    return jax.shard_map(
        body,
        mesh=mesh,
        in_specs=placed,
        out_specs=(P("pop", "dp", None), P("pop", None, "dp")),
        check_vma=False,
    )
```

```python
import functools
import math

import jax
import jax.numpy as jnp
from jax import lax
from jax.experimental import pallas as pl
from jax.experimental.pallas import tpu as pltpu
from jax.sharding import PartitionSpec as P

HID = 1024
ACTIONS = 18
PAD = 32
CHUNKS = (48, 48, 32)
EXTRA = 8
SHARES = (0, 2, 4, 6, 1, 3, 5, 7)
STEPS = [(y, z) for y in (2, 1, 3, 0) for z in (0, 3, 1, 2)]
F32 = jnp.float32
BF16 = jnp.bfloat16
NT = (((1,), (1,)), ((), ()))
TN = (((0,), (0,)), ((), ()))
VMEM_SPEC = pl.BlockSpec(memory_space=pltpu.VMEM)
HBM_SPEC = pl.BlockSpec(memory_space=pltpu.HBM)


def params(mib):
    return pltpu.CompilerParams(vmem_limit_bytes=mib * 1024 * 1024)


def cost(us):
    return pl.CostEstimate(flops=int(us * 1.1e9), bytes_accessed=0, transcendentals=0)


def after(value, *first):
    return lax.optimization_barrier((value, first))[0]


def spot():
    place = lax.axis_index("dp")
    return place // 4, place % 4, lax.axis_index("pop") % len(SHARES)


def block_of(z, y, i):
    step_y, step_z = STEPS[i]
    return (z ^ step_z) * 4 + (y + step_y) % 4


def turn(rows_ref, turned_ref, z, y, blocks):
    width = turned_ref.shape[1]
    for i in blocks:
        start = pl.multiple_of(block_of(z, y, i) * width, width)
        turned_ref[i] = rows_ref[:, pl.ds(start, width)].T


def padded(head_ref, wide_ref):
    wide_ref[...] = jnp.zeros_like(wide_ref)
    wide_ref[0:ACTIONS, :] = head_ref[0].astype(F32)


def split3(v):
    hi = v.astype(BF16)
    rest = v - hi.astype(F32)
    mid = rest.astype(BF16)
    low = (rest - mid.astype(F32)).astype(BF16)
    return jnp.concatenate([hi, mid, low], axis=0)


def join3(v):
    return v[:PAD] + v[PAD : 2 * PAD] + v[2 * PAD :]


def row_onehot(start, size, row):
    ids = lax.broadcasted_iota(jnp.int32, (size, row.shape[1]), 0) + start
    return jnp.where(ids == row, 1.0, 0.0).astype(BF16)


def sigmoid(v):
    return 0.5 * jnp.tanh(0.5 * v) + 0.5


def forward_kernel(
    pool_hbm, w_hbm, head_ref, row_ref, act_ref, target_ref, hid_ref, slope_ref, emb_ref, facts_ref,
    acc_ref, pool_ref, w_ref, wide_ref, sems,
):
    z, _, _ = spot()
    rows, hidden = hid_ref.shape
    tile, width = rows // 2, hidden // 2
    row_of = lambda i: pl.ds(i * tile, tile)
    pools = [pltpu.make_async_copy(pool_hbm.at[row_of(i), :], pool_ref.at[row_of(i), :], sems.at[i]) for i in range(2)]
    halves = [
        pltpu.make_async_copy(w_hbm.at[0, :, pl.ds(j * width, width)], w_ref.at[j], sems.at[2 + j]) for j in range(2)
    ]
    for copy in (pools[0], halves[0], halves[1], pools[1]):
        copy.start()
    padded(head_ref, wide_ref)
    facts_ref[0:1, :] = target_ref[...]
    facts_ref[1:2, :] = row_ref[...].astype(F32)
    facts_ref[2:3, :] = act_ref[...].astype(F32)
    facts_ref[3:, :] = jnp.zeros((facts_ref.shape[0] - 3, facts_ref.shape[1]), F32)
    pools[0].wait()
    for i in range(2):
        if i == 1:
            pools[1].wait()
        for j in range(2):
            if i == 0:
                halves[j].wait()
            columns = slice(j * width, (j + 1) * width)
            v = jnp.dot(pool_ref[row_of(i), :], w_ref[j], preferred_element_type=F32)
            sig = sigmoid(v)
            hid = (v * sig).astype(BF16)
            hid_ref[row_of(i), columns] = hid

            @pl.when(z // 2 == j)
            def _():
                slope_ref[row_of(i), :] = sig * (1.0 + v * (1.0 - sig))

            logits = lax.dot_general(wide_ref[:, columns].astype(BF16), hid, NT, preferred_element_type=F32)
            if j == 0:
                acc_ref[:, row_of(i)] = logits
            else:
                acc_ref[:, row_of(i)] += logits
    logits = acc_ref[...]
    parts = split3(logits - jnp.sum(logits, axis=0, keepdims=True) / ACTIONS)
    picked = jnp.zeros((3 * PAD, row_ref.shape[1]), F32)
    for i in range(0, rows, 256):
        picked += jnp.dot(parts[:, i : i + 256], row_onehot(i, 256, row_ref[...]), preferred_element_type=F32)
    chosen = lax.broadcasted_iota(jnp.int32, (PAD, row_ref.shape[1]), 0) == act_ref[...]
    emb_ref[...] = jnp.sum(jnp.where(chosen, join3(picked), 0.0), axis=0, keepdims=True)


def forward(pool, w, head, row, act, target):
    rows, feat = pool.shape
    hid = w.shape[2]
    probes = row.shape[1]
    return pl.pallas_call(
        forward_kernel,
        in_specs=[HBM_SPEC] * 2 + [VMEM_SPEC] * 4,
        out_specs=[VMEM_SPEC] * 4,
        out_shape=[
            jax.ShapeDtypeStruct((rows, hid), BF16),
            jax.ShapeDtypeStruct((rows, hid // 2), F32),
            jax.ShapeDtypeStruct((1, probes), F32),
            jax.ShapeDtypeStruct((8, probes), F32),
        ],
        scratch_shapes=[
            pltpu.VMEM((PAD, rows), F32),
            pltpu.VMEM((rows, feat), BF16),
            pltpu.VMEM((2, feat, hid // 2), BF16),
            pltpu.VMEM((PAD, hid), F32),
            pltpu.SemaphoreType.DMA((4,)),
        ],
        compiler_params=params(42),
        cost_estimate=cost(0.3),
        name="forward",
    )(pool, w, head, row, act, target)


def turn_kernel(pool_hbm, after_ref, turned_ref, pool_ref, sems):
    del after_ref
    z, y, _ = spot()
    blocks, width, _ = turned_ref.shape
    copies = []
    for i in range(blocks):
        columns = pl.ds(pl.multiple_of(block_of(z, y, i) * width, width), width)
        copies.append(pltpu.make_async_copy(pool_hbm.at[:, columns], pool_ref.at[i], sems.at[i]))
        copies[i].start()
    for i in range(blocks):
        copies[i].wait()
        turned_ref[i] = pool_ref[i].T


def turned_pool(pool, first):
    rows, feat = pool.shape
    blocks = len(STEPS)
    return pl.pallas_call(
        turn_kernel,
        in_specs=[HBM_SPEC, VMEM_SPEC],
        out_specs=VMEM_SPEC,
        out_shape=jax.ShapeDtypeStruct((blocks, feat // blocks, rows), BF16),
        scratch_shapes=[
            pltpu.VMEM((blocks, rows, feat // blocks), BF16),
            pltpu.SemaphoreType.DMA((blocks,)),
        ],
        compiler_params=params(16),
        cost_estimate=cost(5),
        name="turned_pool",
    )(pool, first)


def distance_kernel(near_ref, far_ref, facts_ref, out_ref, pack_ref):
    pop = jnp.concatenate([near_ref[...], far_ref[...]], axis=0)
    agents = pop.shape[0]
    lanes = lax.broadcasted_iota(jnp.int32, (agents, 128), 1)
    total = jnp.zeros((agents, 128), F32)
    for i in range(agents):
        gap = pop - pop[i : i + 1, :]
        total = jnp.where(lanes == i, jnp.sum(gap * gap, axis=1, keepdims=True), total)
    out_ref[...] = total
    pack_ref[0:agents, :] = pop
    pack_ref[agents:, :] = facts_ref[...]


def distance_parts(near, far, facts):
    agents, probes = 2 * near.shape[0], near.shape[1]
    return pl.pallas_call(
        distance_kernel,
        in_specs=[VMEM_SPEC] * 3,
        out_specs=[VMEM_SPEC] * 2,
        out_shape=[
            jax.ShapeDtypeStruct((agents, 128), F32),
            jax.ShapeDtypeStruct((agents + facts.shape[0], probes), F32),
        ],
        compiler_params=params(16),
        cost_estimate=cost(0.2),
        name="distances",
    )(near, far, facts)


def partner_rows(z, y, share_refs, w_hbm, turned_ref, rows_ref, w_ref, sem):
    share, width = share_refs[0].shape[0], w_ref.shape[1]
    columns = pl.ds(pl.multiple_of(z // 2 * width, width), width)
    copy = pltpu.make_async_copy(w_hbm.at[0, :, columns], w_ref, sem)
    copy.start()
    for j, ref in enumerate(share_refs):
        rows_ref[pl.ds(j * share, share), :] = ref[...].astype(BF16)
    copy.wait()
    v = jnp.dot(rows_ref[...], w_ref[...], preferred_element_type=F32)
    turn(rows_ref, turned_ref, z, y, range(turned_ref.shape[0]))
    sig = sigmoid(v)
    return sig * (1.0 + v * (1.0 - sig))


def marked_sums(marked, hot):
    return join3(lax.dot_general(marked, hot, NT, preferred_element_type=F32))


def scaled(sums, cents, slope):
    part_hi = sums.astype(BF16)
    part_lo = (sums - part_hi.astype(F32)).astype(BF16)
    stacked = jnp.concatenate([part_hi, part_hi, part_lo], axis=0)
    return (lax.dot_general(stacked, cents, TN, preferred_element_type=F32) * slope).astype(BF16)


def partner_hot(where, first, share, row):
    return jnp.concatenate([row_onehot((where ^ SHARES[j]) * share, share, row) for j in (first, first + 1)], axis=0)


def partner_a_kernel(a_ref, b_ref, c_ref, d_ref, w_hbm, slope_ref, turned_ref, rows_ref, w_ref, sem):
    z, y, _ = spot()
    slope_ref[...] = partner_rows(z, y, (a_ref, b_ref, c_ref, d_ref), w_hbm, turned_ref, rows_ref, w_ref, sem)


def partner_b_kernel(
    a_ref, b_ref, c_ref, d_ref, w_hbm, marked_ref, cents_ref, pack_ref, dz_ref, turned_ref, rows_ref, w_ref, sem
):
    z, y, where = spot()
    share = a_ref.shape[0]
    slope = partner_rows(z, y, (a_ref, b_ref, c_ref, d_ref), w_hbm, turned_ref, rows_ref, w_ref, sem)
    row = pack_ref[17:18, :].astype(jnp.int32)
    for i in range(2):
        here = slice(2 * i * share, 2 * (i + 1) * share)
        sums = marked_sums(marked_ref[...], partner_hot(where, 4 + 2 * i, share, row))
        dz_ref[here, :] = scaled(sums, cents_ref[...], slope[here])


def partner_part(shares, w, more=()):
    share, feat = shares[0].shape
    half = w.shape[2] // 2
    blocks = len(STEPS)
    return pl.pallas_call(
        partner_b_kernel if more else partner_a_kernel,
        in_specs=[VMEM_SPEC] * 4 + [HBM_SPEC] + [VMEM_SPEC] * len(more),
        out_specs=[VMEM_SPEC] * 2,
        out_shape=[
            jax.ShapeDtypeStruct((4 * share, half), BF16 if more else F32),
            jax.ShapeDtypeStruct((blocks, feat // blocks, 4 * share), BF16),
        ],
        scratch_shapes=[
            pltpu.VMEM((4 * share, feat), BF16),
            pltpu.VMEM((feat, half), BF16),
            pltpu.SemaphoreType.DMA(()),
        ],
        compiler_params=params(16),
        cost_estimate=cost(0.3),
        name="partner",
    )(*shares, w, *more)


def coeff_kernel(
    total_probes, scaling, d0, d1, near_ref, far_ref, facts_ref, pack_ref, head_ref, slope_a_ref, slope_ref, hid_ref,
    dz_ref, heads_ref, marked_ref, cents_ref, sums_ref, wide_ref, ghead_ref,
):
    z, y, where = spot()
    width = slope_ref.shape[1]
    columns = pl.ds(pl.multiple_of(z // 2 * width, width), width)
    padded(head_ref, wide_ref)
    pop = jnp.concatenate([near_ref[...], far_ref[...]], axis=0)
    agents = pop.shape[0]
    pop2 = pack_ref[0:agents, :]
    row, act = facts_ref[1:2, :].astype(jnp.int32), facts_ref[2:3, :].astype(jnp.int32)
    row2 = pack_ref[agents + 1 : agents + 2, :].astype(jnp.int32)
    act2 = pack_ref[agents + 2 : agents + 3, :].astype(jnp.int32)
    lanes = lax.broadcasted_iota(jnp.int32, (agents, 128), 1)
    subs = lax.broadcasted_iota(jnp.int32, (agents, 128), 0)
    kern = jnp.exp(-(d0[...] + d1[...]) / total_probes)
    system = jnp.where(lanes < agents, kern, jnp.where((lanes == agents) & (subs == 0), 1.0, 0.0))
    for k in range(agents):
        pivot_row = system[k : k + 1, :] / system[k : k + 1, k : k + 1]
        system = jnp.where(subs == k, pivot_row, system - system[:, k : k + 1] * pivot_row)
    mix = system[:, agents : agents + 1] * kern[:, 0:1]

    def marked(people, target, act):
        emb = people[0:1, :]
        pulled = jnp.sum(mix * people, axis=0, keepdims=True)
        diverse = 2.0 * (jnp.sum(mix, axis=0, keepdims=True) * emb - pulled)
        coeff = scaling * (emb - target) + scaling * diverse
        chosen = lax.broadcasted_iota(jnp.int32, (PAD, act.shape[1]), 0) == act
        return split3(jnp.where(chosen, coeff, 0.0))

    head = wide_ref[:, columns]
    centered = head - jnp.sum(head, axis=0, keepdims=True) / ACTIONS
    cent_hi = centered.astype(BF16)
    cent_lo = (centered - cent_hi.astype(F32)).astype(BF16)
    cents = jnp.concatenate([cent_hi, cent_lo, cent_hi], axis=0)

    rows = slope_ref.shape[0]
    tile = 256
    mine = marked(pop, facts_ref[0:1, :], act)
    theirs = marked(pop2, pack_ref[agents : agents + 1, :], act2)
    marked_ref[...] = theirs
    cents_ref[...] = cents
    for i in range(rows // tile):
        here = pl.ds(i * tile, tile)
        sums = marked_sums(mine, row_onehot(i * tile, tile, row))
        sums_ref[:, here] = sums
        dz_ref[here, :] = scaled(sums, cents, slope_ref[here, :])
    share = tile // 2
    for i in range(slope_a_ref.shape[0] // tile):
        sums = marked_sums(theirs, partner_hot(where, 2 * i, share, row2))
        dz_ref[pl.ds(rows + i * tile, tile), :] = scaled(sums, cents, slope_a_ref[pl.ds(i * tile, tile), :])
    sums = sums_ref[...]
    even = split3(sums - jnp.sum(sums, axis=0, keepdims=True) / ACTIONS)
    ghead_ref[...] = join3(jnp.dot(even, hid_ref[...], preferred_element_type=F32))
    blocks = heads_ref.shape[0]
    cols = ghead_ref.shape[1] // blocks
    for i in range(blocks):
        place = block_of(z, y, i)
        pair = ghead_ref[:, pl.ds(pl.multiple_of(place // 2 * 2 * cols, 2 * cols), 2 * cols)]
        mine = jnp.where(place % 2 == 0, pair[:, :cols], pair[:, cols:])
        laid = [mine[g * EXTRA : (g + 1) * EXTRA] for g in range(3)]
        rest = jnp.zeros((EXTRA, heads_ref.shape[2] - 3 * cols), F32)
        heads_ref[i] = jnp.concatenate(laid + [rest], axis=1)


def coefficients(total_probes, dists, near, far, facts, pack, head, slope_a, slope, hid):
    rows, width = hid.shape
    half = width // 2
    scaling = math.sqrt(HID / total_probes)
    return pl.pallas_call(
        functools.partial(coeff_kernel, total_probes, scaling),
        in_specs=[VMEM_SPEC] * 10,
        out_specs=[VMEM_SPEC] * 4,
        out_shape=[
            jax.ShapeDtypeStruct((rows + slope_a.shape[0], half), BF16),
            jax.ShapeDtypeStruct((len(STEPS), EXTRA, half), F32),
            jax.ShapeDtypeStruct((3 * PAD, rows), BF16),
            jax.ShapeDtypeStruct((3 * PAD, half), BF16),
        ],
        scratch_shapes=[
            pltpu.VMEM((PAD, rows), F32),
            pltpu.VMEM((PAD, width), F32),
            pltpu.VMEM((PAD, width), F32),
        ],
        compiler_params=params(16),
        cost_estimate=cost(0.3),
        name="coefficients",
    )(*dists, near, far, facts, pack, head, slope_a, slope, hid)


def grad_kernel(plan, *refs):
    own_ref, a_ref, b_ref, dz_ref, dz_b_ref, heads_ref = refs[:6]
    mine, part = own_ref.shape[2], a_ref.shape[2]
    width = dz_ref.shape[1]
    products = ((own_ref, dz_ref, 0, mine), (a_ref, dz_ref, mine, part), (b_ref, dz_b_ref, 0, part))
    for blocks, begin, end, outs, more in plan:
        rows = end - begin
        total = jnp.zeros((2 * rows, width), F32)
        for ref, right_ref, start, depth in products:
            left = jnp.concatenate([ref[i, begin:end, :] for i in blocks], axis=0)
            total += jnp.dot(left, right_ref[start : start + depth, :], preferred_element_type=F32)
        for q, block in enumerate(blocks):
            for out, at, size, extra in outs:
                out_ref, slot = refs[out[q][0]], out[q][1]
                value = total[q * rows + at : q * rows + at + size]
                heads = heads_ref[block] if extra else None
                if more is not None:
                    add_ref, add_slot = refs[more[q][0]], more[q][1]
                    value = value + add_ref[add_slot, 0:size, :]
                    heads = heads + add_ref[add_slot, size:, :] if extra else None
                out_ref[slot, 0:size, :] = value
                if extra:
                    out_ref[slot, size:, :] = heads


def gradient(parts, groups, which, more=None):
    dz = parts[3]
    width = dz.shape[1]
    chunks = [(sum(CHUNKS[:c]), CHUNKS[c], c == len(CHUNKS) - 1) for c in which]
    begin, end = chunks[0][0], chunks[-1][0] + chunks[-1][1]
    shapes = [
        jax.ShapeDtypeStruct((len(group), size + (EXTRA if extra else 0), width), F32)
        for group in groups
        for _, size, extra in chunks
    ]
    extras = [] if more is None else [more]
    first = len(parts) + len(extras)
    places = [(block, g, slot) for g, group in enumerate(groups) for slot, block in enumerate(group)]
    plan = []
    for k in range(0, len(places), 2):
        pair = places[k : k + 2]
        outs = [
            ([(first + g * len(chunks) + c, slot) for _, g, slot in pair], at - begin, size, extra)
            for c, (at, size, extra) in enumerate(chunks)
        ]
        added = None if more is None else [(len(parts), k), (len(parts), k + 1)]
        plan.append(([block for block, _, _ in pair], begin, end, outs, added))
    outs = pl.pallas_call(
        functools.partial(grad_kernel, plan),
        in_specs=[VMEM_SPEC] * first,
        out_specs=[VMEM_SPEC] * len(shapes),
        out_shape=shapes,
        compiler_params=params(16),
        cost_estimate=cost(0.3),
        name="gradient",
    )(*parts, *extras)
    return [outs[i : i + len(chunks)] for i in range(0, len(outs), len(chunks))]


def add_kernel(at, into_ref, more_ref, out_ref):
    here = slice(at, at + more_ref.shape[0])
    out_ref[here] = into_ref[here] + more_ref[...]


def add_into(into, more, at):
    return pl.pallas_call(
        functools.partial(add_kernel, at),
        in_specs=[VMEM_SPEC] * 2,
        out_specs=VMEM_SPEC,
        out_shape=jax.ShapeDtypeStruct(into.shape, F32),
        input_output_aliases={0: 0},
        compiler_params=params(16),
        cost_estimate=cost(0.1),
        name="add_into",
    )(into, more)


def fold_kernel(count, *refs):
    at = 0
    for out_ref in refs[count:]:
        size = out_ref.shape[0]
        out_ref[...] = sum((ref[at : at + size] for ref in refs[1:count]), refs[0][at : at + size])
        at += size


def fold(terms, per):
    blocks = terms[0].shape[0] // per
    return pl.pallas_call(
        functools.partial(fold_kernel, len(terms)),
        in_specs=[VMEM_SPEC] * len(terms),
        out_specs=[VMEM_SPEC] * blocks,
        out_shape=[jax.ShapeDtypeStruct((per, *terms[0].shape[1:]), F32)] * blocks,
        compiler_params=params(16),
        cost_estimate=cost(0.1),
        name="fold",
    )(*terms)


def finish_kernel(*refs):
    out_ref, two_ref = refs[-2:]
    z, _, _ = spot()
    width = refs[0].shape[2]
    left = pl.ds(pl.multiple_of(z // 2 * width, width), width)
    right = pl.ds(pl.multiple_of((1 - z // 2) * width, width), width)
    at = 0
    for c, size in enumerate(CHUNKS):
        own, other = refs[2 * c : 2 * c + 2]
        out_ref[0, at : at + size, left] = own[0, 0:size, :]
        out_ref[0, at : at + size, right] = other[0, 0:size, :]
        at += size
    heads = own[0, CHUNKS[-1] :, :] + other[0, CHUNKS[-1] :, :]
    cols = two_ref.shape[2]
    for g in range(3):
        count = min(EXTRA, ACTIONS - g * EXTRA)
        two_ref[g * EXTRA : g * EXTRA + count] = heads[0:count, g * cols : (g + 1) * cols].reshape(count, 1, cols)


def finish(pieces, cols):
    rows, width = sum(CHUNKS), pieces[0].shape[2]
    return pl.pallas_call(
        finish_kernel,
        grid=(1,),
        in_specs=[VMEM_SPEC] * len(pieces),
        out_specs=[
            pl.BlockSpec((1, rows, 2 * width), lambda i: (0, 0, 0)),
            pl.BlockSpec((ACTIONS, 1, cols), lambda i: (0, 0, 0)),
        ],
        out_shape=[
            jax.ShapeDtypeStruct((1, rows, 2 * width), F32),
            jax.ShapeDtypeStruct((ACTIONS, 1, cols), F32),
        ],
        compiler_params=params(16),
        cost_estimate=cost(0.1),
        name="finish",
    )(*pieces)


def shift_y(v, s):
    return lax.ppermute(v, "dp", [(z * 4 + y, z * 4 + (y + s) % 4) for z in range(4) for y in range(4)])


def swap(v, axis, mask):
    return lax.ppermute(v, axis, [(i, i ^ mask) for i in range(16)])


def to_partner_rows(v):
    return lax.ppermute(
        v,
        ("pop", "dp"),
        [(p * 16 + d, (p ^ (8 if d // 4 in (0, 3) else 0)) * 16 + (d ^ 12)) for p in range(16) for d in range(16)],
    )


def body(state_pool, probe_row, action, w_hidden, w_head, targets):
    probes = probe_row.shape[0]
    total_probes = probes * lax.axis_size("dp")
    share = state_pool.shape[0] // len(SHARES)
    row = probe_row.reshape(1, probes)
    act = action.reshape(1, probes)

    _, _, where = spot()
    cut = lambda i: lax.dynamic_slice_in_dim(state_pool, i * share, share, 0).astype(F32)
    share0 = to_partner_rows(cut(where))
    next_share = cut(where ^ 4)

    hid, slope, near, facts = forward(state_pool, w_hidden, w_head, row, act, targets)
    for mask in (1, 2, 4):
        near = jnp.concatenate([near, swap(near, "pop", mask)], axis=0)
    turned = turned_pool(state_pool, near)
    far = after(swap(near, "pop", 8), turned)
    share4 = to_partner_rows(after(next_share, far))
    share0 = after(share0, far)
    share2, share6 = swap(share0, "pop", 2), swap(share0, "pop", 6)
    part, pack = distance_parts(near, far, facts)
    part = part + swap(part, "dp", 1)
    pack = after(pack, part)
    part = part + swap(part, "dp", 2)
    pack = swap(pack, "dp", 12)
    part = part + swap(part, "dp", 4)
    dists = [part, swap(part, "dp", 8)]

    swapped0 = swap(after(share0, pack), "pop", 1)
    share0, share2, share4, share6 = after([share0, share2, share4, share6], pack, *dists)
    swapped = [swapped0] + [swap(v, "pop", 1) for v in (share2, share4, share6)]
    slope_a, turned_a = partner_part([share0, share2, share4, share6], w_hidden)
    dz, heads, marks, cents = coefficients(
        total_probes, dists, near, far, facts, pack, w_head, slope_a, slope, hid
    )
    dz_b, turned_b = partner_part(swapped, w_hidden, (marks, cents, pack))

    parts = [turned, turned_a, turned_b, dz, dz_b, heads]
    tie = lambda *first: parts[:3] + [after(dz, *first)] + parts[4:]
    early, last = range(len(CHUNKS) - 1), [len(CHUNKS) - 1]
    a2s, b2s = gradient(parts, [[0, 1], [2, 3]], early)
    from_a, from_b = [], []
    for i in early:
        from_a.append(shift_y(a2s[i], 1))
        from_b.append(shift_y(b2s[i], -1))
    away = [4 * g + k for g in range(4) for k in (2, 3)]
    waiting = []
    tied = tie(*a2s)
    for i in early:
        (ones,), (threes,), (zeros,) = gradient(tied, [[4, 5, 6, 7], [8, 9, 10, 11], [12, 13, 14, 15]], [i])
        if i == 0:
            ((sent,),) = gradient(tie(*a2s), [away], last)
            met = swap(sent, "dp", 4)
        ones, threes = add_into(ones, from_a[i], 0), add_into(threes, from_b[i], 2)
        waiting.append((zeros, shift_y(ones, 1), shift_y(threes, -1)))
        tied = tie(ones, threes)
    (a2,), (b2,), (ones,), (threes,), (zeros,) = gradient(tied, [[0], [1], [4, 5], [8, 9], [12, 13]], last, met)
    last_a, last_b = shift_y(a2, 1), shift_y(b2, -1)
    near_0, away_0 = fold(waiting[0], 2)
    met_0 = swap(away_0, "dp", 4)
    own_0, to_0 = fold((near_0, met_0), 1)
    other_0 = swap(to_0, "dp", 12)
    near_1, away_1 = fold(waiting[1], 2)
    met_1 = swap(away_1, "dp", 4)
    last_a, last_b = (last_a, last_b)
    ones, threes = add_into(ones, last_a, 0), add_into(threes, last_b, 1)
    own_2, to_2 = fold((zeros, shift_y(ones, 1), shift_y(threes, -1)), 1)
    other_2 = swap(to_2, "dp", 12)
    own_1, to_1 = fold((near_1, after(met_1, to_2)), 1)
    other_1 = swap(to_1, "dp", 12)
    pieces = [own_0, other_0, own_1, other_1, own_2, other_2]
    grad_one, grad_two = finish(pieces, w_head.shape[2] // 16)
    return grad_one, grad_two.transpose(1, 0, 2)


def solution(mesh):
    placed = (
        P("dp", None),
        P("dp"),
        P("dp"),
        P("pop", None, None),
        P("pop", None, None),
        P("pop", "dp"),
    )
    return jax.shard_map(
        body,
        mesh=mesh,
        in_specs=placed,
        out_specs=(P("pop", "dp", None), P("pop", None, "dp")),
        check_vma=False,
    )
```

```python
import functools
import math

import jax
import jax.numpy as jnp
from jax import lax
from jax.experimental import pallas as pl
from jax.experimental.pallas import tpu as pltpu
from jax.sharding import PartitionSpec as P

HID = 1024
ACTIONS = 18
PAD = 32
CHUNKS = (80, 48)
EXTRA = 8
SHARES = (0, 2, 4, 6, 1, 3, 5, 7)
STEPS = [(y, z) for y in (2, 1, 3, 0) for z in (0, 3, 1, 2)]
F32 = jnp.float32
BF16 = jnp.bfloat16
NT = (((1,), (1,)), ((), ()))
TN = (((0,), (0,)), ((), ()))
VMEM_SPEC = pl.BlockSpec(memory_space=pltpu.VMEM)
HBM_SPEC = pl.BlockSpec(memory_space=pltpu.HBM)


def params(mib):
    return pltpu.CompilerParams(vmem_limit_bytes=mib * 1024 * 1024)


def cost(us):
    return pl.CostEstimate(flops=int(us * 1.1e9), bytes_accessed=0, transcendentals=0)


def after(value, *first):
    return lax.optimization_barrier((value, first))[0]


def spot():
    place = lax.axis_index("dp")
    return place // 4, place % 4, lax.axis_index("pop") % len(SHARES)


def block_of(z, y, i):
    step_y, step_z = STEPS[i]
    return (z ^ step_z) * 4 + (y + step_y) % 4


def turn(rows_ref, turned_ref, z, y, blocks):
    width = turned_ref.shape[1]
    for i in blocks:
        start = pl.multiple_of(block_of(z, y, i) * width, width)
        turned_ref[i] = rows_ref[:, pl.ds(start, width)].T


def padded(head_ref, wide_ref):
    wide_ref[...] = jnp.zeros_like(wide_ref)
    wide_ref[0:ACTIONS, :] = head_ref[0].astype(F32)


def split3(v):
    hi = v.astype(BF16)
    rest = v - hi.astype(F32)
    mid = rest.astype(BF16)
    low = (rest - mid.astype(F32)).astype(BF16)
    return jnp.concatenate([hi, mid, low], axis=0)


def join3(v):
    return v[:PAD] + v[PAD : 2 * PAD] + v[2 * PAD :]


def row_onehot(start, size, row):
    ids = lax.broadcasted_iota(jnp.int32, (size, row.shape[1]), 0) + start
    return jnp.where(ids == row, 1.0, 0.0).astype(BF16)


def sigmoid(v):
    return 0.5 * jnp.tanh(0.5 * v) + 0.5


def forward_kernel(
    pool_hbm, w_hbm, head_ref, row_ref, act_ref, target_ref, hid_ref, slope_ref, turned_ref, emb_ref, facts_ref,
    acc_ref, pool_ref, w_ref, wide_ref, sems,
):
    z, y, _ = spot()
    rows, hidden = hid_ref.shape
    tile, width = rows // 2, hidden // 2
    row_of = lambda i: pl.ds(i * tile, tile)
    pools = [pltpu.make_async_copy(pool_hbm.at[row_of(i), :], pool_ref.at[row_of(i), :], sems.at[i]) for i in range(2)]
    halves = [
        pltpu.make_async_copy(w_hbm.at[0, :, pl.ds(j * width, width)], w_ref.at[j], sems.at[2 + j]) for j in range(2)
    ]
    for copy in (pools[0], halves[0], halves[1], pools[1]):
        copy.start()
    padded(head_ref, wide_ref)
    facts_ref[0:1, :] = target_ref[...]
    facts_ref[1:2, :] = row_ref[...].astype(F32)
    facts_ref[2:3, :] = act_ref[...].astype(F32)
    facts_ref[3:, :] = jnp.zeros((facts_ref.shape[0] - 3, facts_ref.shape[1]), F32)
    pools[0].wait()
    for i in range(2):
        if i == 1:
            pools[1].wait()
        for j in range(2):
            if i == 0:
                halves[j].wait()
            columns = slice(j * width, (j + 1) * width)
            v = jnp.dot(pool_ref[row_of(i), :], w_ref[j], preferred_element_type=F32)
            sig = sigmoid(v)
            hid = (v * sig).astype(BF16)
            hid_ref[row_of(i), columns] = hid

            @pl.when(z // 2 == j)
            def _():
                slope_ref[row_of(i), :] = sig * (1.0 + v * (1.0 - sig))

            logits = lax.dot_general(wide_ref[:, columns].astype(BF16), hid, NT, preferred_element_type=F32)
            if j == 0:
                acc_ref[:, row_of(i)] = logits
            else:
                acc_ref[:, row_of(i)] += logits
                if i == 1:
                    turn(pool_ref, turned_ref, z, y, range(turned_ref.shape[0]))
    logits = acc_ref[...]
    parts = split3(logits - jnp.sum(logits, axis=0, keepdims=True) / ACTIONS)
    picked = jnp.zeros((3 * PAD, row_ref.shape[1]), F32)
    for i in range(0, rows, 256):
        picked += jnp.dot(parts[:, i : i + 256], row_onehot(i, 256, row_ref[...]), preferred_element_type=F32)
    chosen = lax.broadcasted_iota(jnp.int32, (PAD, row_ref.shape[1]), 0) == act_ref[...]
    emb_ref[...] = jnp.sum(jnp.where(chosen, join3(picked), 0.0), axis=0, keepdims=True)


def forward(pool, w, head, row, act, target):
    rows, feat = pool.shape
    hid = w.shape[2]
    probes = row.shape[1]
    blocks = len(STEPS)
    return pl.pallas_call(
        forward_kernel,
        in_specs=[HBM_SPEC] * 2 + [VMEM_SPEC] * 4,
        out_specs=[VMEM_SPEC] * 5,
        out_shape=[
            jax.ShapeDtypeStruct((rows, hid), BF16),
            jax.ShapeDtypeStruct((rows, hid // 2), F32),
            jax.ShapeDtypeStruct((blocks, feat // blocks, rows), BF16),
            jax.ShapeDtypeStruct((1, probes), F32),
            jax.ShapeDtypeStruct((8, probes), F32),
        ],
        scratch_shapes=[
            pltpu.VMEM((PAD, rows), F32),
            pltpu.VMEM((rows, feat), BF16),
            pltpu.VMEM((2, feat, hid // 2), BF16),
            pltpu.VMEM((PAD, hid), F32),
            pltpu.SemaphoreType.DMA((4,)),
        ],
        compiler_params=params(42),
        cost_estimate=cost(0.3),
        name="forward",
    )(pool, w, head, row, act, target)


def distance_kernel(near_ref, far_ref, facts_ref, out_ref, pack_ref):
    pop = jnp.concatenate([near_ref[...], far_ref[...]], axis=0)
    agents = pop.shape[0]
    lanes = lax.broadcasted_iota(jnp.int32, (agents, 128), 1)
    total = jnp.zeros((agents, 128), F32)
    for i in range(agents):
        gap = pop - pop[i : i + 1, :]
        total = jnp.where(lanes == i, jnp.sum(gap * gap, axis=1, keepdims=True), total)
    out_ref[...] = total
    pack_ref[0:agents, :] = pop
    pack_ref[agents:, :] = facts_ref[...]


def distance_parts(near, far, facts):
    agents, probes = 2 * near.shape[0], near.shape[1]
    return pl.pallas_call(
        distance_kernel,
        in_specs=[VMEM_SPEC] * 3,
        out_specs=[VMEM_SPEC] * 2,
        out_shape=[
            jax.ShapeDtypeStruct((agents, 128), F32),
            jax.ShapeDtypeStruct((agents + facts.shape[0], probes), F32),
        ],
        compiler_params=params(16),
        cost_estimate=cost(0.2),
        name="distances",
    )(near, far, facts)


def partner_rows(z, y, share_refs, w_hbm, turned_ref, rows_ref, w_ref, sem):
    share, width = share_refs[0].shape[0], w_ref.shape[1]
    columns = pl.ds(pl.multiple_of(z // 2 * width, width), width)
    copy = pltpu.make_async_copy(w_hbm.at[0, :, columns], w_ref, sem)
    copy.start()
    for j, ref in enumerate(share_refs):
        rows_ref[pl.ds(j * share, share), :] = ref[...].astype(BF16)
    copy.wait()
    v = jnp.dot(rows_ref[...], w_ref[...], preferred_element_type=F32)
    turn(rows_ref, turned_ref, z, y, range(turned_ref.shape[0]))
    sig = sigmoid(v)
    return sig * (1.0 + v * (1.0 - sig))


def marked_sums(marked, hot):
    return join3(lax.dot_general(marked, hot, NT, preferred_element_type=F32))


def scaled(sums, cents, slope):
    part_hi = sums.astype(BF16)
    part_lo = (sums - part_hi.astype(F32)).astype(BF16)
    stacked = jnp.concatenate([part_hi, part_hi, part_lo], axis=0)
    return (lax.dot_general(stacked, cents, TN, preferred_element_type=F32) * slope).astype(BF16)


def partner_hot(where, first, share, row):
    return jnp.concatenate([row_onehot((where ^ SHARES[j]) * share, share, row) for j in (first, first + 1)], axis=0)


def partner_a_kernel(a_ref, b_ref, c_ref, d_ref, w_hbm, slope_ref, turned_ref, rows_ref, w_ref, sem):
    z, y, _ = spot()
    slope_ref[...] = partner_rows(z, y, (a_ref, b_ref, c_ref, d_ref), w_hbm, turned_ref, rows_ref, w_ref, sem)


def partner_b_kernel(
    a_ref, b_ref, c_ref, d_ref, w_hbm, marked_ref, cents_ref, pack_ref, dz_ref, turned_ref, rows_ref, w_ref, sem
):
    z, y, where = spot()
    share = a_ref.shape[0]
    slope = partner_rows(z, y, (a_ref, b_ref, c_ref, d_ref), w_hbm, turned_ref, rows_ref, w_ref, sem)
    row = pack_ref[17:18, :].astype(jnp.int32)
    for i in range(2):
        here = slice(2 * i * share, 2 * (i + 1) * share)
        sums = marked_sums(marked_ref[...], partner_hot(where, 4 + 2 * i, share, row))
        dz_ref[here, :] = scaled(sums, cents_ref[...], slope[here])


def partner_part(shares, w, more=()):
    share, feat = shares[0].shape
    half = w.shape[2] // 2
    blocks = len(STEPS)
    return pl.pallas_call(
        partner_b_kernel if more else partner_a_kernel,
        in_specs=[VMEM_SPEC] * 4 + [HBM_SPEC] + [VMEM_SPEC] * len(more),
        out_specs=[VMEM_SPEC] * 2,
        out_shape=[
            jax.ShapeDtypeStruct((4 * share, half), BF16 if more else F32),
            jax.ShapeDtypeStruct((blocks, feat // blocks, 4 * share), BF16),
        ],
        scratch_shapes=[
            pltpu.VMEM((4 * share, feat), BF16),
            pltpu.VMEM((feat, half), BF16),
            pltpu.SemaphoreType.DMA(()),
        ],
        compiler_params=params(16),
        cost_estimate=cost(0.3),
        name="partner",
    )(*shares, w, *more)


def coeff_kernel(
    total_probes, scaling, d0, d1, near_ref, far_ref, facts_ref, pack_ref, head_ref, slope_a_ref, slope_ref, hid_ref,
    dz_ref, heads_ref, marked_ref, cents_ref, sums_ref, wide_ref, ghead_ref,
):
    z, y, where = spot()
    width = slope_ref.shape[1]
    columns = pl.ds(pl.multiple_of(z // 2 * width, width), width)
    padded(head_ref, wide_ref)
    pop = jnp.concatenate([near_ref[...], far_ref[...]], axis=0)
    agents = pop.shape[0]
    pop2 = pack_ref[0:agents, :]
    row, act = facts_ref[1:2, :].astype(jnp.int32), facts_ref[2:3, :].astype(jnp.int32)
    row2 = pack_ref[agents + 1 : agents + 2, :].astype(jnp.int32)
    act2 = pack_ref[agents + 2 : agents + 3, :].astype(jnp.int32)
    lanes = lax.broadcasted_iota(jnp.int32, (agents, 128), 1)
    subs = lax.broadcasted_iota(jnp.int32, (agents, 128), 0)
    kern = jnp.exp(-(d0[...] + d1[...]) / total_probes)
    system = jnp.where(lanes < agents, kern, jnp.where((lanes == agents) & (subs == 0), 1.0, 0.0))
    for k in range(agents):
        pivot_row = system[k : k + 1, :] / system[k : k + 1, k : k + 1]
        system = jnp.where(subs == k, pivot_row, system - system[:, k : k + 1] * pivot_row)
    mix = system[:, agents : agents + 1] * kern[:, 0:1]

    def marked(people, target, act):
        emb = people[0:1, :]
        pulled = jnp.sum(mix * people, axis=0, keepdims=True)
        diverse = 2.0 * (jnp.sum(mix, axis=0, keepdims=True) * emb - pulled)
        coeff = scaling * (emb - target) + scaling * diverse
        chosen = lax.broadcasted_iota(jnp.int32, (PAD, act.shape[1]), 0) == act
        return split3(jnp.where(chosen, coeff, 0.0))

    head = wide_ref[:, columns]
    centered = head - jnp.sum(head, axis=0, keepdims=True) / ACTIONS
    cent_hi = centered.astype(BF16)
    cent_lo = (centered - cent_hi.astype(F32)).astype(BF16)
    cents = jnp.concatenate([cent_hi, cent_lo, cent_hi], axis=0)

    rows = slope_ref.shape[0]
    tile = 256
    mine = marked(pop, facts_ref[0:1, :], act)
    theirs = marked(pop2, pack_ref[agents : agents + 1, :], act2)
    marked_ref[...] = theirs
    cents_ref[...] = cents
    for i in range(rows // tile):
        here = pl.ds(i * tile, tile)
        sums = marked_sums(mine, row_onehot(i * tile, tile, row))
        sums_ref[:, here] = sums
        dz_ref[here, :] = scaled(sums, cents, slope_ref[here, :])
    share = tile // 2
    for i in range(slope_a_ref.shape[0] // tile):
        sums = marked_sums(theirs, partner_hot(where, 2 * i, share, row2))
        dz_ref[pl.ds(rows + i * tile, tile), :] = scaled(sums, cents, slope_a_ref[pl.ds(i * tile, tile), :])
    sums = sums_ref[...]
    even = split3(sums - jnp.sum(sums, axis=0, keepdims=True) / ACTIONS)
    ghead_ref[...] = join3(jnp.dot(even, hid_ref[...], preferred_element_type=F32))
    blocks = heads_ref.shape[0]
    cols = ghead_ref.shape[1] // blocks
    for i in range(blocks):
        place = block_of(z, y, i)
        pair = ghead_ref[:, pl.ds(pl.multiple_of(place // 2 * 2 * cols, 2 * cols), 2 * cols)]
        mine = jnp.where(place % 2 == 0, pair[:, :cols], pair[:, cols:])
        laid = [mine[g * EXTRA : (g + 1) * EXTRA] for g in range(3)]
        rest = jnp.zeros((EXTRA, heads_ref.shape[2] - 3 * cols), F32)
        heads_ref[i] = jnp.concatenate(laid + [rest], axis=1)


def coefficients(total_probes, dists, near, far, facts, pack, head, slope_a, slope, hid):
    rows, width = hid.shape
    half = width // 2
    scaling = math.sqrt(HID / total_probes)
    return pl.pallas_call(
        functools.partial(coeff_kernel, total_probes, scaling),
        in_specs=[VMEM_SPEC] * 10,
        out_specs=[VMEM_SPEC] * 4,
        out_shape=[
            jax.ShapeDtypeStruct((rows + slope_a.shape[0], half), BF16),
            jax.ShapeDtypeStruct((len(STEPS), EXTRA, half), F32),
            jax.ShapeDtypeStruct((3 * PAD, rows), BF16),
            jax.ShapeDtypeStruct((3 * PAD, half), BF16),
        ],
        scratch_shapes=[
            pltpu.VMEM((PAD, rows), F32),
            pltpu.VMEM((PAD, width), F32),
            pltpu.VMEM((PAD, width), F32),
        ],
        compiler_params=params(16),
        cost_estimate=cost(0.3),
        name="coefficients",
    )(*dists, near, far, facts, pack, head, slope_a, slope, hid)


def grad_kernel(plan, *refs):
    own_ref, a_ref, b_ref, dz_ref, dz_b_ref, heads_ref = refs[:6]
    mine, part = own_ref.shape[2], a_ref.shape[2]
    width = dz_ref.shape[1]
    products = ((own_ref, dz_ref, 0, mine), (a_ref, dz_ref, mine, part), (b_ref, dz_b_ref, 0, part))
    for blocks, begin, end, outs, more in plan:
        rows = end - begin
        total = jnp.zeros((2 * rows, width), F32)
        for ref, right_ref, start, depth in products:
            left = jnp.concatenate([ref[i, begin:end, :] for i in blocks], axis=0)
            total += jnp.dot(left, right_ref[start : start + depth, :], preferred_element_type=F32)
        for q, block in enumerate(blocks):
            for out, at, size, extra in outs:
                out_ref, slot = refs[out[q][0]], out[q][1]
                value = total[q * rows + at : q * rows + at + size]
                heads = heads_ref[block] if extra else None
                if more is not None:
                    add_ref, add_slot = refs[more[q][0]], more[q][1]
                    value = value + add_ref[add_slot, 0:size, :]
                    heads = heads + add_ref[add_slot, size:, :] if extra else None
                out_ref[slot, 0:size, :] = value
                if extra:
                    out_ref[slot, size:, :] = heads


def gradient(parts, groups, which, more=None):
    dz = parts[3]
    width = dz.shape[1]
    chunks = [(sum(CHUNKS[:c]), CHUNKS[c], c == len(CHUNKS) - 1) for c in which]
    begin, end = chunks[0][0], chunks[-1][0] + chunks[-1][1]
    shapes = [
        jax.ShapeDtypeStruct((len(group), size + (EXTRA if extra else 0), width), F32)
        for group in groups
        for _, size, extra in chunks
    ]
    extras = [] if more is None else [more]
    first = len(parts) + len(extras)
    places = [(block, g, slot) for g, group in enumerate(groups) for slot, block in enumerate(group)]
    plan = []
    for k in range(0, len(places), 2):
        pair = places[k : k + 2]
        outs = [
            ([(first + g * len(chunks) + c, slot) for _, g, slot in pair], at - begin, size, extra)
            for c, (at, size, extra) in enumerate(chunks)
        ]
        added = None if more is None else [(len(parts), k), (len(parts), k + 1)]
        plan.append(([block for block, _, _ in pair], begin, end, outs, added))
    outs = pl.pallas_call(
        functools.partial(grad_kernel, plan),
        in_specs=[VMEM_SPEC] * first,
        out_specs=[VMEM_SPEC] * len(shapes),
        out_shape=shapes,
        compiler_params=params(16),
        cost_estimate=cost(0.3),
        name="gradient",
    )(*parts, *extras)
    return [outs[i : i + len(chunks)] for i in range(0, len(outs), len(chunks))]


def add_kernel(at, into_ref, more_ref, out_ref):
    here = slice(at, at + more_ref.shape[0])
    out_ref[here] = into_ref[here] + more_ref[...]


def add_into(into, more, at):
    return pl.pallas_call(
        functools.partial(add_kernel, at),
        in_specs=[VMEM_SPEC] * 2,
        out_specs=VMEM_SPEC,
        out_shape=jax.ShapeDtypeStruct(into.shape, F32),
        input_output_aliases={0: 0},
        compiler_params=params(16),
        cost_estimate=cost(0.1),
        name="add_into",
    )(into, more)


def fold_kernel(count, *refs):
    at = 0
    for out_ref in refs[count:]:
        size = out_ref.shape[0]
        out_ref[...] = sum((ref[at : at + size] for ref in refs[1:count]), refs[0][at : at + size])
        at += size


def fold(terms, per):
    blocks = terms[0].shape[0] // per
    return pl.pallas_call(
        functools.partial(fold_kernel, len(terms)),
        in_specs=[VMEM_SPEC] * len(terms),
        out_specs=[VMEM_SPEC] * blocks,
        out_shape=[jax.ShapeDtypeStruct((per, *terms[0].shape[1:]), F32)] * blocks,
        compiler_params=params(16),
        cost_estimate=cost(0.1),
        name="fold",
    )(*terms)


def finish_kernel(*refs):
    out_ref, two_ref = refs[-2:]
    z, _, _ = spot()
    width = refs[0].shape[2]
    left = pl.ds(pl.multiple_of(z // 2 * width, width), width)
    right = pl.ds(pl.multiple_of((1 - z // 2) * width, width), width)
    at = 0
    for c, size in enumerate(CHUNKS):
        own, other = refs[2 * c : 2 * c + 2]
        out_ref[0, at : at + size, left] = own[0, 0:size, :]
        out_ref[0, at : at + size, right] = other[0, 0:size, :]
        at += size
    heads = own[0, CHUNKS[-1] :, :] + other[0, CHUNKS[-1] :, :]
    cols = two_ref.shape[2]
    for g in range(3):
        count = min(EXTRA, ACTIONS - g * EXTRA)
        two_ref[g * EXTRA : g * EXTRA + count] = heads[0:count, g * cols : (g + 1) * cols].reshape(count, 1, cols)


def finish(pieces, cols):
    rows, width = sum(CHUNKS), pieces[0].shape[2]
    return pl.pallas_call(
        finish_kernel,
        grid=(1,),
        in_specs=[VMEM_SPEC] * len(pieces),
        out_specs=[
            pl.BlockSpec((1, rows, 2 * width), lambda i: (0, 0, 0)),
            pl.BlockSpec((ACTIONS, 1, cols), lambda i: (0, 0, 0)),
        ],
        out_shape=[
            jax.ShapeDtypeStruct((1, rows, 2 * width), F32),
            jax.ShapeDtypeStruct((ACTIONS, 1, cols), F32),
        ],
        compiler_params=params(16),
        cost_estimate=cost(0.1),
        name="finish",
    )(*pieces)


def shift_y(v, s):
    return lax.ppermute(v, "dp", [(z * 4 + y, z * 4 + (y + s) % 4) for z in range(4) for y in range(4)])


def swap(v, axis, mask):
    return lax.ppermute(v, axis, [(i, i ^ mask) for i in range(16)])


def to_partner_rows(v):
    return lax.ppermute(
        v,
        ("pop", "dp"),
        [(p * 16 + d, (p ^ (8 if d // 4 in (0, 3) else 0)) * 16 + (d ^ 12)) for p in range(16) for d in range(16)],
    )


def body(state_pool, probe_row, action, w_hidden, w_head, targets):
    probes = probe_row.shape[0]
    total_probes = probes * lax.axis_size("dp")
    share = state_pool.shape[0] // len(SHARES)
    row = probe_row.reshape(1, probes)
    act = action.reshape(1, probes)

    _, _, where = spot()
    cut = lambda i: lax.dynamic_slice_in_dim(state_pool, i * share, share, 0).astype(F32)
    share0 = to_partner_rows(cut(where))
    next_share = cut(where ^ 4)

    hid, slope, turned, near, facts = forward(state_pool, w_hidden, w_head, row, act, targets)
    for mask in (1, 2, 4):
        near = jnp.concatenate([near, swap(near, "pop", mask)], axis=0)
    far = swap(near, "pop", 8)
    share4 = to_partner_rows(after(next_share, far))
    share0 = after(share0, far)
    share2, share6 = swap(share0, "pop", 2), swap(share0, "pop", 6)
    part, pack = distance_parts(near, far, facts)
    part = part + swap(part, "dp", 1)
    pack = after(pack, part)
    part = part + swap(part, "dp", 2)
    pack = swap(pack, "dp", 12)
    part = part + swap(part, "dp", 4)
    dists = [part, swap(part, "dp", 8)]

    swapped0 = swap(after(share0, pack), "pop", 1)
    share0, share2, share4, share6 = after([share0, share2, share4, share6], pack, *dists)
    swapped = [swapped0] + [swap(v, "pop", 1) for v in (share2, share4, share6)]
    slope_a, turned_a = partner_part([share0, share2, share4, share6], w_hidden)
    dz, heads, marks, cents = coefficients(
        total_probes, dists, near, far, facts, pack, w_head, slope_a, slope, hid
    )
    dz_b, turned_b = partner_part(swapped, w_hidden, (marks, cents, pack))

    parts = [turned, turned_a, turned_b, dz, dz_b, heads]
    tie = lambda *first: parts[:3] + [after(dz, *first)] + parts[4:]
    early, last = range(len(CHUNKS) - 1), [len(CHUNKS) - 1]
    a2s, b2s = gradient(parts, [[0, 1], [2, 3]], early)
    from_a, from_b = [], []
    for i in early:
        from_a.append(shift_y(a2s[i], 1))
        from_b.append(shift_y(b2s[i], -1))
    away = [4 * g + k for g in range(4) for k in (2, 3)]
    waiting = []
    tied = tie(*a2s)
    for i in early:
        (ones,), (threes,), (zeros,) = gradient(tied, [[4, 5, 6, 7], [8, 9, 10, 11], [12, 13, 14, 15]], [i])
        if i == 0:
            ((sent,),) = gradient(tie(*a2s), [away], last)
            met = swap(sent, "dp", 4)
        ones, threes = add_into(ones, from_a[i], 0), add_into(threes, from_b[i], 2)
        waiting.append((zeros, shift_y(ones, 1), shift_y(threes, -1)))
        tied = tie(ones, threes)
    (a2,), (b2,), (ones,), (threes,), (zeros,) = gradient(tied, [[0], [1], [4, 5], [8, 9], [12, 13]], last, met)
    last_a, last_b = shift_y(a2, 1), shift_y(b2, -1)
    near_0, away_0 = fold(after(waiting[0], a2, b2), 2)
    met_0 = swap(away_0, "dp", 4)
    last_a, last_b = after((last_a, last_b), away_0)
    ones, threes = add_into(ones, last_a, 0), add_into(threes, last_b, 1)
    last_terms = (zeros, shift_y(ones, 1), shift_y(threes, -1))
    own_0, to_0 = fold((near_0, met_0), 1)
    other_0 = swap(to_0, "dp", 12)
    own_1, to_1 = fold(last_terms, 1)
    other_1 = swap(to_1, "dp", 12)
    pieces = [own_0, other_0, own_1, other_1]
    grad_one, grad_two = finish(pieces, w_head.shape[2] // 16)
    return grad_one, grad_two.transpose(1, 0, 2)


def solution(mesh):
    placed = (
        P("dp", None),
        P("dp"),
        P("dp"),
        P("pop", None, None),
        P("pop", None, None),
        P("pop", "dp"),
    )
    return jax.shard_map(
        body,
        mesh=mesh,
        in_specs=placed,
        out_specs=(P("pop", "dp", None), P("pop", None, "dp")),
        check_vma=False,
    )
```

```python
import functools
import math

import jax
import jax.numpy as jnp
from jax import lax
from jax.experimental import pallas as pl
from jax.experimental.pallas import tpu as pltpu
from jax.sharding import PartitionSpec as P

HID = 1024
ACTIONS = 18
PAD = 32
CHUNKS = (80, 48)
EXTRA = 8
SHARES = (0, 2, 4, 6, 1, 3, 5, 7)
STEPS = [(y, z) for y in (2, 1, 3, 0) for z in (0, 3, 1, 2)]
F32 = jnp.float32
BF16 = jnp.bfloat16
NT = (((1,), (1,)), ((), ()))
TN = (((0,), (0,)), ((), ()))
VMEM_SPEC = pl.BlockSpec(memory_space=pltpu.VMEM)
HBM_SPEC = pl.BlockSpec(memory_space=pltpu.HBM)


def params(mib):
    return pltpu.CompilerParams(vmem_limit_bytes=mib * 1024 * 1024)


def cost(us):
    return pl.CostEstimate(flops=int(us * 1.1e9), bytes_accessed=0, transcendentals=0)


def after(value, *first):
    return lax.optimization_barrier((value, first))[0]


def spot():
    place = lax.axis_index("dp")
    return place // 4, place % 4, lax.axis_index("pop") % len(SHARES)


def block_of(z, y, i):
    step_y, step_z = STEPS[i]
    return (z ^ step_z) * 4 + (y + step_y) % 4


def turn(rows_ref, turned_ref, z, y, blocks):
    width = turned_ref.shape[1]
    for i in blocks:
        start = pl.multiple_of(block_of(z, y, i) * width, width)
        turned_ref[i] = rows_ref[:, pl.ds(start, width)].T


def padded(head_ref, wide_ref):
    wide_ref[...] = jnp.zeros_like(wide_ref)
    wide_ref[0:ACTIONS, :] = head_ref[0].astype(F32)


def split3(v):
    hi = v.astype(BF16)
    rest = v - hi.astype(F32)
    mid = rest.astype(BF16)
    low = (rest - mid.astype(F32)).astype(BF16)
    return jnp.concatenate([hi, mid, low], axis=0)


def join3(v):
    return v[:PAD] + v[PAD : 2 * PAD] + v[2 * PAD :]


def row_onehot(start, size, row):
    ids = lax.broadcasted_iota(jnp.int32, (size, row.shape[1]), 0) + start
    return jnp.where(ids == row, 1.0, 0.0).astype(BF16)


def sigmoid(v):
    return 0.5 * jnp.tanh(0.5 * v) + 0.5


def forward_kernel(
    pool_hbm, w_hbm, head_ref, row_ref, act_ref, target_ref, hid_ref, slope_ref, turned_ref, emb_ref, facts_ref,
    acc_ref, pool_ref, w_ref, wide_ref, sems,
):
    z, y, _ = spot()
    rows, hidden = hid_ref.shape
    tile, width = rows // 2, hidden // 2
    row_of = lambda i: pl.ds(i * tile, tile)
    pools = [pltpu.make_async_copy(pool_hbm.at[row_of(i), :], pool_ref.at[row_of(i), :], sems.at[i]) for i in range(2)]
    halves = [
        pltpu.make_async_copy(w_hbm.at[0, :, pl.ds(j * width, width)], w_ref.at[j], sems.at[2 + j]) for j in range(2)
    ]
    for copy in (pools[0], halves[0], halves[1], pools[1]):
        copy.start()
    padded(head_ref, wide_ref)
    facts_ref[0:1, :] = target_ref[...]
    facts_ref[1:2, :] = row_ref[...].astype(F32)
    facts_ref[2:3, :] = act_ref[...].astype(F32)
    facts_ref[3:, :] = jnp.zeros((facts_ref.shape[0] - 3, facts_ref.shape[1]), F32)
    pools[0].wait()
    for i in range(2):
        if i == 1:
            pools[1].wait()
        for j in range(2):
            if i == 0:
                halves[j].wait()
            columns = slice(j * width, (j + 1) * width)
            v = jnp.dot(pool_ref[row_of(i), :], w_ref[j], preferred_element_type=F32)
            sig = sigmoid(v)
            hid = (v * sig).astype(BF16)
            hid_ref[row_of(i), columns] = hid

            @pl.when(z // 2 == j)
            def _():
                slope_ref[row_of(i), :] = sig * (1.0 + v * (1.0 - sig))

            logits = lax.dot_general(wide_ref[:, columns].astype(BF16), hid, NT, preferred_element_type=F32)
            if j == 0:
                acc_ref[:, row_of(i)] = logits
            else:
                acc_ref[:, row_of(i)] += logits
                if i == 1:
                    turn(pool_ref, turned_ref, z, y, range(turned_ref.shape[0]))
    logits = acc_ref[...]
    parts = split3(logits - jnp.sum(logits, axis=0, keepdims=True) / ACTIONS)
    picked = jnp.zeros((3 * PAD, row_ref.shape[1]), F32)
    for i in range(0, rows, 256):
        picked += jnp.dot(parts[:, i : i + 256], row_onehot(i, 256, row_ref[...]), preferred_element_type=F32)
    chosen = lax.broadcasted_iota(jnp.int32, (PAD, row_ref.shape[1]), 0) == act_ref[...]
    emb_ref[...] = jnp.sum(jnp.where(chosen, join3(picked), 0.0), axis=0, keepdims=True)


def forward(pool, w, head, row, act, target):
    rows, feat = pool.shape
    hid = w.shape[2]
    probes = row.shape[1]
    blocks = len(STEPS)
    return pl.pallas_call(
        forward_kernel,
        in_specs=[HBM_SPEC] * 2 + [VMEM_SPEC] * 4,
        out_specs=[VMEM_SPEC] * 5,
        out_shape=[
            jax.ShapeDtypeStruct((rows, hid), BF16),
            jax.ShapeDtypeStruct((rows, hid // 2), F32),
            jax.ShapeDtypeStruct((blocks, feat // blocks, rows), BF16),
            jax.ShapeDtypeStruct((1, probes), F32),
            jax.ShapeDtypeStruct((8, probes), F32),
        ],
        scratch_shapes=[
            pltpu.VMEM((PAD, rows), F32),
            pltpu.VMEM((rows, feat), BF16),
            pltpu.VMEM((2, feat, hid // 2), BF16),
            pltpu.VMEM((PAD, hid), F32),
            pltpu.SemaphoreType.DMA((4,)),
        ],
        compiler_params=params(42),
        cost_estimate=cost(0.3),
        name="forward",
    )(pool, w, head, row, act, target)


def distance_kernel(near_ref, far_ref, facts_ref, out_ref, pack_ref):
    pop = jnp.concatenate([near_ref[...], far_ref[...]], axis=0)
    agents = pop.shape[0]
    lanes = lax.broadcasted_iota(jnp.int32, (agents, 128), 1)
    total = jnp.zeros((agents, 128), F32)
    for i in range(agents):
        gap = pop - pop[i : i + 1, :]
        total = jnp.where(lanes == i, jnp.sum(gap * gap, axis=1, keepdims=True), total)
    out_ref[...] = total
    pack_ref[0:agents, :] = pop
    pack_ref[agents:, :] = facts_ref[...]


def distance_parts(near, far, facts):
    agents, probes = 2 * near.shape[0], near.shape[1]
    return pl.pallas_call(
        distance_kernel,
        in_specs=[VMEM_SPEC] * 3,
        out_specs=[VMEM_SPEC] * 2,
        out_shape=[
            jax.ShapeDtypeStruct((agents, 128), F32),
            jax.ShapeDtypeStruct((agents + facts.shape[0], probes), F32),
        ],
        compiler_params=params(16),
        cost_estimate=cost(0.2),
        name="distances",
    )(near, far, facts)


def partner_rows(z, y, share_refs, w_hbm, turned_ref, rows_ref, w_ref, sem):
    share, width = share_refs[0].shape[0], w_ref.shape[1]
    columns = pl.ds(pl.multiple_of(z // 2 * width, width), width)
    copy = pltpu.make_async_copy(w_hbm.at[0, :, columns], w_ref, sem)
    copy.start()
    for j, ref in enumerate(share_refs):
        rows_ref[pl.ds(j * share, share), :] = ref[...].astype(BF16)
    copy.wait()
    v = jnp.dot(rows_ref[...], w_ref[...], preferred_element_type=F32)
    turn(rows_ref, turned_ref, z, y, range(turned_ref.shape[0]))
    sig = sigmoid(v)
    return sig * (1.0 + v * (1.0 - sig))


def marked_sums(marked, hot):
    return join3(lax.dot_general(marked, hot, NT, preferred_element_type=F32))


def scaled(sums, cents, slope):
    part_hi = sums.astype(BF16)
    part_lo = (sums - part_hi.astype(F32)).astype(BF16)
    stacked = jnp.concatenate([part_hi, part_hi, part_lo], axis=0)
    return (lax.dot_general(stacked, cents, TN, preferred_element_type=F32) * slope).astype(BF16)


def partner_hot(where, first, share, row):
    return jnp.concatenate([row_onehot((where ^ SHARES[j]) * share, share, row) for j in (first, first + 1)], axis=0)


def partner_a_kernel(a_ref, b_ref, c_ref, d_ref, w_hbm, slope_ref, turned_ref, rows_ref, w_ref, sem):
    z, y, _ = spot()
    slope_ref[...] = partner_rows(z, y, (a_ref, b_ref, c_ref, d_ref), w_hbm, turned_ref, rows_ref, w_ref, sem)


def partner_b_kernel(
    a_ref, b_ref, c_ref, d_ref, w_hbm, marked_ref, cents_ref, pack_ref, dz_ref, turned_ref, rows_ref, w_ref, sem
):
    z, y, where = spot()
    share = a_ref.shape[0]
    slope = partner_rows(z, y, (a_ref, b_ref, c_ref, d_ref), w_hbm, turned_ref, rows_ref, w_ref, sem)
    row = pack_ref[17:18, :].astype(jnp.int32)
    for i in range(2):
        here = slice(2 * i * share, 2 * (i + 1) * share)
        sums = marked_sums(marked_ref[...], partner_hot(where, 4 + 2 * i, share, row))
        dz_ref[here, :] = scaled(sums, cents_ref[...], slope[here])


def partner_part(shares, w, more=()):
    share, feat = shares[0].shape
    half = w.shape[2] // 2
    blocks = len(STEPS)
    return pl.pallas_call(
        partner_b_kernel if more else partner_a_kernel,
        in_specs=[VMEM_SPEC] * 4 + [HBM_SPEC] + [VMEM_SPEC] * len(more),
        out_specs=[VMEM_SPEC] * 2,
        out_shape=[
            jax.ShapeDtypeStruct((4 * share, half), BF16 if more else F32),
            jax.ShapeDtypeStruct((blocks, feat // blocks, 4 * share), BF16),
        ],
        scratch_shapes=[
            pltpu.VMEM((4 * share, feat), BF16),
            pltpu.VMEM((feat, half), BF16),
            pltpu.SemaphoreType.DMA(()),
        ],
        compiler_params=params(16),
        cost_estimate=cost(0.3),
        name="partner",
    )(*shares, w, *more)


def coeff_kernel(
    total_probes, scaling, d0, d1, near_ref, far_ref, facts_ref, pack_ref, head_ref, slope_a_ref, slope_ref, hid_ref,
    dz_ref, heads_ref, marked_ref, cents_ref, sums_ref, wide_ref, ghead_ref,
):
    z, y, where = spot()
    width = slope_ref.shape[1]
    columns = pl.ds(pl.multiple_of(z // 2 * width, width), width)
    padded(head_ref, wide_ref)
    pop = jnp.concatenate([near_ref[...], far_ref[...]], axis=0)
    agents = pop.shape[0]
    pop2 = pack_ref[0:agents, :]
    row, act = facts_ref[1:2, :].astype(jnp.int32), facts_ref[2:3, :].astype(jnp.int32)
    row2 = pack_ref[agents + 1 : agents + 2, :].astype(jnp.int32)
    act2 = pack_ref[agents + 2 : agents + 3, :].astype(jnp.int32)
    lanes = lax.broadcasted_iota(jnp.int32, (agents, 128), 1)
    subs = lax.broadcasted_iota(jnp.int32, (agents, 128), 0)
    kern = jnp.exp(-(d0[...] + d1[...]) / total_probes)
    system = jnp.where(lanes < agents, kern, jnp.where((lanes == agents) & (subs == 0), 1.0, 0.0))
    for k in range(agents):
        pivot_row = system[k : k + 1, :] / system[k : k + 1, k : k + 1]
        system = jnp.where(subs == k, pivot_row, system - system[:, k : k + 1] * pivot_row)
    mix = system[:, agents : agents + 1] * kern[:, 0:1]

    def marked(people, target, act):
        emb = people[0:1, :]
        pulled = jnp.sum(mix * people, axis=0, keepdims=True)
        diverse = 2.0 * (jnp.sum(mix, axis=0, keepdims=True) * emb - pulled)
        coeff = scaling * (emb - target) + scaling * diverse
        chosen = lax.broadcasted_iota(jnp.int32, (PAD, act.shape[1]), 0) == act
        return split3(jnp.where(chosen, coeff, 0.0))

    head = wide_ref[:, columns]
    centered = head - jnp.sum(head, axis=0, keepdims=True) / ACTIONS
    cent_hi = centered.astype(BF16)
    cent_lo = (centered - cent_hi.astype(F32)).astype(BF16)
    cents = jnp.concatenate([cent_hi, cent_lo, cent_hi], axis=0)

    rows = slope_ref.shape[0]
    tile = 256
    mine = marked(pop, facts_ref[0:1, :], act)
    theirs = marked(pop2, pack_ref[agents : agents + 1, :], act2)
    marked_ref[...] = theirs
    cents_ref[...] = cents
    for i in range(rows // tile):
        here = pl.ds(i * tile, tile)
        sums = marked_sums(mine, row_onehot(i * tile, tile, row))
        sums_ref[:, here] = sums
        dz_ref[here, :] = scaled(sums, cents, slope_ref[here, :])
    share = tile // 2
    for i in range(slope_a_ref.shape[0] // tile):
        sums = marked_sums(theirs, partner_hot(where, 2 * i, share, row2))
        dz_ref[pl.ds(rows + i * tile, tile), :] = scaled(sums, cents, slope_a_ref[pl.ds(i * tile, tile), :])
    sums = sums_ref[...]
    even = split3(sums - jnp.sum(sums, axis=0, keepdims=True) / ACTIONS)
    ghead_ref[...] = join3(jnp.dot(even, hid_ref[...], preferred_element_type=F32))
    blocks = heads_ref.shape[0]
    cols = ghead_ref.shape[1] // blocks
    for i in range(blocks):
        place = block_of(z, y, i)
        pair = ghead_ref[:, pl.ds(pl.multiple_of(place // 2 * 2 * cols, 2 * cols), 2 * cols)]
        mine = jnp.where(place % 2 == 0, pair[:, :cols], pair[:, cols:])
        laid = [mine[g * EXTRA : (g + 1) * EXTRA] for g in range(3)]
        rest = jnp.zeros((EXTRA, heads_ref.shape[2] - 3 * cols), F32)
        heads_ref[i] = jnp.concatenate(laid + [rest], axis=1)


def coefficients(total_probes, dists, near, far, facts, pack, head, slope_a, slope, hid):
    rows, width = hid.shape
    half = width // 2
    scaling = math.sqrt(HID / total_probes)
    return pl.pallas_call(
        functools.partial(coeff_kernel, total_probes, scaling),
        in_specs=[VMEM_SPEC] * 10,
        out_specs=[VMEM_SPEC] * 4,
        out_shape=[
            jax.ShapeDtypeStruct((rows + slope_a.shape[0], half), BF16),
            jax.ShapeDtypeStruct((len(STEPS), EXTRA, half), F32),
            jax.ShapeDtypeStruct((3 * PAD, rows), BF16),
            jax.ShapeDtypeStruct((3 * PAD, half), BF16),
        ],
        scratch_shapes=[
            pltpu.VMEM((PAD, rows), F32),
            pltpu.VMEM((PAD, width), F32),
            pltpu.VMEM((PAD, width), F32),
        ],
        compiler_params=params(16),
        cost_estimate=cost(0.3),
        name="coefficients",
    )(*dists, near, far, facts, pack, head, slope_a, slope, hid)


def grad_kernel(plan, *refs):
    own_ref, a_ref, b_ref, dz_ref, dz_b_ref, heads_ref = refs[:6]
    mine, part = own_ref.shape[2], a_ref.shape[2]
    width = dz_ref.shape[1]
    products = ((own_ref, dz_ref, 0, mine), (a_ref, dz_ref, mine, part), (b_ref, dz_b_ref, 0, part))
    for blocks, begin, end, outs, more in plan:
        rows = end - begin
        total = jnp.zeros((2 * rows, width), F32)
        for ref, right_ref, start, depth in products:
            left = jnp.concatenate([ref[i, begin:end, :] for i in blocks], axis=0)
            total += jnp.dot(left, right_ref[start : start + depth, :], preferred_element_type=F32)
        for q, block in enumerate(blocks):
            for out, at, size, extra in outs:
                out_ref, slot = refs[out[q][0]], out[q][1]
                value = total[q * rows + at : q * rows + at + size]
                heads = heads_ref[block] if extra else None
                if more is not None:
                    add_ref, add_slot = refs[more[q][0]], more[q][1]
                    value = value + add_ref[add_slot, 0:size, :]
                    heads = heads + add_ref[add_slot, size:, :] if extra else None
                out_ref[slot, 0:size, :] = value
                if extra:
                    out_ref[slot, size:, :] = heads


def gradient(parts, groups, which, more=None):
    dz = parts[3]
    width = dz.shape[1]
    chunks = [(sum(CHUNKS[:c]), CHUNKS[c], c == 0) for c in which]
    begin, end = chunks[0][0], chunks[-1][0] + chunks[-1][1]
    shapes = [
        jax.ShapeDtypeStruct((len(group), size + (EXTRA if extra else 0), width), F32)
        for group in groups
        for _, size, extra in chunks
    ]
    extras = [] if more is None else [more]
    first = len(parts) + len(extras)
    places = [(block, g, slot) for g, group in enumerate(groups) for slot, block in enumerate(group)]
    plan = []
    for k in range(0, len(places), 2):
        pair = places[k : k + 2]
        outs = [
            ([(first + g * len(chunks) + c, slot) for _, g, slot in pair], at - begin, size, extra)
            for c, (at, size, extra) in enumerate(chunks)
        ]
        added = None if more is None else [(len(parts), k), (len(parts), k + 1)]
        plan.append(([block for block, _, _ in pair], begin, end, outs, added))
    outs = pl.pallas_call(
        functools.partial(grad_kernel, plan),
        in_specs=[VMEM_SPEC] * first,
        out_specs=[VMEM_SPEC] * len(shapes),
        out_shape=shapes,
        compiler_params=params(16),
        cost_estimate=cost(0.3),
        name="gradient",
    )(*parts, *extras)
    return [outs[i : i + len(chunks)] for i in range(0, len(outs), len(chunks))]


def add_kernel(at, into_ref, more_ref, out_ref):
    here = slice(at, at + more_ref.shape[0])
    out_ref[here] = into_ref[here] + more_ref[...]


def add_into(into, more, at):
    return pl.pallas_call(
        functools.partial(add_kernel, at),
        in_specs=[VMEM_SPEC] * 2,
        out_specs=VMEM_SPEC,
        out_shape=jax.ShapeDtypeStruct(into.shape, F32),
        input_output_aliases={0: 0},
        compiler_params=params(16),
        cost_estimate=cost(0.1),
        name="add_into",
    )(into, more)


def fold_kernel(count, *refs):
    at = 0
    for out_ref in refs[count:]:
        size = out_ref.shape[0]
        out_ref[...] = sum((ref[at : at + size] for ref in refs[1:count]), refs[0][at : at + size])
        at += size


def fold(terms, per):
    blocks = terms[0].shape[0] // per
    return pl.pallas_call(
        functools.partial(fold_kernel, len(terms)),
        in_specs=[VMEM_SPEC] * len(terms),
        out_specs=[VMEM_SPEC] * blocks,
        out_shape=[jax.ShapeDtypeStruct((per, *terms[0].shape[1:]), F32)] * blocks,
        compiler_params=params(16),
        cost_estimate=cost(0.1),
        name="fold",
    )(*terms)


def finish_kernel(*refs):
    out_ref, two_ref = refs[-2:]
    z, _, _ = spot()
    width = refs[0].shape[2]
    left = pl.ds(pl.multiple_of(z // 2 * width, width), width)
    right = pl.ds(pl.multiple_of((1 - z // 2) * width, width), width)
    at = 0
    for c, size in enumerate(CHUNKS):
        own, other = refs[2 * c : 2 * c + 2]
        out_ref[0, at : at + size, left] = own[0, 0:size, :]
        out_ref[0, at : at + size, right] = other[0, 0:size, :]
        at += size
    heads = refs[0][0, CHUNKS[0] :, :] + refs[1][0, CHUNKS[0] :, :]
    cols = two_ref.shape[2]
    for g in range(3):
        count = min(EXTRA, ACTIONS - g * EXTRA)
        two_ref[g * EXTRA : g * EXTRA + count] = heads[0:count, g * cols : (g + 1) * cols].reshape(count, 1, cols)


def finish(pieces, cols):
    rows, width = sum(CHUNKS), pieces[0].shape[2]
    return pl.pallas_call(
        finish_kernel,
        grid=(1,),
        in_specs=[VMEM_SPEC] * len(pieces),
        out_specs=[
            pl.BlockSpec((1, rows, 2 * width), lambda i: (0, 0, 0)),
            pl.BlockSpec((ACTIONS, 1, cols), lambda i: (0, 0, 0)),
        ],
        out_shape=[
            jax.ShapeDtypeStruct((1, rows, 2 * width), F32),
            jax.ShapeDtypeStruct((ACTIONS, 1, cols), F32),
        ],
        compiler_params=params(16),
        cost_estimate=cost(0.1),
        name="finish",
    )(*pieces)


def shift_y(v, s):
    return lax.ppermute(v, "dp", [(z * 4 + y, z * 4 + (y + s) % 4) for z in range(4) for y in range(4)])


def swap(v, axis, mask):
    return lax.ppermute(v, axis, [(i, i ^ mask) for i in range(16)])


def to_partner_rows(v):
    return lax.ppermute(
        v,
        ("pop", "dp"),
        [(p * 16 + d, (p ^ (8 if d // 4 in (0, 3) else 0)) * 16 + (d ^ 12)) for p in range(16) for d in range(16)],
    )


def body(state_pool, probe_row, action, w_hidden, w_head, targets):
    probes = probe_row.shape[0]
    total_probes = probes * lax.axis_size("dp")
    share = state_pool.shape[0] // len(SHARES)
    row = probe_row.reshape(1, probes)
    act = action.reshape(1, probes)

    _, _, where = spot()
    cut = lambda i: lax.dynamic_slice_in_dim(state_pool, i * share, share, 0).astype(F32)
    share0 = to_partner_rows(cut(where))
    next_share = cut(where ^ 4)

    hid, slope, turned, near, facts = forward(state_pool, w_hidden, w_head, row, act, targets)
    for mask in (1, 2, 4):
        near = jnp.concatenate([near, swap(near, "pop", mask)], axis=0)
    far = swap(near, "pop", 8)
    share4 = to_partner_rows(after(next_share, far))
    share0 = after(share0, far)
    share2, share6 = swap(share0, "pop", 2), swap(share0, "pop", 6)
    part, pack = distance_parts(near, far, facts)
    part = part + swap(part, "dp", 1)
    pack = after(pack, part)
    part = part + swap(part, "dp", 2)
    pack = swap(pack, "dp", 12)
    part = part + swap(part, "dp", 4)
    dists = [part, swap(part, "dp", 8)]

    swapped0 = swap(after(share0, pack), "pop", 1)
    share0, share2, share4, share6 = after([share0, share2, share4, share6], pack, *dists)
    swapped = [swapped0] + [swap(v, "pop", 1) for v in (share2, share4, share6)]
    slope_a, turned_a = partner_part([share0, share2, share4, share6], w_hidden)
    dz, heads, marks, cents = coefficients(
        total_probes, dists, near, far, facts, pack, w_head, slope_a, slope, hid
    )
    dz_b, turned_b = partner_part(swapped, w_hidden, (marks, cents, pack))

    parts = [turned, turned_a, turned_b, dz, dz_b, heads]
    tie = lambda *first: parts[:3] + [after(dz, *first)] + parts[4:]
    early, last = range(len(CHUNKS) - 1), [len(CHUNKS) - 1]
    a2s, b2s = gradient(parts, [[0, 1], [2, 3]], early)
    from_a, from_b = [], []
    for i in early:
        from_a.append(shift_y(a2s[i], 1))
        from_b.append(shift_y(b2s[i], -1))
    away = [4 * g + k for g in range(4) for k in (2, 3)]
    waiting = []
    tied = tie(*a2s)
    for i in early:
        (ones,), (threes,), (zeros,) = gradient(tied, [[4, 5, 6, 7], [8, 9, 10, 11], [12, 13, 14, 15]], [i])
        if i == 0:
            ((sent,),) = gradient(tie(*a2s), [away], last)
            met = swap(sent, "dp", 4)
        ones, threes = add_into(ones, from_a[i], 0), add_into(threes, from_b[i], 2)
        waiting.append((zeros, shift_y(ones, 1), shift_y(threes, -1)))
        tied = tie(ones, threes)
    (a2,), (b2,), (ones,), (threes,), (zeros,) = gradient(tied, [[0], [1], [4, 5], [8, 9], [12, 13]], last, met)
    last_a, last_b = shift_y(a2, 1), shift_y(b2, -1)
    near_0, away_0 = fold(after(waiting[0], a2, b2), 2)
    met_0 = swap(away_0, "dp", 4)
    last_a, last_b = after((last_a, last_b), away_0)
    ones, threes = add_into(ones, last_a, 0), add_into(threes, last_b, 1)
    last_terms = (zeros, shift_y(ones, 1), shift_y(threes, -1))
    own_0, to_0 = fold((near_0, met_0), 1)
    other_0 = swap(to_0, "dp", 12)
    own_1, to_1 = fold(last_terms, 1)
    other_1 = swap(to_1, "dp", 12)
    pieces = [own_0, other_0, own_1, other_1]
    grad_one, grad_two = finish(pieces, w_head.shape[2] // 16)
    return grad_one, grad_two.transpose(1, 0, 2)


def solution(mesh):
    placed = (
        P("dp", None),
        P("dp"),
        P("dp"),
        P("pop", None, None),
        P("pop", None, None),
        P("pop", "dp"),
    )
    return jax.shard_map(
        body,
        mesh=mesh,
        in_specs=placed,
        out_specs=(P("pop", "dp", None), P("pop", None, "dp")),
        check_vma=False,
    )
```
